32 devices in a mesh: dp: 8 (over y, x, core), tensor: 4 (over z).
Axes of the slice: x: 2, y: 2, z: 4, core: 2. Of those that a mesh axis runs over, the one named last changes fastest.
Arguments:
- tokens: bfloat16 [28672, 768], P(('dp', 'tensor')), may hold values from -6 to 6
- gain_attn: float32 [768], P(('dp', 'tensor')), may hold values from 0.5 to 1.5
- w_query: bfloat16 [768, 768], P('dp', 'tensor'), may hold values from -0.3125 to 0.3125
- w_key: bfloat16 [768, 768], P('dp', 'tensor'), may hold values from -0.3125 to 0.3125
- w_value: bfloat16 [768, 768], P('dp', 'tensor'), may hold values from -0.21875 to 0.21875
- w_out: bfloat16 [768, 768], P('tensor', 'dp'), may hold values from -0.875 to 0.875
- gain_ffn: float32 [768], P(('dp', 'tensor')), may hold values from 0.5 to 1.5
- w_gate: bfloat16 [768, 2048], P('dp', 'tensor'), may hold values from -0.21875 to 0.21875
- w_up: bfloat16 [768, 2048], P('dp', 'tensor'), may hold values from -0.21875 to 0.21875
- w_down: bfloat16 [2048, 768], P('tensor', 'dp'), may hold values from -0.125 to 0.125
- segment_ids: int32 [28672], P('dp'), may hold values from 0 to 12, as said below
- parent_ids: int32 [28672], P('dp'), may hold values from 0 to 12, as said below
- positions: int32 [28672], P('dp'), may hold values from 0 to 2046, as said below
- cotangent: bfloat16 [28672, 768], P(('dp', 'tensor')), may hold values from -6 to 6
Outputs:
- mixed: bfloat16 [28672, 768], P(('dp', 'tensor'))
- grad_tokens: float32 [28672, 768], P(('dp', 'tensor'))
- grad_gain_attn: float32 [768], P(('dp', 'tensor'))
- grad_w_query: float32 [768, 768], P('dp', 'tensor')
- grad_w_key: float32 [768, 768], P('dp', 'tensor')
- grad_w_value: float32 [768, 768], P('dp', 'tensor')
- grad_w_out: float32 [768, 768], P('tensor', 'dp')
- grad_gain_ffn: float32 [768], P(('dp', 'tensor'))
- grad_w_gate: float32 [768, 2048], P('dp', 'tensor')
- grad_w_up: float32 [768, 2048], P('dp', 'tensor')
- grad_w_down: float32 [2048, 768], P('tensor', 'dp')
The draws below stay inside these ranges and needn't reach their ends.
Inputs may be any that keep to these rules, and one draw needn't show every extreme that they name: `segment_ids`: each block of 3584 rows is one tree of 13 segments with distinct ids: a root of 512 tokens, 4 branches of 256 tokens under the root and 2 leaves of 256 tokens under each branch. A segment's tokens are contiguous and follow its parent's tokens. `parent_ids`: the id of the parent of the token's segment; on the root's tokens, the root's own id. `positions`: A tree's offset, 0 to 1023, plus the number of tokens before the token on its root-to-leaf path.
All inputs are finite; a program needn't handle non-finite values.
Results may differ from the reference program's by a relative error of at most 0.02.
Values may be sent and summed in bfloat16 or wider, within the bound.
No kernel may reach another device: no remote copies, remote signals or barrier semaphores. Data moves between devices by JAX's collectives and lax.ppermute only.
A program may use at most 192 MiB of HBM per device.

```python
import jax
import jax.numpy as jnp
import numpy as np
from jax import lax

D = 768
HEADS = 12
HEAD_DIM = 64
FF = 2048
TRUNK = 512
BRANCHES = 4
LEAVES = 2
BRANCH_LEN = 256
QBLOCK = 512
TREE = 3584
TOKENS = 28672


def tree_tables():
    seg_total = 1 + BRANCHES + BRANCHES * LEAVES
    parents = [0] + [0] * BRANCHES + [1 + branch for branch in range(BRANCHES) for leaf_pos in range(LEAVES)]
    depth_first = [0] + [TRUNK] * BRANCHES + [TRUNK + BRANCH_LEN] * (BRANCHES * LEAVES)
    lengths = [TRUNK] + [BRANCH_LEN] * (seg_total - 1)
    wide_order = list(range(seg_total))
    deep_order = [0]
    for branch in range(BRANCHES):
        deep_order = deep_order + [1 + branch] + [1 + BRANCHES + branch * LEAVES + leaf_pos for leaf_pos in range(LEAVES)]

    def expand(ordering):
        seg_part = np.concatenate([np.full(lengths[seg_item], seg_item, np.int32) for seg_item in ordering])
        depth_part = np.concatenate([depth_first[seg_item] + np.arange(lengths[seg_item], dtype=np.int32) for seg_item in ordering])
        return (seg_part, depth_part)
    wide_seg, wide_depth = expand(wide_order)
    deep_seg, deep_depth = expand(deep_order)
    return (np.array(parents, np.int32), wide_seg, wide_depth, deep_seg, deep_depth)


def tree_draw(key):
    parents, wide_seg, wide_depth, deep_seg, deep_depth = tree_tables()
    seg_total = parents.shape[0]
    tree_count = TOKENS // TREE

    def one_tree(tree_key, tree_index):
        label_key = jax.random.fold_in(tree_key, 1)
        shape_key = jax.random.fold_in(tree_key, 2)
        shift_key = jax.random.fold_in(tree_key, 3)
        labels = jax.random.permutation(label_key, seg_total).astype(jnp.int32)
        target = jnp.where(tree_index == 0, seg_total - 1, jnp.where(tree_index == 1, 0, labels[0])).astype(jnp.int32)
        labels = jnp.where(labels == target, labels[0], labels)
        labels = labels.at[0].set(target)
        deep_flag = jax.random.randint(shape_key, (), 0, 2)
        struct_seg = jnp.where(deep_flag == 1, jnp.asarray(deep_seg), jnp.asarray(wide_seg))
        depth_pos = jnp.where(deep_flag == 1, jnp.asarray(deep_depth), jnp.asarray(wide_depth))
        offset_val = jax.random.randint(shift_key, (), 0, 1024)
        offset_val = jnp.where(tree_index == 0, 0, jnp.where(tree_index == 1, 1023, offset_val))
        seg_ids = labels[struct_seg]
        par_ids = labels[jnp.asarray(parents)[struct_seg]]
        return (seg_ids, par_ids, (depth_pos + offset_val).astype(jnp.int32))
    tree_keys = jax.random.split(jax.random.fold_in(key, 17), tree_count)
    tree_indices = jnp.arange(tree_count).astype(jnp.int32)
    return jax.vmap(one_tree)(tree_keys, tree_indices)


def draw_segment_ids(key, part):
    return tree_draw(key)[0].reshape(TOKENS).astype(jnp.int32)


def draw_parent_ids(key, part):
    return tree_draw(key)[1].reshape(TOKENS).astype(jnp.int32)


def draw_positions(key, part):
    return tree_draw(key)[2].reshape(TOKENS).astype(jnp.int32)


def shard_levels(rng, extent, cuts, least, top_value):
    def one(axis_at, shards_of):
        steps = jax.random.uniform(jax.random.fold_in(jax.random.fold_in(rng, 6), axis_at), (shards_of,), jnp.float32, least / len(cuts), top_value / len(cuts))
        return jnp.repeat(jnp.exp(steps), extent[axis_at] // shards_of).reshape((-1,) + (1,) * (len(extent) - axis_at - 1))

    gain = one(*cuts[0])
    for cut in cuts[1:]:
        gain = gain * one(*cut)
    return gain


def noise(key, shape, deviation, limit, shards=(), kind=jnp.bfloat16):
    result = jax.random.normal(key, shape, jnp.float32) * deviation
    if len(shards) > 0:
        result = shard_levels(key, shape, shards, -0.22, 0.18) * result
    return jnp.clip(result, min=-limit, max=limit).astype(kind)


def setup_inputs(seed: int = 0) -> dict:
    key_list = jax.random.split(jax.random.key(seed), 15)
    tokens = noise(key_list[0], (TOKENS, D), 1.0, 6.0, ((0, 32),))
    gain_attn = jnp.clip(1.0 + 0.1 * jax.random.normal(key_list[1], (D,), jnp.float32), 0.5, 1.5)
    w_query = noise(key_list[2], (D, D), (D // 2) ** -0.5, 0.3125, ((0, 8), (1, 4)))
    w_key = noise(key_list[3], (D, D), (D // 2) ** -0.5, 0.3125, ((0, 8), (1, 4)))
    w_value = noise(key_list[4], (D, D), D ** -0.5, 0.21875, ((0, 8), (1, 4)))
    w_out = noise(key_list[5], (D, D), (D // 16) ** -0.5, 0.875, ((0, 4), (1, 8)))
    gain_ffn = jnp.clip(1.0 + 0.1 * jax.random.normal(key_list[6], (D,), jnp.float32), 0.5, 1.5)
    w_gate = noise(key_list[7], (D, FF), D ** -0.5, 0.21875, ((0, 8), (1, 4)))
    w_up = noise(key_list[8], (D, FF), D ** -0.5, 0.21875, ((0, 8), (1, 4)))
    w_down = noise(key_list[9], (FF, D), FF ** -0.5, 0.125, ((0, 4), (1, 8)))
    segment_ids = draw_segment_ids(jax.random.fold_in(key_list[14], 71), 0)
    parent_ids = draw_parent_ids(jax.random.fold_in(key_list[14], 71), 0)
    positions = draw_positions(jax.random.fold_in(key_list[14], 71), 0)
    cotangent = noise(key_list[13], (TOKENS, D), 1.0, 6.0, ((0, 32),))
    return {"tokens": tokens, "gain_attn": gain_attn, "w_query": w_query, "w_key": w_key, "w_value": w_value, "w_out": w_out, "gain_ffn": gain_ffn, "w_gate": w_gate, "w_up": w_up, "w_down": w_down, "segment_ids": segment_ids, "parent_ids": parent_ids, "positions": positions, "cotangent": cotangent}


EPSILON = 1e-05
MASKED = -1e+30
PRECISION = lax.Precision.HIGHEST

@jax.custom_vjp
def low(v):
    return lax.optimization_barrier(v.astype(jnp.bfloat16)).astype(jnp.float32)

@jax.custom_vjp
def low_back(v):
    return v

def low_keep(v):
    return (low(v), None)

def low_pass(kept, grad):
    return (grad,)

def back_keep(v):
    return (v, None)

def back_low(kept, grad):
    return (low(grad),)
low.defvjp(low_keep, low_pass)
low_back.defvjp(back_keep, back_low)

def rms_norm(values, gain_vec):
    row_scale = lax.rsqrt(lax.optimization_barrier(jnp.mean(values * values, axis=-1, keepdims=True)) + EPSILON)
    return values * row_scale * gain_vec

def tables(pos_ids):
    half_dim = HEAD_DIM // 2
    freq_table = jnp.exp(-jnp.log(10000.0) * (2.0 * jnp.arange(half_dim).astype(jnp.float32) / HEAD_DIM))
    freq_table = jnp.concatenate([freq_table, freq_table])
    angles = pos_ids.astype(jnp.float32)[:, None] * freq_table[None, :]
    return (jnp.cos(angles)[:, None, :], jnp.sin(angles)[:, None, :])

def rotate(values, cos_tab, sine_tab):
    half_dim = values.shape[-1] // 2
    turned = jnp.concatenate([-values[..., half_dim:], values[..., :half_dim]], axis=-1)
    return values * cos_tab + turned * sine_tab

def attend(first_row, query_rot, key_rot, values, seg_ids, par_ids):
    q_block = lax.dynamic_slice_in_dim(query_rot, first_row, QBLOCK, 0)
    seg_rows = lax.dynamic_slice_in_dim(seg_ids, first_row, QBLOCK, 0)
    par_rows = lax.dynamic_slice_in_dim(par_ids, first_row, QBLOCK, 0)
    row_index = first_row + jnp.arange(QBLOCK).astype(jnp.int32)
    col_index = jnp.arange(seg_ids.shape[0]).astype(jnp.int32)
    causal = col_index[None, :] <= row_index[:, None]
    kinship = (seg_ids[None, :] == seg_rows[:, None]) | (seg_ids[None, :] == par_rows[:, None]) | (par_ids == seg_ids)[None, :]
    allowed = causal & kinship
    raw_score = low_back(jnp.einsum('qhd,khd->hqk', q_block, key_rot, precision=PRECISION))
    scores = jnp.where(allowed[None], raw_score * HEAD_DIM ** (-0.5), MASKED)
    row_top = lax.optimization_barrier(jnp.max(scores, axis=-1, keepdims=True))
    expo_vals = jnp.exp(scores - row_top)
    prob_vals = expo_vals / lax.optimization_barrier(jnp.sum(expo_vals, axis=-1, keepdims=True))
    return jnp.einsum('hqk,khd->qhd', low(prob_vals), values, precision=PRECISION)

def forward(x_vals, gain_one, query_w, key_w, value_w, out_w, gain_two, gate_w, up_w, down_w, seg_ids, par_ids, pos_ids):
    row_count = x_vals.shape[0]
    normed = low(rms_norm(x_vals, gain_one))
    cos_tab, sine_tab = tables(pos_ids)

    def project(weight):
        return jnp.dot(normed, weight, precision=PRECISION).reshape(row_count, HEADS, HEAD_DIM)
    query_rot = low(rotate(low_back(project(query_w)), cos_tab, sine_tab))
    key_rot = low(rotate(low_back(project(key_w)), cos_tab, sine_tab))
    values = low(low_back(project(value_w)))
    starts = jnp.arange(row_count // QBLOCK).astype(jnp.int32) * QBLOCK
    blocks = lax.map(lambda first_row: jax.checkpoint(attend)(first_row, query_rot, key_rot, values, seg_ids, par_ids), starts)
    attn_out = low(low_back(blocks.reshape(row_count, HEADS * HEAD_DIM)))
    hidden_state = x_vals + low_back(jnp.dot(attn_out, out_w, precision=PRECISION))
    normed_two = low(rms_norm(hidden_state, gain_two))
    gate_pre = low_back(jnp.dot(normed_two, gate_w, precision=PRECISION))
    up_pre = low_back(jnp.dot(normed_two, up_w, precision=PRECISION))
    inner_act = low(jax.nn.silu(gate_pre) * up_pre)
    return hidden_state + low_back(jnp.dot(inner_act, down_w, precision=PRECISION))

def reference(tokens, gain_attn, w_query, w_key, w_value, w_out, gain_ffn, w_gate, w_up, w_down, segment_ids, parent_ids, positions, cotangent):
    params = (gain_attn.astype(jnp.float32), w_query.astype(jnp.float32), w_key.astype(jnp.float32), w_value.astype(jnp.float32), w_out.astype(jnp.float32), gain_ffn.astype(jnp.float32), w_gate.astype(jnp.float32), w_up.astype(jnp.float32), w_down.astype(jnp.float32))
    tree_count = TOKENS // TREE
    x_trees = tokens.astype(jnp.float32).reshape(tree_count, TREE, D)
    cot_trees = cotangent.astype(jnp.float32).reshape(tree_count, TREE, D)
    seg_trees = segment_ids.reshape(tree_count, TREE)
    par_trees = parent_ids.reshape(tree_count, TREE)
    pos_trees = positions.reshape(tree_count, TREE)

    def one_tree(running, inputs):
        x_vals, seg_ids, par_ids, pos_ids, cot_vals = inputs

        def layer(x_in, *weights):
            return forward(x_in, *weights, seg_ids, par_ids, pos_ids)
        output, pullback = jax.vjp(layer, x_vals, *params)
        gradients = pullback(cot_vals)
        running = tuple((acc_val + gradient for acc_val, gradient in zip(running, gradients[1:])))
        return (running, (output.astype(jnp.bfloat16), gradients[0]))
    zeros_init = tuple((jnp.zeros_like(weight) for weight in params))
    running, (outputs, grad_x) = lax.scan(one_tree, zeros_init, (x_trees, seg_trees, par_trees, pos_trees, cot_trees))
    return (outputs.reshape(TOKENS, D), grad_x.reshape(TOKENS, D), running[0], running[1], running[2], running[3], running[4], running[5], running[6], running[7], running[8])
```

```python
import functools

import jax
import jax.numpy as jnp
from jax import lax
from jax.experimental import pallas as pl
from jax.experimental.pallas import tpu as pltpu
from jax.sharding import PartitionSpec as P

HEAD_DIM = 64
BLOCK = 256
TILE = 128
ROOT = 512
KEYS = 1024
EPSILON = 1e-05
MASKED = -1e30
VMEM = 60 * 1024 * 1024
F32 = jnp.float32
BF16 = jnp.bfloat16
ROWS = (((0,), (0,)), ((), ()))
COLS = (((1,), (1,)), ((), ()))


def dot(a, b, dims=(((1,), (0,)), ((), ()))):
    return lax.dot_general(a, b, dims, preferred_element_type=F32)


def half_turn(u):
    lane = lax.broadcasted_iota(jnp.int32, u.shape, 1)
    return jnp.where(lane % HEAD_DIM < HEAD_DIM // 2, pltpu.roll(u, 96, 1), pltpu.roll(u, 32, 1))


def proj_kernel(x_ref, xl_ref, gain_ref, wq_ref, wk_ref, wv_ref, cos_ref, sin_ref, cosl_ref, sinl_ref,
                a_ref, k_ref, v_ref, q_ref):
    def normed(ref):
        x = ref[...].astype(F32)
        scale = lax.rsqrt(jnp.mean(x * x, axis=-1, keepdims=True) + EPSILON)
        return (x * scale * gain_ref[...]).astype(BF16)

    def rotated(u, cos, sin, out_ref, factor):
        for c in range(u.shape[1] // 128):
            part = u[:, c * 128:(c + 1) * 128]
            r = (part * cos + half_turn(part) * sin).astype(BF16)
            out_ref[:, c * 128:(c + 1) * 128] = r * factor if factor is not None else r

    a = normed(x_ref)
    a_ref[...] = a
    rotated(dot(a, wk_ref[...]), cos_ref[...], sin_ref[...], k_ref, None)
    v_ref[...] = dot(a, wv_ref[...]).astype(BF16)
    al = normed(xl_ref)
    rotated(dot(al, wq_ref[...]), cosl_ref[...], sinl_ref[...], q_ref, jnp.asarray(HEAD_DIM ** -0.5, BF16))


def project(x_full, x_loc, gain, w_all, cos, sin, cos_l, sin_l):
    rows, d = x_full.shape
    loc = x_loc.shape[0]
    steps = loc // TILE
    big = rows // steps

    def tiles(n, w):
        return pl.BlockSpec((n, w), lambda i: (i, 0))

    def weight(j):
        return pl.BlockSpec((d, d), lambda i: (0, j))

    return pl.pallas_call(
        proj_kernel,
        grid=(steps,),
        in_specs=[tiles(big, d), tiles(TILE, d), pl.BlockSpec((1, d), lambda i: (0, 0)),
                  weight(0), weight(1), weight(2),
                  tiles(big, 128), tiles(big, 128), tiles(TILE, 128), tiles(TILE, 128)],
        out_specs=[tiles(big, d), tiles(big, d), tiles(big, d), tiles(TILE, d)],
        out_shape=[jax.ShapeDtypeStruct((rows, d), BF16)] * 3 + [jax.ShapeDtypeStruct((loc, d), BF16)],
        compiler_params=pltpu.CompilerParams(vmem_limit_bytes=VMEM),
        name="project",
    )(x_full, x_loc, gain, w_all, w_all, w_all, cos, sin, cos_l, sin_l)


def fill_bias(meta_ref, bias_ref, keys_axis):
    shape = bias_ref.shape[1:]

    def one(i, carry):
        sub, leaf = meta_ref[i, 0], meta_ref[i, 1]
        key = lax.broadcasted_iota(jnp.int32, shape, keys_axis)
        row = lax.broadcasted_iota(jnp.int32, shape, 1 - keys_axis)
        in_root = sub < ROOT // TILE
        root_top = jnp.where(in_root, sub * TILE, ROOT)
        own_top = jnp.where(in_root, -ROOT, (sub % 2) * TILE)
        root_ok = (key < ROOT) & (key <= row + root_top)
        parent_ok = (key >= ROOT) & (key < ROOT + jnp.where(leaf > 0, BLOCK, 0))
        own_ok = (key >= ROOT + BLOCK) & (key - (ROOT + BLOCK) <= row + own_top)
        bias_ref[i] = jnp.where(root_ok | parent_ok | own_ok, 0.0, MASKED).astype(F32)
        return carry

    lax.fori_loop(0, bias_ref.shape[0], one, 0)


def half_masks():
    lane = lax.broadcasted_iota(jnp.int32, (TILE, 128), 1)
    return lane < HEAD_DIM


def fwd_kernel(meta_ref, q_ref, k_ref, v_ref, o_ref, l_ref, bias_ref):
    @pl.when(pl.program_id(0) == 0)
    def _():
        fill_bias(meta_ref, bias_ref, 1)

    low = half_masks()

    def one(i, carry):
        row = pl.multiple_of(i * TILE, TILE)
        par = pl.multiple_of(meta_ref[i, 2], BLOCK)
        own = pl.multiple_of(meta_ref[i, 3], TILE)
        q = q_ref[pl.ds(row, TILE), :]
        spans = ((pl.ds(0, ROOT), 0, ROOT), (pl.ds(par, BLOCK), ROOT, BLOCK), (pl.ds(own, BLOCK), ROOT + BLOCK, BLOCK))
        outs = []
        logs = []
        for head in range(2):
            qh = jnp.where(low if head == 0 else ~low, q, jnp.zeros_like(q))
            s = [dot(qh, k_ref[sl, :], COLS) + bias_ref[i, :, at:at + n] for sl, at, n in spans]
            top = functools.reduce(jnp.maximum, [jnp.max(part, axis=1, keepdims=True) for part in s])
            e = [jnp.exp(part - top) for part in s]
            total = sum(jnp.sum(part, axis=1, keepdims=True) for part in e)
            acc = sum(dot(part.astype(BF16), v_ref[sl, :]) for part, (sl, _, _) in zip(e, spans))
            outs.append(acc / total)
            logs.append(top + jnp.log(total))
        o_ref[pl.ds(row, TILE), :] = jnp.where(low, outs[0], outs[1]).astype(BF16)
        both = jnp.where(low, logs[0], logs[1]).T
        l_ref[0, :, pl.ds(row, TILE)] = both[60:68, :]
        return carry

    lax.fori_loop(0, q_ref.shape[0] // TILE, one, 0)


def attend(meta, q, k, v):
    loc, d = q.shape
    rows = k.shape[0]
    pairs = d // 128
    pair = lambda n: pl.BlockSpec((n, 128), lambda p: (0, p))
    return pl.pallas_call(
        fwd_kernel,
        grid=(pairs,),
        in_specs=[pl.BlockSpec(memory_space=pltpu.SMEM), pair(loc), pair(rows), pair(rows)],
        out_specs=[pair(loc), pl.BlockSpec((1, 8, loc), lambda p: (p, 0, 0))],
        out_shape=[jax.ShapeDtypeStruct((loc, d), BF16), jax.ShapeDtypeStruct((pairs, 8, loc), F32)],
        scratch_shapes=[pltpu.VMEM((loc // TILE, TILE, KEYS), F32)],
        compiler_params=pltpu.CompilerParams(vmem_limit_bytes=VMEM),
        name="attend",
    )(meta, q, k, v)


def bwd_kernel(meta_ref, q_ref, k_ref, v_ref, do_ref, o_ref, l_ref, cos_ref, sin_ref, cosl_ref, sinl_ref,
               dq_ref, dk_ref, dv_ref, bias_ref, dk_acc, dv_acc):
    @pl.when(pl.program_id(0) == 0)
    def _():
        fill_bias(meta_ref, bias_ref, 0)

    low = half_masks()
    dk_acc[...] = jnp.zeros_like(dk_acc)
    dv_acc[...] = jnp.zeros_like(dv_acc)

    def one(i, carry):
        row = pl.multiple_of(i * TILE, TILE)
        par = pl.multiple_of(meta_ref[i, 2], BLOCK)
        own = pl.multiple_of(meta_ref[i, 3], TILE)
        here = pl.ds(row, TILE)
        q = q_ref[here, :]
        do = do_ref[here, :]
        dots = (do.astype(F32) * o_ref[here, :].astype(F32)).T
        spans = ((pl.ds(0, ROOT), 0, ROOT), (pl.ds(par, BLOCK), ROOT, BLOCK), (pl.ds(own, BLOCK), ROOT + BLOCK, BLOCK))
        dqs = []
        for head in range(2):
            keep = low if head == 0 else ~low
            qh = jnp.where(keep, q, jnp.zeros_like(q))
            doh = jnp.where(keep, do, jnp.zeros_like(do))
            log = l_ref[0, 3 + head:4 + head, here]
            row_dot = jnp.sum(dots[head * HEAD_DIM:(head + 1) * HEAD_DIM, :], axis=0, keepdims=True)
            dq = jnp.zeros((TILE, 128), F32)
            for sl, at, n in spans:
                kk = k_ref[sl, :]
                s = dot(kk, qh, COLS) + bias_ref[i, at:at + n, :]
                p = jnp.exp(s - log)
                dp = dot(v_ref[sl, :], doh, COLS)
                ds = (p * (dp - row_dot)).astype(BF16)
                dv_acc[sl, :] += dot(p.astype(BF16), doh)
                dk_acc[sl, :] += dot(ds, qh)
                dq += dot(ds, kk, ROWS)
            dqs.append(dq)
        dq = jnp.where(low, dqs[0], dqs[1]) * HEAD_DIM ** -0.5
        dq_ref[here, :] = (dq * cosl_ref[here, :] - half_turn(dq) * sinl_ref[here, :]).astype(BF16)
        return carry

    lax.fori_loop(0, q_ref.shape[0] // TILE, one, 0)

    def last(j, carry):
        here = pl.ds(pl.multiple_of(j * BLOCK, BLOCK), BLOCK)
        dk = dk_acc[here, :]
        dk_ref[here, :] = (dk * cos_ref[here, :] - half_turn(dk) * sin_ref[here, :]).astype(BF16)
        dv_ref[here, :] = dv_acc[here, :].astype(BF16)
        return carry

    lax.fori_loop(0, k_ref.shape[0] // BLOCK, last, 0)


def attend_back(meta, q, k, v, do, o, logs, cos, sin, cos_l, sin_l):
    loc, d = q.shape
    rows = k.shape[0]
    pairs = d // 128
    pair = lambda n: pl.BlockSpec((n, 128), lambda p: (0, p))
    whole = lambda n: pl.BlockSpec((n, 128), lambda p: (0, 0))
    return pl.pallas_call(
        bwd_kernel,
        grid=(pairs,),
        in_specs=[pl.BlockSpec(memory_space=pltpu.SMEM), pair(loc), pair(rows), pair(rows), pair(loc), pair(loc),
                  pl.BlockSpec((1, 8, loc), lambda p: (p, 0, 0)), whole(rows), whole(rows), whole(loc), whole(loc)],
        out_specs=[pair(loc), pair(rows), pair(rows)],
        out_shape=[jax.ShapeDtypeStruct((loc, d), BF16)] + [jax.ShapeDtypeStruct((rows, d), BF16)] * 2,
        scratch_shapes=[pltpu.VMEM((loc // TILE, KEYS, TILE), F32), pltpu.VMEM((rows, 128), F32), pltpu.VMEM((rows, 128), F32)],
        compiler_params=pltpu.CompilerParams(vmem_limit_bytes=VMEM),
        name="attend_back",
    )(meta, q, k, v, do, o, logs, cos, sin, cos_l, sin_l)


def tables(pos):
    half = HEAD_DIM // 2
    freq = jnp.exp(-jnp.log(10000.0) * (2.0 * jnp.arange(half, dtype=F32) / HEAD_DIM))
    angle = pos.astype(F32)[:, None] * jnp.concatenate([freq, freq, freq, freq])[None, :]
    sign = jnp.where(jnp.arange(2 * HEAD_DIM) % HEAD_DIM < half, -1.0, 1.0).astype(F32)
    return jnp.cos(angle), jnp.sin(angle) * sign[None, :]


def norm_back(grad_out, x_hat, scale, gain):
    scaled = grad_out * gain
    return scale * (scaled - x_hat * jnp.mean(scaled * x_hat, axis=-1, keepdims=True))


def per_device(tokens, gain_attn, w_query, w_key, w_value, w_out, gain_ffn, w_gate, w_up, w_down,
               segment_ids, parent_ids, positions, cotangent):
    loc, d = tokens.shape
    t_size = lax.axis_size("tensor")
    t_at = lax.axis_index("tensor")
    rows = loc * t_size
    ff = w_gate.shape[1] * t_size

    gains = jnp.zeros((8, 128), F32)
    own_gain = gain_attn.shape[0]
    gains = gains.at[0, :own_gain].set(gain_attn).at[1, :own_gain].set(gain_ffn)
    gains = lax.all_gather(gains, ("dp", "tensor"), axis=0, tiled=False)
    gain_one = gains[:, 0, :own_gain].reshape(1, d)
    gain_two = gains[:, 1, :own_gain].reshape(1, d)

    x_full = lax.all_gather(tokens, "tensor", axis=0, tiled=True)

    parts = (w_query, w_key, w_value, w_out.T, w_gate, w_up, w_down.T)
    pack = jnp.concatenate(parts, axis=1)
    pack = lax.all_gather(pack, "tensor", axis=0, tiled=False)
    cuts = []
    at = 0
    for part in parts:
        n = part.shape[1]
        cuts.append(jnp.swapaxes(pack[:, :, at:at + n], 0, 1).reshape(part.shape[0], n * t_size))
        at += n
    w_qkv = lax.all_gather(jnp.concatenate(cuts[:3], axis=1), "dp", axis=0, tiled=True)
    w_rest = lax.all_gather(jnp.concatenate(cuts[3:], axis=1), "dp", axis=0, tiled=True)
    out_t = w_rest[:, :d]
    gate = w_rest[:, d:d + ff]
    up = w_rest[:, d + ff:d + 2 * ff]
    down_t = w_rest[:, d + 2 * ff:]

    seg = segment_ids[::BLOCK]
    par = parent_ids[::BLOCK]
    sub = t_at * (loc // TILE) + jnp.arange(loc // TILE, dtype=jnp.int32)
    block = sub // 2
    my_par = par[block]
    parent = jnp.argmax(seg[None, :] == my_par[:, None], axis=1).astype(jnp.int32)
    leaf = ((my_par != seg[0]) & (block >= 2)).astype(jnp.int32)
    meta = jnp.stack([sub, leaf, parent * BLOCK * leaf, block * BLOCK], axis=1)

    cos, sin = tables(positions)
    cos_l = lax.dynamic_slice_in_dim(cos, t_at * loc, loc, 0)
    sin_l = lax.dynamic_slice_in_dim(sin, t_at * loc, loc, 0)

    a_full, k, v, q = project(x_full, tokens, gain_one, w_qkv, cos, sin, cos_l, sin_l)
    o, logs = attend(meta, q, k, v)

    x = tokens.astype(F32)
    scale_one = lax.rsqrt(jnp.mean(x * x, axis=-1, keepdims=True) + EPSILON)
    h = x + dot(o, out_t, COLS)
    scale_two = lax.rsqrt(jnp.mean(h * h, axis=-1, keepdims=True) + EPSILON)
    c_hat = h * scale_two
    c = (c_hat * gain_two).astype(BF16)
    g = dot(c, gate)
    u = dot(c, up)
    sig = jax.nn.sigmoid(g)
    silu = g * sig
    m = (silu * u).astype(BF16)
    mixed = (h + dot(m, down_t, COLS)).astype(BF16)

    dm = dot(cotangent, down_t)
    dg = (dm * u * sig * (1.0 + g * (1.0 - sig))).astype(BF16)
    du = (dm * silu).astype(BF16)
    g_down = dot(cotangent, m, ROWS)
    g_gate = dot(c, dg, ROWS)
    g_up = dot(c, du, ROWS)
    dc = dot(dg, gate, COLS) + dot(du, up, COLS)
    gain_two_sum = jnp.sum(dc * c_hat, axis=0)
    dh = cotangent.astype(F32) + norm_back(dc, c_hat, scale_two, gain_two)
    dhb = dh.astype(BF16)
    do = dot(dhb, out_t).astype(BF16)
    g_out = dot(dhb, o, ROWS)
    rest = jnp.concatenate([g_out.astype(BF16), g_gate.astype(BF16), g_up.astype(BF16), g_down.astype(BF16)], axis=1)

    def owners(grads, widths):
        mine = lax.psum_scatter(grads, "dp", scatter_dimension=0, tiled=True)
        pieces = []
        at = 0
        for n in widths:
            pieces.append(jnp.swapaxes(mine[:, at:at + n].reshape(mine.shape[0], t_size, n // t_size), 0, 1))
            at += n
        packed = jnp.concatenate(pieces, axis=2)
        total = lax.psum_scatter(packed, "tensor", scatter_dimension=0, tiled=False).astype(F32)
        outs = []
        at = 0
        for n in widths:
            outs.append(total[:, at:at + n // t_size])
            at += n // t_size
        return outs

    r_out, r_gate, r_up, r_down = owners(rest, (d, ff, ff, ff))

    dq, dk, dv = attend_back(meta, q, k, v, do, o, logs, cos, sin, cos_l, sin_l)
    w_q, w_k, w_v = w_qkv[:, :d], w_qkv[:, d:2 * d], w_qkv[:, 2 * d:]
    da_part = (dot(dk, w_k, COLS) + dot(dv, w_v, COLS)).astype(BF16)
    da_sum = lax.psum_scatter(da_part, "tensor", scatter_dimension=0, tiled=True)
    a_loc = lax.dynamic_slice_in_dim(a_full, t_at * loc, loc, 0)
    g_qkv = jnp.concatenate([dot(a_loc, dq, ROWS).astype(BF16), dot(a_full, dk, ROWS).astype(BF16),
                             dot(a_full, dv, ROWS).astype(BF16)], axis=1)
    r_q, r_k, r_v = owners(g_qkv, (d, d, d))
    da = da_sum.astype(F32) + dot(dq, w_q, COLS)
    x_hat = x * scale_one
    grad_tokens = dh + norm_back(da, x_hat, scale_one, gain_one)
    gain_one_sum = jnp.sum(da * x_hat, axis=0)
    sums = lax.psum(jnp.stack([gain_one_sum, gain_two_sum]), ("dp", "tensor"))
    at = (lax.axis_index("dp") * t_size + t_at) * own_gain
    mine = lax.dynamic_slice_in_dim(sums, at, own_gain, 1)
    return (mixed, grad_tokens, mine[0], r_q, r_k, r_v, r_out.T, mine[1], r_gate, r_up, r_down.T)


def solution(mesh):
    rows = P(("dp", "tensor"), None)
    gain = P(("dp", "tensor"))
    wide = P("dp", "tensor")
    tall = P("tensor", "dp")
    return jax.shard_map(
        per_device,
        mesh=mesh,
        in_specs=(rows, gain, wide, wide, wide, tall, gain, wide, wide, tall, P("dp"), P("dp"), P("dp"), rows),
        out_specs=(rows, rows, gain, wide, wide, wide, tall, gain, wide, wide, tall),
        check_vma=False,
    )
```

```python
import functools

import jax
import jax.numpy as jnp
from jax import lax
from jax.experimental import pallas as pl
from jax.experimental.pallas import tpu as pltpu
from jax.sharding import PartitionSpec as P

HEAD_DIM = 64
BLOCK = 256
TILE = 128
ROOT = 512
BRANCHES = 4
SLOTS = BRANCHES * BLOCK
FAR = ROOT + SLOTS
EARLY = ROOT + BLOCK
GAIN_LANES = 128
EPSILON = 1e-05
MASKED = -1e30
VMEM = 60 * 1024 * 1024
F32 = jnp.float32
BF16 = jnp.bfloat16
PLAIN = (((1,), (0,)), ((), ()))
ROWS = (((0,), (0,)), ((), ()))
COLS = (((1,), (1,)), ((), ()))


def dot(a, b, dims=PLAIN):
    return lax.dot_general(a, b, dims, preferred_element_type=F32)


def cost(us):
    return pl.CostEstimate(flops=int(us * 3e7), bytes_accessed=0, transcendentals=0)


def params():
    return pltpu.CompilerParams(vmem_limit_bytes=VMEM)


def half_turn(u):
    lane = lax.broadcasted_iota(jnp.int32, u.shape, 1)
    return jnp.where(lane % HEAD_DIM < HEAD_DIM // 2, pltpu.roll(u, 96, 1), pltpu.roll(u, 32, 1))


SMEM = pl.BlockSpec(memory_space=pltpu.SMEM)
ANY = pl.BlockSpec(memory_space=pl.ANY)


def after(count, kernel):
    return lambda *refs: kernel(*refs[count:])


def fixed(shape):
    return pl.BlockSpec(shape, lambda i: (0,) * len(shape), pipeline_mode=pl.Buffered(1))


def tiled(n, w):
    return pl.BlockSpec((n, w), lambda i: (i, 0))


def pair(n):
    return pl.BlockSpec((n, 128), lambda p: (0, p))


def aligned(row, n, unit=TILE):
    return pl.ds(pl.multiple_of(row, unit), n)


def shape(n, w, kind):
    return jax.ShapeDtypeStruct((n, w), kind)


def inv_rms(x):
    return lax.rsqrt(jnp.mean(x * x, axis=-1, keepdims=True) + EPSILON)


def plan_kernel(tiles, blocks, at_ref, seg_ref, par_ref, meta_ref, slot_ref):
    t = at_ref[0]
    first = ROOT // BLOCK
    root = seg_ref[0]
    seg = [seg_ref[b * BLOCK] for b in range(blocks)]
    par = [par_ref[b * BLOCK] for b in range(blocks)]
    rank = []
    count = jnp.int32(0)
    for b in range(blocks):
        rank.append(count)
        if b >= first:
            count = count + (par[b] == root).astype(jnp.int32)
    for beta in range(BRANCHES):
        at = jnp.int32(0)
        for b in range(first, blocks):
            at = jnp.where((par[b] == root) & (rank[b] == beta), b, at)
        for half in range(2):
            sub = 2 * at + half
            h = 2 * beta + half
            slot_ref[h, 0] = sub // tiles
            slot_ref[h, 1] = sub % tiles
            slot_ref[h, 2] = sub
            for j in range(3, 8):
                slot_ref[h, j] = 0
    for i in range(8):
        sub = t * tiles + min(i, tiles - 1)
        block = sub // 2
        mine = par_ref[block * BLOCK]
        leaf = ((mine != root) & (block >= first)).astype(jnp.int32)
        slot = jnp.int32(0)
        for b in range(first, blocks):
            slot = jnp.where((seg[b] == mine) & (par[b] == root), rank[b], slot)
        given = jnp.int32(-1)
        for h in range(2, 2 * BRANCHES):
            given = jnp.where((slot_ref[h, 2] == sub) & (t > 0), (h - 2) * TILE, given)
        meta_ref[i, 0] = sub
        meta_ref[i, 1] = leaf
        meta_ref[i, 2] = slot * leaf * BLOCK
        meta_ref[i, 3] = block * BLOCK - t * tiles * TILE + TILE
        meta_ref[i, 4] = given
        meta_ref[i, 5] = t
        meta_ref[i, 6] = jnp.where(t == 0, (slot_ref[2, 0] == 0).astype(jnp.int32), 0)
        meta_ref[i, 7] = 0


def plan(t_at, seg, par, tiles):
    out = jax.ShapeDtypeStruct((8, 8), jnp.int32)
    return pl.pallas_call(
        functools.partial(plan_kernel, tiles, seg.shape[0] // BLOCK),
        in_specs=[SMEM] * 3,
        out_specs=[SMEM] * 2,
        out_shape=[out, out],
        name="plan",
    )(t_at.reshape(1), seg, par)


def normed(x, gain):
    return (x * inv_rms(x) * gain).astype(BF16)


def rotated(u, cos, sin, out_ref, rows, factor):
    for c in range(u.shape[1] // 128):
        part = u[:, c * 128:(c + 1) * 128]
        r = (part * cos + half_turn(part) * sin).astype(BF16)
        out_ref[rows, c * 128:(c + 1) * 128] = r * factor if factor is not None else r


def line_kernel(out_ref, parts):
    n = (parts[0].shape[1] - GAIN_LANES) // 4
    for j in range(4):
        for r, part in enumerate(parts):
            out_ref[:, (j * len(parts) + r) * n:(j * len(parts) + r + 1) * n] = part[:, j * n:(j + 1) * n]
    out_ref[:, 4 * n * len(parts):] = sum(part[:, 4 * n:] for part in parts)


def line(deps, parts):
    rows, wide = parts[0].shape
    out = (rows, (wide - GAIN_LANES) * len(parts) + GAIN_LANES)
    return pl.pallas_call(
        after(len(deps), lambda *refs: line_kernel(refs[-1], refs[:-1])),
        grid=(1,),
        in_specs=[ANY] * len(deps) + [fixed(one.shape) for one in parts],
        out_specs=fixed(out),
        out_shape=shape(*out, BF16),
        compiler_params=params(),
        cost_estimate=cost(2),
        name="line",
    )(*deps, *parts)


def join_kernel(ins, out_ref):
    at = 0
    for part in ins:
        out_ref[:, at:at + part.shape[1]] = part[...]
        at += part.shape[1]


def join(deps, *parts):
    out = (parts[0].shape[0], sum(part.shape[1] for part in parts))
    return pl.pallas_call(
        after(len(deps), lambda *refs: join_kernel(refs[:-1], refs[-1])),
        grid=(1,),
        in_specs=[ANY] * len(deps) + [fixed(one.shape) for one in parts],
        out_specs=fixed(out),
        out_shape=shape(*out, BF16),
        compiler_params=params(),
        cost_estimate=cost(2),
        name="join",
    )(*deps, *parts)


def meet_kernel(kept_ref, kept_gain, away_ref, out_ref):
    d = kept_ref.shape[2]
    out_ref[:, :, :d] = (kept_ref[...].astype(F32) + away_ref[:, :, :d].astype(F32)).astype(BF16)
    out_ref[:, :, d:] = (kept_gain[...].astype(F32) + away_ref[:, :, d:].astype(F32)).astype(BF16)


def meet(deps, kept, kept_gain, away):
    chips = kept.shape[0]
    block = lambda one: pl.BlockSpec((1,) + one.shape[1:], lambda i: (i, 0, 0))
    return pl.pallas_call(
        after(len(deps), meet_kernel),
        grid=(chips,),
        in_specs=[ANY] * len(deps) + [block(one) for one in (kept, kept_gain, away)],
        out_specs=block(away),
        out_shape=jax.ShapeDtypeStruct(away.shape, BF16),
        compiler_params=params(),
        cost_estimate=cost(3),
        name="meet",
    )(*deps, kept, kept_gain, away)


def own_kernel(count, at_ref, x_ref, cos_ref, sin_ref, *refs):
    pieces, (w_ref, gain_ref, a_ref, q_ref, k_ref, v_ref) = refs[:count], refs[count:]
    d = x_ref.shape[1]
    t, dp = at_ref[0], at_ref[1]
    step = pl.program_id(0)

    @pl.when(step == 0)
    def _():
        cols = []
        for m, piece in enumerate(pieces):
            rows = piece.shape[0]
            w_ref[aligned((dp ^ m) * rows if count > 1 else 0, rows, 8), :] = piece[:, :4 * d]
        for j in range(count):
            row = jnp.zeros((pieces[0].shape[0], GAIN_LANES), F32)
            for m, piece in enumerate(pieces):
                row = jnp.where((dp ^ m) == j if count > 1 else True, piece[:, 4 * d:].astype(F32), row)
            cols.append(row)
        table = jnp.concatenate(cols, axis=0).T
        gain_ref[...] = jnp.zeros_like(gain_ref)
        gain_ref[0:1, :] = table[0:1, :] + table[1:2, :] + table[2:3, :]
        gain_ref[1:2, :] = table[3:4, :] + table[4:5, :] + table[5:6, :]

    n = x_ref.shape[0]
    here = aligned(t * (n * pl.num_programs(0)) + step * n, n, 16)
    cos, sin = cos_ref[here, :], sin_ref[here, :]
    a = normed(x_ref[...].astype(F32), gain_ref[0:1, :])
    a_ref[...] = a
    rotated(dot(a, w_ref[:, :d]), cos, sin, q_ref, slice(None), jnp.asarray(HEAD_DIM ** -0.5, BF16))
    rotated(dot(a, w_ref[:, d:2 * d]), cos, sin, k_ref, slice(None), None)
    v_ref[...] = dot(a, w_ref[:, 2 * d:3 * d]).astype(BF16)


def project_own(deps, at, x, tab, pieces):
    loc, d = x.shape
    n = loc // 2
    return pl.pallas_call(
        after(len(deps), functools.partial(own_kernel, len(pieces))),
        grid=(2,),
        in_specs=[ANY] * len(deps) + [SMEM, tiled(n, d), fixed(tab[0].shape), fixed(tab[0].shape)] + [fixed(one.shape) for one in pieces],
        out_specs=[pl.BlockSpec((d, 4 * d), lambda i: (0, 0)), pl.BlockSpec((8, d), lambda i: (0, 0))] + [tiled(n, d)] * 4,
        out_shape=[shape(d, 4 * d, BF16), shape(8, d, F32)] + [shape(loc, d, BF16)] * 4,
        compiler_params=params(),
        cost_estimate=cost(10),
        name="project_own",
    )(*deps, at, x, *tab, *pieces)


def near_rows_kernel(at_ref, x_ref, r1_ref, r2_ref, r3_ref, f1_ref, gain_ref, wk_ref, wv_ref, cos_ref, sin_ref,
                     x_out, a_ref, k_ref, v_ref):
    t = at_ref[0]
    loc = x_ref.shape[0]
    root = pl.ds(0, ROOT)
    edge = pl.ds(ROOT, TILE)

    @pl.when(t == 0)
    def _():
        x_out[root, :] = x_ref[root, :]

    for at, ref in ((1, r1_ref), (2, r2_ref), (3, r3_ref)):
        @pl.when(t == at)
        def _():
            x_out[root, :] = ref[...]

    x_out[edge, :] = f1_ref[f1_ref.shape[0] - TILE:, :]

    a = normed(x_out[...].astype(F32), gain_ref[0:1, :])
    a_ref[...] = a
    k = dot(a, wk_ref[...])
    back = aligned(jnp.maximum(t * loc - TILE, 0), TILE)
    rotated(k[:ROOT], cos_ref[root, :], sin_ref[root, :], k_ref, root, None)
    rotated(k[ROOT:], cos_ref[back, :], sin_ref[back, :], k_ref, edge, None)
    v_ref[...] = dot(a, wv_ref[...]).astype(BF16)


def weight(d, j):
    return pl.BlockSpec((d, d), lambda i: (0, j), pipeline_mode=pl.Buffered(1))


def project_near(at, x, r1, r2, r3, f1, gains, w, tab):
    d = x.shape[1]
    n = ROOT + TILE
    return pl.pallas_call(
        near_rows_kernel,
        grid=(1,),
        in_specs=[SMEM] + [fixed(one.shape) for one in (x, r1, r2, r3, f1, gains)] + [weight(d, 1), weight(d, 2)]
        + [fixed(one.shape) for one in tab],
        out_specs=[fixed((n, d))] * 4,
        out_shape=[shape(n, d, BF16)] * 4,
        compiler_params=params(),
        cost_estimate=cost(5),
        name="project_near",
    )(at, x, r1, r2, r3, f1, gains, w, w, *tab)


def far_rows_kernel(meta_ref, slot_ref, x_ref, a1_ref, a2_ref, a3_ref, b1_ref, b2_ref, b3_ref, gain_ref, wk_ref, wv_ref, cos_ref, sin_ref,
                    x_out, a_ref, k_ref, v_ref):
    t = meta_ref[0, 5]
    for h in range(2 * BRANCHES):
        owner, at = slot_ref[h, 0], slot_ref[h, 1]
        rows = aligned(at * TILE, TILE)
        head = aligned(jnp.minimum(at * TILE, ROOT - TILE), TILE)
        back = aligned(jnp.maximum(at * TILE - ROOT, 0), TILE)
        to = pl.ds(h * TILE, TILE)

        @pl.when(owner > t)
        def _():
            x_out[to, :] = jnp.zeros((TILE, x_out.shape[1]), BF16)

        @pl.when(owner == t)
        def _():
            x_out[to, :] = x_ref[rows, :]

        for hop, a_from, b_from in ((1, a1_ref, b1_ref), (2, a2_ref, b2_ref), (3, a3_ref, b3_ref)):
            @pl.when((owner + hop == t) & (at < ROOT // TILE))
            def _():
                x_out[to, :] = a_from[head, :]

            @pl.when((owner + hop == t) & (at >= ROOT // TILE))
            def _():
                x_out[to, :] = b_from[back, :]

    a = normed(x_out[...].astype(F32), gain_ref[0:1, :])
    a_ref[...] = a
    k = dot(a, wk_ref[...])
    for h in range(2 * BRANCHES):
        back = aligned(slot_ref[h, 2] * TILE, TILE)
        rotated(k[h * TILE:(h + 1) * TILE], cos_ref[back, :], sin_ref[back, :], k_ref, pl.ds(h * TILE, TILE), None)
    v_ref[...] = dot(a, wv_ref[...]).astype(BF16)


def project_far(meta, slots, x, ups, gains, w, tab):
    d = x.shape[1]
    return pl.pallas_call(
        far_rows_kernel,
        grid=(1,),
        in_specs=[SMEM, SMEM] + [fixed(one.shape) for one in (x, *ups, gains)] + [weight(d, 1), weight(d, 2)]
        + [fixed(one.shape) for one in tab],
        out_specs=[fixed((SLOTS, d))] * 4,
        out_shape=[shape(SLOTS, d, BF16)] * 4,
        compiler_params=params(),
        cost_estimate=cost(7),
        name="project_far",
    )(meta, slots, x, *ups, gains, w, w, *tab)


def fill_bias(root_ref, own_ref, keys_axis):
    for ref in (root_ref, own_ref):
        if ref is None:
            continue
        key = lax.broadcasted_iota(jnp.int32, ref.shape[1:], keys_axis)
        row = lax.broadcasted_iota(jnp.int32, ref.shape[1:], 1 - keys_axis)
        for s in range(ref.shape[0]):
            ref[s] = jnp.where(key <= row + s * TILE, 0.0, MASKED).astype(F32)


def low_half():
    return lax.broadcasted_iota(jnp.int32, (TILE, 128), 1) < HEAD_DIM


def tile_of(meta_ref, i):
    return (meta_ref[i, 0], meta_ref[i, 1], aligned(meta_ref[i, 2], BLOCK), aligned(meta_ref[i, 3], BLOCK),
            aligned(i * TILE, TILE))


def line_up(to_ref, near_ref, own_ref):
    loc = own_ref.shape[0]
    to_ref[pl.ds(0, TILE), :] = near_ref[pl.ds(ROOT, TILE), :]
    to_ref[pl.ds(TILE, loc), :] = own_ref[...]
    to_ref[pl.ds(TILE + loc, TILE), :] = jnp.zeros((TILE, 128), to_ref.dtype)


def attend_near_kernel(meta_ref, q_ref, kn_ref, vn_ref, k_ref, v_ref, acc_ref, top_ref, sum_ref, root_ref, own_ref, ko_ref, vo_ref):
    @pl.when(pl.program_id(0) == 0)
    def _():
        fill_bias(root_ref, own_ref, 1)

    line_up(ko_ref, kn_ref, k_ref)
    line_up(vo_ref, vn_ref, v_ref)
    low = low_half()
    root = pl.ds(0, ROOT)

    def one(i, carry):
        sub, leaf, par, own, here = tile_of(meta_ref, i)
        q = q_ref[here, :]

        def soft(spans):
            outs = []
            for head in range(2):
                qh = jnp.where(low if head == 0 else ~low, q, jnp.zeros_like(q))
                s = [dot(qh, kk, COLS) if b is None else dot(qh, kk, COLS) + b for kk, _, b in spans]
                top = functools.reduce(jnp.maximum, [jnp.max(part, axis=1, keepdims=True) for part in s])
                e = [jnp.exp(part - top) for part in s]
                total = sum(jnp.sum(part, axis=1, keepdims=True) for part in e)
                acc = sum(dot(part.astype(BF16), vv) for part, (_, vv, _) in zip(e, spans))
                outs.append((acc, top, total))
            acc_ref[here, :] = jnp.where(low, outs[0][0], outs[1][0])
            top_ref[here, :] = jnp.where(low, outs[0][1], outs[1][1])
            sum_ref[here, :] = jnp.where(low, outs[0][2], outs[1][2])

        @pl.when(sub < ROOT // TILE)
        def _():
            soft([(kn_ref[root, :], vn_ref[root, :], root_ref[sub])])

        @pl.when(sub >= ROOT // TILE)
        def _():
            soft([(kn_ref[root, :], vn_ref[root, :], None), (ko_ref[own, :], vo_ref[own, :], own_ref[sub % 2])])

        return carry

    lax.fori_loop(0, acc_ref.shape[0] // TILE, one, 0)


def bias_scratch(keys_axis):
    def one(n):
        return pltpu.VMEM((n // TILE,) + ((n, TILE) if keys_axis == 0 else (TILE, n)), F32)
    return one(ROOT), one(BLOCK)


def line_scratch(loc, kind):
    return pltpu.VMEM((loc + 2 * TILE, 128), kind)


def attend_near(meta, q, near, own):
    loc, d = q.shape
    n = ROOT + TILE
    return pl.pallas_call(
        attend_near_kernel,
        grid=(d // 128,),
        in_specs=[SMEM, pair(loc), pair(n), pair(n), pair(loc), pair(loc)],
        out_specs=[pair(loc)] * 3,
        out_shape=[shape(loc, d, F32)] * 3,
        scratch_shapes=[*bias_scratch(1), line_scratch(loc, BF16), line_scratch(loc, BF16)],
        compiler_params=params(),
        cost_estimate=cost(30),
        name="attend_near",
    )(meta, q, *near, *own)


def attend_far_kernel(meta_ref, q_ref, ks_ref, vs_ref, acc_ref, top_ref, sum_ref, o_ref, l_ref):
    low = low_half()

    def one(i, carry):
        sub, leaf, par, own, here = tile_of(meta_ref, i)
        acc, tops, sums = acc_ref[here, :], top_ref[here, :], sum_ref[here, :]

        def finish(acc, top, total):
            o_ref[here, :] = (acc / total).astype(BF16)
            l_ref[0, :, here] = (top + jnp.log(total)).T[60:68, :]

        @pl.when(leaf == 0)
        def _():
            finish(acc, tops, sums)

        @pl.when(leaf > 0)
        def _():
            q = q_ref[here, :]
            kk, vv = ks_ref[par, :], vs_ref[par, :]
            outs = []
            for head in range(2):
                qh = jnp.where(low if head == 0 else ~low, q, jnp.zeros_like(q))
                old = tops[:, head * HEAD_DIM:head * HEAD_DIM + 1]
                s = dot(qh, kk, COLS)
                top = jnp.maximum(jnp.max(s, axis=1, keepdims=True), old)
                e = jnp.exp(s - top)
                outs.append((dot(e.astype(BF16), vv), top, jnp.sum(e, axis=1, keepdims=True)))
            new, top, total = (jnp.where(low, outs[0][j], outs[1][j]) for j in range(3))
            fade = jnp.exp(tops - top)
            finish(acc * fade + new, top, sums * fade + total)

        return carry

    lax.fori_loop(0, o_ref.shape[0] // TILE, one, 0)


def log_spec(loc):
    return pl.BlockSpec((1, 8, loc), lambda p: (p, 0, 0))


def attend_far(meta, q, far, acc, top, total):
    loc, d = q.shape
    return pl.pallas_call(
        attend_far_kernel,
        grid=(d // 128,),
        in_specs=[SMEM, pair(loc), pair(SLOTS), pair(SLOTS), pair(loc), pair(loc), pair(loc)],
        out_specs=[pair(loc), log_spec(loc)],
        out_shape=[shape(loc, d, BF16), jax.ShapeDtypeStruct((d // 128, 8, loc), F32)],
        compiler_params=params(),
        cost_estimate=cost(11),
        name="attend_far",
    )(meta, q, *far, acc, top, total)


def split_cores(core, got, kept_ref, away_ref, where):
    @pl.when(core == 0)
    def _():
        kept_ref[where] = got[:, 0]
        away_ref[where] = got[:, 1]

    @pl.when(core == 1)
    def _():
        kept_ref[where] = got[:, 1]
        away_ref[where] = got[:, 0]


def ffn_kernel(at_ref, x_ref, o_ref, ct_ref, gain_ref, wo_ref, w_ref,
               mixed_ref, do_ref, dhb_ref, dh_ref, sum_ref, kept_ref, away_ref, c_s, m_s, dg_s, du_s, ct_t, c_t):
    step = pl.program_id(0)
    loc, d = ct_ref.shape
    n = x_ref.shape[0]
    parts, hid = m_s.shape[0], m_s.shape[2]

    def slab(t, j):
        return w_ref[:, t, :, j * hid:(j + 1) * hid].reshape(d, hid)

    @pl.when(step < loc // n)
    def _():
        here = aligned(step * n, n, 16)
        ct = ct_ref[here, :]
        h = x_ref[...].astype(F32) + dot(o_ref[...], wo_ref[...], COLS)
        scale = inv_rms(h)
        c_hat = h * scale
        gain = gain_ref[1:2, :]
        c = (c_hat * gain).astype(BF16)
        c_s[here, :] = c
        y = h
        dc = jnp.zeros_like(h)
        for t in range(parts):
            g = dot(c, slab(t, 0))
            u = dot(c, slab(t, 1))
            dm = dot(ct, slab(t, 2))
            sig = jax.nn.sigmoid(g)
            silu = g * sig
            m = (silu * u).astype(BF16)
            dg = (dm * u * (sig * (1.0 + g * (1.0 - sig)))).astype(BF16)
            du = (dm * silu).astype(BF16)
            y = y + dot(m, slab(t, 2), COLS)
            dc = dc + dot(dg, slab(t, 0), COLS) + dot(du, slab(t, 1), COLS)
            m_s[t, here, :] = m
            dg_s[t, here, :] = dg
            du_s[t, here, :] = du
        mixed_ref[...] = y.astype(BF16)
        part = jnp.sum(dc * c_hat, axis=0, keepdims=True)

        @pl.when(step == 0)
        def _():
            sum_ref[...] = jnp.zeros_like(sum_ref)

        sum_ref[0:1, :] += part
        scaled = dc * gain
        dh = ct.astype(F32) + scale * (scaled - c_hat * jnp.mean(scaled * c_hat, axis=-1, keepdims=True))
        dh_ref[...] = dh
        dhb = dh.astype(BF16)
        dhb_ref[...] = dhb
        do_ref[...] = dot(dhb, wo_ref[...]).astype(BF16)

    @pl.when(step == loc // n)
    def _():
        ct_t[...] = ct_ref[...].T
        c_t[...] = c_s[...].T

    @pl.when(step >= loc // n)
    def _():
        t = step - loc // n
        for j, (left, right) in enumerate(((c_t, dg_s), (c_t, du_s), (ct_t, m_s))):
            got = dot(left[...], right[t]).astype(BF16)
            chips, _, rows, _ = kept_ref.shape
            split_cores(at_ref[1] % 2, got.reshape(chips, 2, rows, hid), kept_ref, away_ref,
                        (slice(None), 0, slice(None), slice(j * hid, (j + 1) * hid)))


def feed_forward(at_core, x, o, ct, gains, w, rest):
    loc, d = x.shape
    dp, parts, rows, wide = rest.shape
    hid = wide // 3
    steps = 2
    n = loc // steps
    at = lambda i: (jnp.minimum(i, steps - 1), 0)
    tile = pl.BlockSpec((n, d), at)
    grads = pl.BlockSpec((dp // 2, 1, rows, wide), lambda i: (0, jnp.maximum(i - steps, 0), 0, 0))
    return pl.pallas_call(
        ffn_kernel,
        grid=(steps + parts,),
        in_specs=[SMEM, tile, tile, fixed((loc, d)), fixed((8, d)), weight(d, 3), fixed(rest.shape)],
        out_specs=[tile, tile, tile, tile, pl.BlockSpec((8, d), lambda i: (0, 0)), grads, grads],
        out_shape=[shape(loc, d, BF16), shape(loc, d, BF16), shape(loc, d, BF16), shape(loc, d, F32), shape(8, d, F32)]
        + [jax.ShapeDtypeStruct((dp // 2, parts, rows, wide), BF16)] * 2,
        scratch_shapes=[pltpu.VMEM((loc, d), BF16)] + [pltpu.VMEM((parts, loc, hid), BF16)] * 3 + [pltpu.VMEM((d, loc), BF16)] * 2,
        compiler_params=params(),
        cost_estimate=cost(40),
        name="feed_forward",
    )(at_core, x, o, ct, gains, w, rest)


def unrotate(w, cos, sin):
    return w * cos - half_turn(w) * sin


def back_setup(low, q_ref, do_ref, o_ref, l_ref, here):
    q, do = q_ref[here, :], do_ref[here, :]
    dots = (do.astype(F32) * o_ref[here, :].astype(F32)).T
    heads = []
    for head in range(2):
        keep = low if head == 0 else ~low
        heads.append((jnp.where(keep, q, jnp.zeros_like(q)), jnp.where(keep, do, jnp.zeros_like(do)),
                      l_ref[0, 3 + head:4 + head, here],
                      jnp.sum(dots[head * HEAD_DIM:(head + 1) * HEAD_DIM, :], axis=0, keepdims=True)))
    return heads


def back_span(low, heads, kk, vv, bias, acc, dk_acc, dv_acc):
    dqs = []
    for qh, doh, log, row_dot in heads:
        s = dot(kk, qh, COLS)
        if bias is not None:
            s = s + bias
        p = jnp.exp(s - log)
        dp = dot(vv, doh, COLS)
        ds = (p * (dp - row_dot)).astype(BF16)
        dv_acc[acc, :] += dot(p.astype(BF16), doh)
        dk_acc[acc, :] += dot(ds, qh)
        dqs.append(dot(ds, kk, ROWS))
    return jnp.where(low, dqs[0], dqs[1])


def back_far_kernel(meta_ref, slot_ref, q_ref, do_ref, o_ref, l_ref, kn_ref, vn_ref, ks_ref, vs_ref, cos_ref, sin_ref,
                    dq_ref, dk_ref, dv_ref, root_ref, dk_acc, dv_acc):
    @pl.when(pl.program_id(0) == 0)
    def _():
        fill_bias(root_ref, None, 0)

    low = low_half()
    root = pl.ds(0, ROOT)
    for ref in (dk_acc, dv_acc):
        ref[...] = jnp.zeros_like(ref)

    def one(i, carry):
        sub, leaf, par, own, here = tile_of(meta_ref, i)
        heads = back_setup(low, q_ref, do_ref, o_ref, l_ref, here)

        @pl.when(sub < ROOT // TILE)
        def _():
            dq_ref[here, :] = back_span(low, heads, kn_ref[root, :], vn_ref[root, :], root_ref[sub], root, dk_acc, dv_acc)

        @pl.when(sub >= ROOT // TILE)
        def _():
            dq_ref[here, :] = back_span(low, heads, kn_ref[root, :], vn_ref[root, :], None, root, dk_acc, dv_acc)

        @pl.when(leaf > 0)
        def _():
            acc = aligned(meta_ref[i, 2] + ROOT, BLOCK, BLOCK)
            dq_ref[here, :] += back_span(low, heads, ks_ref[par, :], vs_ref[par, :], None, acc, dk_acc, dv_acc)

        return carry

    lax.fori_loop(0, do_ref.shape[0] // TILE, one, 0)
    dk_ref[root, :] = unrotate(dk_acc[root, :], cos_ref[root, :], sin_ref[root, :]).astype(BF16)
    for h in range(2 * BRANCHES):
        at, back = pl.ds(ROOT + h * TILE, TILE), aligned(slot_ref[h, 2] * TILE, TILE)
        dk_ref[at, :] = unrotate(dk_acc[at, :], cos_ref[back, :], sin_ref[back, :]).astype(BF16)
    dv_ref[...] = dv_acc[...].astype(BF16)


def back_far(meta, slots, q, do, o, logs, near, far, tab):
    loc, d = do.shape
    n = ROOT + TILE
    return pl.pallas_call(
        back_far_kernel,
        grid=(d // 128,),
        in_specs=[SMEM, SMEM, pair(loc), pair(loc), pair(loc), log_spec(loc), pair(n), pair(n), pair(SLOTS), pair(SLOTS)]
        + [fixed(one.shape) for one in tab],
        out_specs=[pair(loc), pair(FAR), pair(FAR)],
        out_shape=[shape(loc, d, F32), shape(FAR, d, BF16), shape(FAR, d, BF16)],
        scratch_shapes=[bias_scratch(0)[0], pltpu.VMEM((FAR, 128), F32), pltpu.VMEM((FAR, 128), F32)],
        compiler_params=params(),
        cost_estimate=cost(50),
        name="back_far",
    )(meta, slots, q, do, o, logs, *near, *far, *tab)


def back_near_kernel(meta_ref, q_ref, do_ref, o_ref, l_ref, kn_ref, vn_ref, k_ref, v_ref, cos_ref, sin_ref, part_ref,
                     dq_ref, dk_ref, dv_ref, dke_ref, dve_ref, own_ref, ko_ref, vo_ref, dk_acc, dv_acc):
    @pl.when(pl.program_id(0) == 0)
    def _():
        fill_bias(None, own_ref, 0)

    line_up(ko_ref, kn_ref, k_ref)
    line_up(vo_ref, vn_ref, v_ref)
    low = low_half()
    loc = do_ref.shape[0]
    t = meta_ref[0, 5]
    for ref in (dk_acc, dv_acc):
        ref[...] = jnp.zeros_like(ref)

    def one(i, carry):
        sub, leaf, par, own, here = tile_of(meta_ref, i)
        back = aligned(sub * TILE, TILE)

        def put(dq):
            dq_ref[here, :] = unrotate(dq * HEAD_DIM ** -0.5, cos_ref[back, :], sin_ref[back, :]).astype(BF16)

        @pl.when(sub < ROOT // TILE)
        def _():
            put(part_ref[here, :])

        @pl.when(sub >= ROOT // TILE)
        def _():
            heads = back_setup(low, q_ref, do_ref, o_ref, l_ref, here)
            put(part_ref[here, :] + back_span(low, heads, ko_ref[own, :], vo_ref[own, :], own_ref[sub % 2], own, dk_acc, dv_acc))

        return carry

    lax.fori_loop(0, loc // TILE, one, 0)
    edge, mine = pl.ds(0, TILE), pl.ds(TILE, loc)
    before = aligned(jnp.maximum(t * loc - TILE, 0), TILE)
    here = aligned(t * loc, loc)
    dke_ref[...] = unrotate(dk_acc[edge, :], cos_ref[before, :], sin_ref[before, :]).astype(BF16)
    dve_ref[...] = dv_acc[edge, :].astype(BF16)
    dk_ref[...] = unrotate(dk_acc[mine, :], cos_ref[here, :], sin_ref[here, :]).astype(BF16)
    dv_ref[...] = dv_acc[mine, :].astype(BF16)


def back_near(deps, meta, q, do, o, logs, near, own, tab, dq_part):
    loc, d = do.shape
    n = ROOT + TILE
    return pl.pallas_call(
        after(len(deps), back_near_kernel),
        grid=(d // 128,),
        in_specs=[ANY] * len(deps) + [SMEM, pair(loc), pair(loc), pair(loc), log_spec(loc), pair(n), pair(n), pair(loc), pair(loc)]
        + [fixed(one.shape) for one in tab] + [pair(loc)],
        out_specs=[pair(loc)] * 3 + [pair(TILE)] * 2,
        out_shape=[shape(loc, d, BF16)] * 3 + [shape(TILE, d, BF16)] * 2,
        scratch_shapes=[bias_scratch(0)[1], line_scratch(loc, BF16), line_scratch(loc, BF16), line_scratch(loc, F32),
                        line_scratch(loc, F32)],
        compiler_params=params(),
        cost_estimate=cost(25),
        name="back_near",
    )(*deps, meta, q, do, o, logs, *near, *own, *tab, dq_part)


def spread_kernel(dk_ref, dv_ref, xn_ref, xs_ref, wk_ref, wv_ref, early_ref, late_ref, sum_ref):
    step = pl.program_id(0)
    da = dot(dk_ref[...], wk_ref[...], COLS) + dot(dv_ref[...], wv_ref[...], COLS)

    @pl.when(step < EARLY // BLOCK)
    def _():
        early_ref[...] = da.astype(BF16)

    @pl.when(step >= EARLY // BLOCK)
    def _():
        late_ref[...] = da.astype(BF16)

    x = jnp.where(step < ROOT // BLOCK, xn_ref[...], xs_ref[...]).astype(F32)

    @pl.when(step == 0)
    def _():
        sum_ref[...] = jnp.zeros_like(sum_ref)

    sum_ref[0:1, :] += jnp.sum(da * (x * inv_rms(x)), axis=0, keepdims=True)


def spread(deps, dk, dv, x_near, x_slot, w):
    d = w.shape[0]
    near, early = ROOT // BLOCK, EARLY // BLOCK
    at = lambda f: pl.BlockSpec((BLOCK, d), lambda i: (f(i), 0))
    return pl.pallas_call(
        after(len(deps), spread_kernel),
        grid=(FAR // BLOCK,),
        in_specs=[ANY] * len(deps) + [at(lambda i: i), at(lambda i: i), at(lambda i: jnp.minimum(i, near - 1)), at(lambda i: jnp.maximum(i - near, 0)),
                  weight(d, 1), weight(d, 2)],
        out_specs=[at(lambda i: jnp.minimum(i, early - 1)), at(lambda i: jnp.maximum(i - early, 0)),
                   pl.BlockSpec((8, d), lambda i: (0, 0))],
        out_shape=[shape(EARLY, d, BF16), shape(FAR - EARLY, d, BF16), shape(8, d, F32)],
        compiler_params=params(),
        cost_estimate=cost(6),
        name="spread",
    )(*deps, dk, dv, x_near, x_slot, w, w)


def own_back_kernel(x_ref, xe_ref, dq_ref, dk_ref, dv_ref, dke_ref, dve_ref, wq_ref, wk_ref, wv_ref, da_ref, edge_ref, sum_ref):
    step = pl.program_id(0)
    wk, wv = wk_ref[...], wv_ref[...]

    def gain_part(da, x):
        x = x.astype(F32)
        return jnp.sum(da * (x * inv_rms(x)), axis=0, keepdims=True)

    @pl.when(step == 0)
    def _():
        edge = dot(dke_ref[...], wk, COLS) + dot(dve_ref[...], wv, COLS)
        edge_ref[...] = edge.astype(BF16)
        sum_ref[...] = jnp.zeros_like(sum_ref)
        sum_ref[0:1, :] = gain_part(edge, xe_ref[pl.ds(ROOT, TILE), :])

    da = dot(dq_ref[...], wq_ref[...], COLS) + dot(dk_ref[...], wk, COLS) + dot(dv_ref[...], wv, COLS)
    da_ref[...] = da
    sum_ref[0:1, :] += gain_part(da, x_ref[...])


def own_back(deps, x, x_near, dq, dk, dv, dke, dve, w):
    loc, d = x.shape
    n = loc // 2
    return pl.pallas_call(
        after(len(deps), own_back_kernel),
        grid=(2,),
        in_specs=[ANY] * len(deps) + [tiled(n, d), fixed(x_near.shape), tiled(n, d), tiled(n, d), tiled(n, d), fixed((TILE, d)), fixed((TILE, d)),
                  weight(d, 0), weight(d, 1), weight(d, 2)],
        out_specs=[tiled(n, d), pl.BlockSpec((TILE, d), lambda i: (0, 0)), pl.BlockSpec((8, d), lambda i: (0, 0))],
        out_shape=[shape(loc, d, F32), shape(TILE, d, BF16), shape(8, d, F32)],
        compiler_params=params(),
        cost_estimate=cost(6),
        name="own_back",
    )(*deps, x, x_near, dq, dk, dv, dke, dve, w, w, w)


def weights_kernel(at_ref, s1_ref, s2_ref, s3_ref, a_ref, an_ref, as_ref, dhb_ref, dq_ref, dk_ref, dv_ref, dkf_ref, dvf_ref,
                   dke_ref, dve_ref, o_ref, kept_ref, away_ref, kept_gain, away_gain):
    step = pl.program_id(0)
    core = at_ref[1] % 2
    chips, rows, d = kept_ref.shape

    def put(total, kept, away):
        split_cores(core, total.astype(BF16).reshape(chips, 2, rows, total.shape[1]), kept, away, (slice(None),) * 3)

    def keyed(own, far, edge):
        root, tail = pl.ds(0, ROOT), pl.ds(ROOT, TILE)
        return (dot(a_ref[...], own[...], ROWS) + dot(an_ref[root, :], far[root, :], ROWS)
                + dot(as_ref[...], far[pl.ds(ROOT, SLOTS), :], ROWS) + dot(an_ref[tail, :], edge[...], ROWS))

    @pl.when(step == 0)
    def _():
        line = lax.broadcasted_iota(jnp.int32, (GAIN_LANES, d), 0)
        table = jnp.where(line == 0, s1_ref[0:1, :] + s2_ref[0:1, :], jnp.where(line == 1, s3_ref[0:1, :], 0.0))
        put(table.T, kept_gain, away_gain)
        put(dot(a_ref[...], dq_ref[...], ROWS), kept_ref, away_ref)

    @pl.when(step == 1)
    def _():
        put(keyed(dk_ref, dkf_ref, dke_ref), kept_ref, away_ref)

    @pl.when(step == 2)
    def _():
        put(keyed(dv_ref, dvf_ref, dve_ref), kept_ref, away_ref)

    @pl.when(step == 3)
    def _():
        put(dot(dhb_ref[...], o_ref[...], ROWS), kept_ref, away_ref)


def weight_sums(deps, at, sums, a_own, a_near, a_slot, dhb, dq, dk, dv, dkf, dvf, dke, dve, o, dp):
    loc, d = a_own.shape
    chips, rows = dp // 2, d // dp
    arrays = (*sums, a_own, a_near, a_slot, dhb, dq, dk, dv, dkf, dvf, dke, dve, o)
    out = pl.BlockSpec((chips, rows, d), lambda i: (0, 0, i))
    gain = pl.BlockSpec((chips, rows, GAIN_LANES), lambda i: (0, 0, 0))
    return pl.pallas_call(
        after(len(deps), weights_kernel),
        grid=(4,),
        in_specs=[ANY] * len(deps) + [SMEM] + [fixed(one.shape) for one in arrays],
        out_specs=[out, out, gain, gain],
        out_shape=[jax.ShapeDtypeStruct((chips, rows, 4 * d), BF16)] * 2 + [jax.ShapeDtypeStruct((chips, rows, GAIN_LANES), BF16)] * 2,
        compiler_params=params(),
        cost_estimate=cost(14),
        name="weight_sums",
    )(*deps, at, *arrays)


def finish_kernel(meta_ref, da_ref, dh_ref, x_ref, gain_ref, early_ref, late_ref, low_ref, edge_ref, out_ref):
    t = meta_ref[0, 5]
    tiles = x_ref.shape[0] // TILE

    def one(i, carry):
        here = aligned(i * TILE, TILE)
        given = meta_ref[i, 4]
        x = x_ref[here, :].astype(F32)
        scale = inv_rms(x)
        x_hat = x * scale
        gain = gain_ref[0:1, :]
        da = da_ref[here, :]
        none = jnp.zeros((TILE, x.shape[1]), F32)
        late = late_ref[aligned(jnp.maximum(given, 0), TILE), :].astype(F32)
        early = early_ref[aligned(jnp.minimum(i * TILE, EARLY - TILE), TILE), :].astype(F32)
        da = da + jnp.where(given >= 0, late, none)
        da = da + jnp.where((t == 0) & (i < EARLY // TILE), early, none)
        last = i == tiles - 1
        da = da + jnp.where(last & (meta_ref[0, 6] > 0), low_ref[...].astype(F32), none)
        da = da + jnp.where(last & (t % 2 == 0), edge_ref[...].astype(F32), none)
        scaled = da * gain
        out_ref[here, :] = dh_ref[here, :] + scale * (scaled - x_hat * jnp.mean(scaled * x_hat, axis=-1, keepdims=True))
        return carry

    lax.fori_loop(0, tiles, one, 0)


def finish(meta, da, dh, x, gains, early, late, low, edge):
    loc, d = x.shape
    arrays = (da, dh, x, gains, early, late, low, edge)
    return pl.pallas_call(
        finish_kernel,
        grid=(1,),
        in_specs=[SMEM] + [fixed(one.shape) for one in arrays],
        out_specs=fixed((loc, d)),
        out_shape=shape(loc, d, F32),
        compiler_params=params(),
        cost_estimate=cost(6),
        name="finish",
    )(meta, *arrays)


def tables(pos):
    half = HEAD_DIM // 2
    freq = jnp.exp(-jnp.log(10000.0) * (2.0 * jnp.arange(half, dtype=F32) / HEAD_DIM))
    angle = pos.astype(F32)[:, None] * jnp.concatenate([freq, freq, freq, freq])[None, :]
    sign = jnp.where(jnp.arange(2 * HEAD_DIM) % HEAD_DIM < half, -1.0, 1.0).astype(F32)
    return jnp.cos(angle), jnp.sin(angle) * sign[None, :]


def swap(x, axis, mask):
    return lax.ppermute(x, axis, [(i, i ^ mask) for i in range(lax.axis_size(axis))])


def send(x, *pairs):
    return lax.ppermute(x, "tensor", list(pairs))


def three(g):
    high = lax.reduce_precision(g, 8, 7)
    mid = lax.reduce_precision(g - high, 8, 7)
    return [high.astype(BF16), mid.astype(BF16), (g - high - mid).astype(BF16)]


def total_kernel(own_ref, *refs):
    ins, out_ref = refs[:-1], refs[-1]
    out_ref[...] = sum((one[...].astype(F32) for one in ins), own_ref[...].astype(F32)).astype(BF16)


def total(deps, *parts):
    one = fixed(parts[0].shape)
    return pl.pallas_call(
        after(len(deps), total_kernel),
        grid=(1,),
        in_specs=[ANY] * len(deps) + [one] * len(parts),
        out_specs=one,
        out_shape=jax.ShapeDtypeStruct(parts[0].shape, BF16),
        compiler_params=params(),
        cost_estimate=cost(3),
        name="total",
    )(*deps, *parts)


def meet_chips(deps, part, chip):
    blocks = [lax.dynamic_index_in_dim(part, chip ^ m, 0, keepdims=False) for m in range(part.shape[0])]
    moved = [swap(block, "dp", 2 * m) for m, block in enumerate(blocks) if m]
    return total(deps, blocks[0], *moved)


def per_device(tokens, gain_attn, w_query, w_key, w_value, w_out, gain_ffn, w_gate, w_up, w_down,
               segment_ids, parent_ids, positions, cotangent):
    loc, d = tokens.shape
    t_size, t_at = lax.axis_size("tensor"), lax.axis_index("tensor")
    d_size, d_at = lax.axis_size("dp"), lax.axis_index("dp")
    tiles = loc // TILE
    own_gain = gain_attn.shape[0]
    rows, hid = w_gate.shape
    n = w_query.shape[1]
    at = jnp.stack([t_at, d_at]).astype(jnp.int32)

    up = [(i, i + 1) for i in range(t_size - 1)]
    a1 = send(tokens[:ROOT], *up)
    gain_cols = jnp.stack(three(gain_attn) + three(gain_ffn), axis=1)
    gain_cols = lax.dynamic_update_slice(jnp.zeros((rows, GAIN_LANES), BF16), gain_cols, (t_at * own_gain, 0))
    pack = jnp.concatenate([w_query, w_key, w_value, w_out.T, gain_cols], axis=1)
    others = [pack] + [swap(pack, "tensor", m) for m in range(1, t_size)]
    lined = line((a1,), others)
    a2 = send(a1, *up[1:])
    pieces = [None] * d_size
    for m in range(0, d_size, 2):
        pieces[m] = swap(lined, "dp", m) if m else lined
    ready = (a2, *(pieces[m] for m in range(2, d_size, 2)))
    rest = join(ready, w_gate, w_up, w_down.T)
    b1 = send(join(ready, tokens[ROOT:]), *up)
    a3 = send(a2, *up[2:])
    for m in range(0, d_size, 2):
        pieces[m + 1] = swap(pieces[m], "dp", 1)
    if rows % 16:
        whole = jnp.zeros((d_size * rows, lined.shape[1]), BF16)
        for m in range(d_size):
            whole = lax.dynamic_update_slice_in_dim(whole, pieces[m], (d_at ^ m) * rows, 0)
        pieces = [whole]
    rest = lax.all_gather(rest, ("dp", "tensor"), axis=0, tiled=False).reshape(d_size, t_size, rows, 3 * hid)
    meta, slots = plan(at[:1], segment_ids, parent_ids, tiles)
    tab = tables(positions)
    w, gains, a_own, q, k_own, v_own = project_own((), at, tokens, tab, pieces)
    front = join((a3, k_own), tokens[ROOT:])
    b2 = send(front, (0, 2), (1, 3))
    b3 = send(front, (0, 3))
    x_near, a_near, k_near, v_near = project_near(at, tokens, a1, a2, a3, b1, gains, w, tab)
    near, own = (k_near, v_near), (k_own, v_own)
    acc, top, weight_sum = attend_near(meta, q, near, own)
    x_slot, a_slot, k_slot, v_slot = project_far(meta, slots, tokens, (a1, a2, a3, b1, b2, b3), gains, w, tab)
    far = (k_slot, v_slot)
    o, logs = attend_far(meta, q, far, acc, top, weight_sum)

    mixed, do, dhb, dh, ffn_sum, kept, away = feed_forward(at, tokens, o, cotangent, gains, w, rest)
    chip = d_at // 2
    away = swap(away, "dp", 1)
    dq_part, dk_far, dv_far = back_far(meta, slots, q, do, o, logs, near, far, tab)
    rest_part = (kept.astype(F32) + away.astype(F32)).astype(BF16)
    early, late, far_sum = spread((rest_part,), dk_far, dv_far, x_near, x_slot, w)
    rest_sum = meet_chips((), rest_part, chip)
    late_in = send(late, (3, 2))
    early_in = send(early, (3, 2), (1, 0))
    dq, dk, dv, dke, dve = back_near((early, late), meta, q, do, o, logs, near, own, tab, dq_part)
    late = late + late_in
    early = early + early_in
    late_in = send(late, (2, 1))
    early_in = send(early, (2, 0))
    da, edge, own_sum = own_back((rest_sum, late, early), tokens, x_near, dq, dk, dv, dke, dve, w)
    kept, away, kept_gain, away_gain = weight_sums(
        (late_in, early), at, (far_sum, own_sum, ffn_sum), a_own, a_near, a_slot, dhb, dq, dk, dv, dk_far, dv_far, dke, dve, o, d_size)
    edge = send(edge, (1, 0), (3, 2))
    away = swap(jnp.concatenate([away, away_gain], axis=2), "dp", 1)
    part = meet((), kept, kept_gain, away)
    late = late + late_in
    early = early + early_in
    low_edge = send(late[:TILE], (1, 0))
    grad_tokens = finish(meta, da, dh, tokens, gains, early, late, low_edge, edge)
    rest_sum = join((part,), rest_sum.reshape(t_size * rows, 3 * hid)).reshape(rest_sum.shape)
    rest_owned = lax.dynamic_index_in_dim(rest_sum, t_at, 0, keepdims=False).astype(F32)
    for m in range(1, t_size):
        rest_owned = rest_owned + swap(lax.dynamic_index_in_dim(rest_sum, t_at ^ m, 0, keepdims=False), "tensor", m).astype(F32)
    summed = meet_chips((early_in,), part, chip)

    def share(m):
        return jnp.concatenate([summed[:, j * d + m * n:j * d + (m + 1) * n] for j in range(4)] + [summed[:, 4 * d:]], axis=1)

    owned = share(0).astype(F32)
    for m in range(1, t_size):
        owned = owned + swap(share(m), "tensor", m).astype(F32)
    gain_sums = lax.dynamic_slice(owned, (t_at * own_gain, 4 * n), (own_gain, GAIN_LANES))
    return (mixed, grad_tokens, gain_sums[:, 0], owned[:, :n], owned[:, n:2 * n], owned[:, 2 * n:3 * n], owned[:, 3 * n:4 * n].T,
            gain_sums[:, 1], rest_owned[:, :hid], rest_owned[:, hid:2 * hid], rest_owned[:, 2 * hid:].T)


def solution(mesh):
    rows = P(("dp", "tensor"), None)
    gain = P(("dp", "tensor"))
    wide = P("dp", "tensor")
    tall = P("tensor", "dp")
    return jax.shard_map(
        per_device,
        mesh=mesh,
        in_specs=(rows, gain, wide, wide, wide, tall, gain, wide, wide, tall, P("dp"), P("dp"), P("dp"), rows),
        out_specs=(rows, rows, gain, wide, wide, wide, tall, gain, wide, wide, tall),
        check_vma=False,
    )
```

```python
import functools

import jax
import jax.numpy as jnp
from jax import lax
from jax.experimental import pallas as pl
from jax.experimental.pallas import tpu as pltpu
from jax.sharding import PartitionSpec as P

HEAD_DIM = 64
BLOCK = 256
TILE = 128
ROOT = 512
BRANCHES = 4
SLOTS = BRANCHES * BLOCK
FAR = ROOT + SLOTS
EARLY = ROOT + BLOCK
GAIN_LANES = 128
EPSILON = 1e-05
MASKED = -1e30
VMEM = 60 * 1024 * 1024
F32 = jnp.float32
BF16 = jnp.bfloat16
PLAIN = (((1,), (0,)), ((), ()))
ROWS = (((0,), (0,)), ((), ()))
COLS = (((1,), (1,)), ((), ()))


def dot(a, b, dims=PLAIN):
    return lax.dot_general(a, b, dims, preferred_element_type=F32)


def cost(us):
    return pl.CostEstimate(flops=int(us * 3e7), bytes_accessed=0, transcendentals=0)


def params():
    return pltpu.CompilerParams(vmem_limit_bytes=VMEM)


def half_turn(u):
    lane = lax.broadcasted_iota(jnp.int32, u.shape, 1)
    return jnp.where(lane % HEAD_DIM < HEAD_DIM // 2, pltpu.roll(u, 96, 1), pltpu.roll(u, 32, 1))


SMEM = pl.BlockSpec(memory_space=pltpu.SMEM)
ANY = pl.BlockSpec(memory_space=pl.ANY)


def after(count, kernel):
    return lambda *refs: kernel(*refs[count:])


def fixed(shape):
    return pl.BlockSpec(shape, lambda i: (0,) * len(shape), pipeline_mode=pl.Buffered(1))


def tiled(n, w):
    return pl.BlockSpec((n, w), lambda i: (i, 0))


def pair(n):
    return pl.BlockSpec((n, 128), lambda p: (0, p))


def aligned(row, n, unit=TILE):
    return pl.ds(pl.multiple_of(row, unit), n)


def shape(n, w, kind):
    return jax.ShapeDtypeStruct((n, w), kind)


def inv_rms(x):
    return lax.rsqrt(jnp.mean(x * x, axis=-1, keepdims=True) + EPSILON)


def plan_kernel(tiles, blocks, at_ref, seg_ref, par_ref, meta_ref, slot_ref):
    t = at_ref[0]
    first = ROOT // BLOCK
    root = seg_ref[0]
    seg = [seg_ref[b * BLOCK] for b in range(blocks)]
    par = [par_ref[b * BLOCK] for b in range(blocks)]
    rank = []
    count = jnp.int32(0)
    for b in range(blocks):
        rank.append(count)
        if b >= first:
            count = count + (par[b] == root).astype(jnp.int32)
    for beta in range(BRANCHES):
        at = jnp.int32(0)
        for b in range(first, blocks):
            at = jnp.where((par[b] == root) & (rank[b] == beta), b, at)
        for half in range(2):
            sub = 2 * at + half
            h = 2 * beta + half
            slot_ref[h, 0] = sub // tiles
            slot_ref[h, 1] = sub % tiles
            slot_ref[h, 2] = sub
            for j in range(3, 8):
                slot_ref[h, j] = 0
    for i in range(8):
        sub = t * tiles + min(i, tiles - 1)
        block = sub // 2
        mine = par_ref[block * BLOCK]
        leaf = ((mine != root) & (block >= first)).astype(jnp.int32)
        slot = jnp.int32(0)
        for b in range(first, blocks):
            slot = jnp.where((seg[b] == mine) & (par[b] == root), rank[b], slot)
        given = jnp.int32(-1)
        for h in range(2, 2 * BRANCHES):
            given = jnp.where((slot_ref[h, 2] == sub) & (t > 0), (h - 2) * TILE, given)
        meta_ref[i, 0] = sub
        meta_ref[i, 1] = leaf
        meta_ref[i, 2] = slot * leaf * BLOCK
        meta_ref[i, 3] = block * BLOCK - t * tiles * TILE + TILE
        meta_ref[i, 4] = given
        meta_ref[i, 5] = t
        meta_ref[i, 6] = jnp.where(t == 0, (slot_ref[2, 0] == 0).astype(jnp.int32), 0)
        meta_ref[i, 7] = 0


def plan(t_at, seg, par, tiles):
    out = jax.ShapeDtypeStruct((8, 8), jnp.int32)
    return pl.pallas_call(
        functools.partial(plan_kernel, tiles, seg.shape[0] // BLOCK),
        in_specs=[SMEM] * 3,
        out_specs=[SMEM] * 2,
        out_shape=[out, out],
        name="plan",
    )(t_at.reshape(1), seg, par)


def normed(x, gain):
    return (x * inv_rms(x) * gain).astype(BF16)


def rotated(u, cos, sin, out_ref, rows, factor):
    for c in range(u.shape[1] // 128):
        part = u[:, c * 128:(c + 1) * 128]
        r = (part * cos + half_turn(part) * sin).astype(BF16)
        out_ref[rows, c * 128:(c + 1) * 128] = r * factor if factor is not None else r


def line_kernel(out_ref, parts):
    n = (parts[0].shape[1] - GAIN_LANES) // 4
    for j in range(4):
        for r, part in enumerate(parts):
            out_ref[:, (j * len(parts) + r) * n:(j * len(parts) + r + 1) * n] = part[:, j * n:(j + 1) * n]
    out_ref[:, 4 * n * len(parts):] = sum(part[:, 4 * n:] for part in parts)


def line(deps, parts):
    rows, wide = parts[0].shape
    out = (rows, (wide - GAIN_LANES) * len(parts) + GAIN_LANES)
    return pl.pallas_call(
        after(len(deps), lambda *refs: line_kernel(refs[-1], refs[:-1])),
        grid=(1,),
        in_specs=[ANY] * len(deps) + [fixed(one.shape) for one in parts],
        out_specs=fixed(out),
        out_shape=shape(*out, BF16),
        compiler_params=params(),
        cost_estimate=cost(2),
        name="line",
    )(*deps, *parts)


def join_kernel(ins, out_ref):
    at = 0
    for part in ins:
        out_ref[:, at:at + part.shape[1]] = part[...]
        at += part.shape[1]


def join(deps, *parts):
    out = (parts[0].shape[0], sum(part.shape[1] for part in parts))
    return pl.pallas_call(
        after(len(deps), lambda *refs: join_kernel(refs[:-1], refs[-1])),
        grid=(1,),
        in_specs=[ANY] * len(deps) + [fixed(one.shape) for one in parts],
        out_specs=fixed(out),
        out_shape=shape(*out, BF16),
        compiler_params=params(),
        cost_estimate=cost(2),
        name="join",
    )(*deps, *parts)


def begin_kernel(x_ref, *refs):
    ins, rest_ref, front_ref = refs[:-2], refs[-2], refs[-1]
    join_kernel(ins, rest_ref)
    front_ref[...] = x_ref[ROOT:, :]


def begin(deps, x, *parts):
    outs = ((parts[0].shape[0], sum(part.shape[1] for part in parts)), (x.shape[0] - ROOT, x.shape[1]))
    return pl.pallas_call(
        after(len(deps), begin_kernel),
        grid=(1,),
        in_specs=[ANY] * len(deps) + [fixed(one.shape) for one in (x, *parts)],
        out_specs=[fixed(one) for one in outs],
        out_shape=[shape(*one, BF16) for one in outs],
        compiler_params=params(),
        cost_estimate=cost(2),
        name="begin",
    )(*deps, x, *parts)


def cores_kernel(at_ref, kept_ref, away_ref, *outs):
    chip = at_ref[1] // 2
    for m, out_ref in enumerate(outs):
        out_ref[0] = (kept_ref[chip ^ m, 0].astype(F32) + away_ref[chip ^ m, 0].astype(F32)).astype(BF16)


def meet_rest(at, kept, away):
    chips, parts, rows, wide = kept.shape
    block = pl.BlockSpec((chips, 1, rows, wide), lambda i: (0, i, 0, 0))
    out = pl.BlockSpec((1, rows, wide), lambda i: (i, 0, 0))
    return pl.pallas_call(
        cores_kernel,
        grid=(parts,),
        in_specs=[SMEM, block, block],
        out_specs=[out] * chips,
        out_shape=[jax.ShapeDtypeStruct((parts, rows, wide), BF16)] * chips,
        compiler_params=params(),
        cost_estimate=cost(5),
        name="meet_rest",
    )(at, kept, away)


def meet_kernel(count, at_ref, *refs):
    ins, outs = refs[:2 * count], refs[2 * count:]
    chip = at_ref[1] // 2
    for m, out_ref in enumerate(outs):
        at = 0
        for kept, away in zip(ins[:count], ins[count:]):
            n = kept.shape[2]
            out_ref[:, at:at + n] = (kept[chip ^ m].astype(F32) + away[chip ^ m].astype(F32)).astype(BF16)
            at += n


def meet(deps, at, kept, away):
    chips, rows, _ = kept[0].shape
    ins = (*kept, *away)
    out = (rows, sum(one.shape[2] for one in kept))
    return pl.pallas_call(
        after(len(deps), functools.partial(meet_kernel, len(kept))),
        grid=(1,),
        in_specs=[ANY] * len(deps) + [SMEM] + [fixed(one.shape) for one in ins],
        out_specs=[fixed(out)] * chips,
        out_shape=[shape(*out, BF16)] * chips,
        compiler_params=params(),
        cost_estimate=cost(4),
        name="meet",
    )(*deps, at, *ins)


def fold_kernel(at_ref, *refs):
    ins, (keep_ref, send_ref) = refs[:-2], refs[-2:]
    t = at_ref[0]
    half = keep_ref.shape[0]
    for r in range(2 * half):
        got = sum((one[t ^ r].astype(F32) for one in ins[1:]), ins[0][t ^ r].astype(F32)).astype(BF16)
        if r < half:
            keep_ref[r] = got
        else:
            send_ref[r - half] = got


def fold(at, *blocks):
    parts, rows, wide = blocks[0].shape
    out = (parts // 2, rows, wide)
    return pl.pallas_call(
        fold_kernel,
        grid=(1,),
        in_specs=[SMEM] + [fixed(one.shape) for one in blocks],
        out_specs=[fixed(out)] * 2,
        out_shape=[jax.ShapeDtypeStruct(out, BF16)] * 2,
        compiler_params=params(),
        cost_estimate=cost(4),
        name="fold",
    )(at, *blocks)


def middle_kernel(keep_ref, got_ref, mine_ref, send_ref):
    for r, out_ref in enumerate((mine_ref, send_ref)):
        out_ref[...] = (keep_ref[r].astype(F32) + got_ref[r].astype(F32)).astype(BF16)


def middle(deps, keep, got):
    out = keep.shape[1:]
    return pl.pallas_call(
        after(len(deps), middle_kernel),
        grid=(1,),
        in_specs=[ANY] * len(deps) + [fixed(keep.shape)] * 2,
        out_specs=[fixed(out)] * 2,
        out_shape=[shape(*out, BF16)] * 2,
        compiler_params=params(),
        cost_estimate=cost(2),
        name="middle",
    )(*deps, keep, got)


def own_kernel(count, at_ref, x_ref, cos_ref, sin_ref, *refs):
    pieces, (w_ref, gain_ref, a_ref, q_ref, k_ref, v_ref) = refs[:count], refs[count:]
    d = x_ref.shape[1]
    t, dp = at_ref[0], at_ref[1]
    step = pl.program_id(0)

    @pl.when(step == 0)
    def _():
        cols = []
        for m, piece in enumerate(pieces):
            rows = piece.shape[0]
            w_ref[aligned((dp ^ m) * rows if count > 1 else 0, rows, 8), :] = piece[:, :4 * d]
        for j in range(count):
            row = jnp.zeros((pieces[0].shape[0], GAIN_LANES), F32)
            for m, piece in enumerate(pieces):
                row = jnp.where((dp ^ m) == j if count > 1 else True, piece[:, 4 * d:].astype(F32), row)
            cols.append(row)
        table = jnp.concatenate(cols, axis=0).T
        gain_ref[...] = jnp.zeros_like(gain_ref)
        gain_ref[0:1, :] = table[0:1, :] + table[1:2, :] + table[2:3, :]
        gain_ref[1:2, :] = table[3:4, :] + table[4:5, :] + table[5:6, :]

    n = x_ref.shape[0]
    here = aligned(t * (n * pl.num_programs(0)) + step * n, n, 16)
    cos, sin = cos_ref[here, :], sin_ref[here, :]
    a = normed(x_ref[...].astype(F32), gain_ref[0:1, :])
    a_ref[...] = a
    rotated(dot(a, w_ref[:, :d]), cos, sin, q_ref, slice(None), jnp.asarray(HEAD_DIM ** -0.5, BF16))
    rotated(dot(a, w_ref[:, d:2 * d]), cos, sin, k_ref, slice(None), None)
    v_ref[...] = dot(a, w_ref[:, 2 * d:3 * d]).astype(BF16)


def project_own(deps, at, x, tab, pieces):
    loc, d = x.shape
    n = loc // 2
    return pl.pallas_call(
        after(len(deps), functools.partial(own_kernel, len(pieces))),
        grid=(2,),
        in_specs=[ANY] * len(deps) + [SMEM, tiled(n, d), fixed(tab[0].shape), fixed(tab[0].shape)] + [fixed(one.shape) for one in pieces],
        out_specs=[pl.BlockSpec((d, 4 * d), lambda i: (0, 0)), pl.BlockSpec((8, d), lambda i: (0, 0))] + [tiled(n, d)] * 4,
        out_shape=[shape(d, 4 * d, BF16), shape(8, d, F32)] + [shape(loc, d, BF16)] * 4,
        compiler_params=params(),
        cost_estimate=cost(10),
        name="project_own",
    )(*deps, at, x, *tab, *pieces)


def near_rows_kernel(at_ref, x_ref, r1_ref, r2_ref, r3_ref, f1_ref, gain_ref, wk_ref, wv_ref, cos_ref, sin_ref,
                     x_out, a_ref, k_ref, v_ref):
    t = at_ref[0]
    loc = x_ref.shape[0]
    root = pl.ds(0, ROOT)
    edge = pl.ds(ROOT, TILE)

    @pl.when(t == 0)
    def _():
        x_out[root, :] = x_ref[root, :]

    for at, ref in ((1, r1_ref), (2, r2_ref), (3, r3_ref)):
        @pl.when(t == at)
        def _():
            x_out[root, :] = ref[...]

    x_out[edge, :] = f1_ref[f1_ref.shape[0] - TILE:, :]

    a = normed(x_out[...].astype(F32), gain_ref[0:1, :])
    a_ref[...] = a
    k = dot(a, wk_ref[...])
    back = aligned(jnp.maximum(t * loc - TILE, 0), TILE)
    rotated(k[:ROOT], cos_ref[root, :], sin_ref[root, :], k_ref, root, None)
    rotated(k[ROOT:], cos_ref[back, :], sin_ref[back, :], k_ref, edge, None)
    v_ref[...] = dot(a, wv_ref[...]).astype(BF16)


def weight(d, j):
    return pl.BlockSpec((d, d), lambda i: (0, j), pipeline_mode=pl.Buffered(1))


def project_near(at, x, r1, r2, r3, f1, gains, w, tab):
    d = x.shape[1]
    n = ROOT + TILE
    return pl.pallas_call(
        near_rows_kernel,
        grid=(1,),
        in_specs=[SMEM] + [fixed(one.shape) for one in (x, r1, r2, r3, f1, gains)] + [weight(d, 1), weight(d, 2)]
        + [fixed(one.shape) for one in tab],
        out_specs=[fixed((n, d))] * 4,
        out_shape=[shape(n, d, BF16)] * 4,
        compiler_params=params(),
        cost_estimate=cost(5),
        name="project_near",
    )(at, x, r1, r2, r3, f1, gains, w, w, *tab)


def far_rows_kernel(meta_ref, slot_ref, x_ref, a1_ref, a2_ref, a3_ref, b1_ref, b2_ref, b3_ref, gain_ref, wk_ref, wv_ref, cos_ref, sin_ref,
                    x_out, a_ref, k_ref, v_ref):
    t = meta_ref[0, 5]
    for h in range(2 * BRANCHES):
        owner, at = slot_ref[h, 0], slot_ref[h, 1]
        rows = aligned(at * TILE, TILE)
        head = aligned(jnp.minimum(at * TILE, ROOT - TILE), TILE)
        back = aligned(jnp.maximum(at * TILE - ROOT, 0), TILE)
        to = pl.ds(h * TILE, TILE)

        @pl.when(owner > t)
        def _():
            x_out[to, :] = jnp.zeros((TILE, x_out.shape[1]), BF16)

        @pl.when(owner == t)
        def _():
            x_out[to, :] = x_ref[rows, :]

        for hop, a_from, b_from in ((1, a1_ref, b1_ref), (2, a2_ref, b2_ref), (3, a3_ref, b3_ref)):
            @pl.when((owner + hop == t) & (at < ROOT // TILE))
            def _():
                x_out[to, :] = a_from[head, :]

            @pl.when((owner + hop == t) & (at >= ROOT // TILE))
            def _():
                x_out[to, :] = b_from[back, :]

    a = normed(x_out[...].astype(F32), gain_ref[0:1, :])
    a_ref[...] = a
    k = dot(a, wk_ref[...])
    for h in range(2 * BRANCHES):
        back = aligned(slot_ref[h, 2] * TILE, TILE)
        rotated(k[h * TILE:(h + 1) * TILE], cos_ref[back, :], sin_ref[back, :], k_ref, pl.ds(h * TILE, TILE), None)
    v_ref[...] = dot(a, wv_ref[...]).astype(BF16)


def project_far(meta, slots, x, ups, gains, w, tab):
    d = x.shape[1]
    return pl.pallas_call(
        far_rows_kernel,
        grid=(1,),
        in_specs=[SMEM, SMEM] + [fixed(one.shape) for one in (x, *ups, gains)] + [weight(d, 1), weight(d, 2)]
        + [fixed(one.shape) for one in tab],
        out_specs=[fixed((SLOTS, d))] * 4,
        out_shape=[shape(SLOTS, d, BF16)] * 4,
        compiler_params=params(),
        cost_estimate=cost(7),
        name="project_far",
    )(meta, slots, x, *ups, gains, w, w, *tab)


def fill_bias(root_ref, own_ref, keys_axis):
    for ref in (root_ref, own_ref):
        if ref is None:
            continue
        key = lax.broadcasted_iota(jnp.int32, ref.shape[1:], keys_axis)
        row = lax.broadcasted_iota(jnp.int32, ref.shape[1:], 1 - keys_axis) % TILE
        for s in range(ref.shape[0]):
            ref[s] = jnp.where(key <= row + s * TILE, 0.0, MASKED).astype(F32)


def low_half():
    return lax.broadcasted_iota(jnp.int32, (TILE, 128), 1) < HEAD_DIM


def both(low, x):
    none = jnp.zeros_like(x)
    return jnp.concatenate([jnp.where(low, x, none), jnp.where(low, none, x)], axis=0)


def diagonal(x):
    return jnp.concatenate([x[:HEAD_DIM, :TILE], x[HEAD_DIM:, TILE:]], axis=0)


def per_half(row):
    upper = lax.broadcasted_iota(jnp.int32, (128, TILE), 0) < HEAD_DIM
    return jnp.where(upper, row[:, :TILE], row[:, TILE:])


def tile_of(meta_ref, i):
    return (meta_ref[i, 0], meta_ref[i, 1], aligned(meta_ref[i, 2], BLOCK), aligned(meta_ref[i, 3], BLOCK),
            aligned(i * TILE, TILE))


def line_up(to_ref, near_ref, own_ref):
    loc = own_ref.shape[0]
    to_ref[pl.ds(0, TILE), :] = near_ref[pl.ds(ROOT, TILE), :]
    to_ref[pl.ds(TILE, loc), :] = own_ref[...]
    to_ref[pl.ds(TILE + loc, TILE), :] = jnp.zeros((TILE, 128), to_ref.dtype)


def soften(q, spans):
    s = [dot(kk, q, COLS) if b is None else dot(kk, q, COLS) + b for kk, _, b in spans]
    top = functools.reduce(jnp.maximum, [jnp.max(part, axis=0, keepdims=True) for part in s])
    return s, top


def weigh(s, top, spans):
    e = [jnp.exp(part - top) for part in s]
    total = sum(jnp.sum(part, axis=0, keepdims=True) for part in e)
    return diagonal(sum(dot(vt, part.astype(BF16)) for part, (_, vt, _) in zip(e, spans))), total


def attend_near_kernel(meta_ref, q_ref, kn_ref, vn_ref, k_ref, v_ref, acc_ref, stat_ref, root_ref, own_ref, ko_ref, vo_ref, vr_ref):
    @pl.when(pl.program_id(0) == 0)
    def _():
        fill_bias(root_ref, own_ref, 0)

    loc = q_ref.shape[0]
    line_up(ko_ref, kn_ref, k_ref)
    root = pl.ds(0, ROOT)
    vr_ref[...] = vn_ref[root, :].T
    vo_ref[:, :TILE] = vn_ref[pl.ds(ROOT, TILE), :].T
    vo_ref[:, TILE:TILE + loc] = v_ref[...].T
    vo_ref[:, TILE + loc:] = jnp.zeros((128, TILE), BF16)
    low = low_half()
    stat_ref[...] = jnp.zeros_like(stat_ref)

    def one(i, rooted):
        sub, leaf, par, own, here = tile_of(meta_ref, i)
        q = both(low, q_ref[here, :])
        spans = [(kn_ref[root, :], vr_ref[...], root_ref[i] if rooted else None)]
        if not rooted:
            spans.append((ko_ref[own, :], vo_ref[:, own], own_ref[sub % 2]))
        s, top = soften(q, spans)
        acc, total = weigh(s, top, spans)
        acc_ref[:, here] = acc
        for h in range(2):
            stat_ref[0, h:h + 1, here] = top[:, h * TILE:(h + 1) * TILE]
            stat_ref[0, 2 + h:3 + h, here] = total[:, h * TILE:(h + 1) * TILE]

    tiles = loc // TILE

    @pl.when(meta_ref[0, 0] > 0)
    def _():
        for i in range(tiles):
            one(i, False)

    @pl.when(meta_ref[0, 0] == 0)
    def _():
        for i in range(tiles):
            one(i, i < ROOT // TILE)


def bias_scratch(keys_axis):
    def one(n):
        return pltpu.VMEM((n // TILE,) + ((n, 2 * TILE) if keys_axis == 0 else (2 * TILE, n)), F32)
    return one(ROOT), one(BLOCK)


def line_scratch(loc, kind):
    return pltpu.VMEM((loc + 2 * TILE, 128), kind)


def attend_near(meta, q, near, own):
    loc, d = q.shape
    n = ROOT + TILE
    return pl.pallas_call(
        attend_near_kernel,
        grid=(d // 128,),
        in_specs=[SMEM, pair(loc), pair(n), pair(n), pair(loc), pair(loc)],
        out_specs=[pl.BlockSpec((128, loc), lambda p: (p, 0)), log_spec(loc)],
        out_shape=[shape(d, loc, F32), jax.ShapeDtypeStruct((d // 128, 8, loc), F32)],
        scratch_shapes=[*bias_scratch(0), line_scratch(loc, BF16), pltpu.VMEM((128, loc + 2 * TILE), BF16), pltpu.VMEM((128, ROOT), BF16)],
        compiler_params=params(),
        cost_estimate=cost(20),
        name="attend_near",
    )(meta, q, *near, *own)


def attend_far_kernel(meta_ref, q_ref, ks_ref, vs_ref, acc_ref, stat_ref, o_ref, l_ref, vt_ref):
    low = low_half()
    vt_ref[...] = vs_ref[...].T
    l_ref[...] = jnp.zeros_like(l_ref)
    for i in range(o_ref.shape[0] // TILE):
        sub, leaf, par, own, here = tile_of(meta_ref, i)
        stat = stat_ref[0, :, here]
        old = jnp.concatenate([stat[0:1], stat[1:2]], axis=1)
        old_total = jnp.concatenate([stat[2:3], stat[3:4]], axis=1)
        spans = [(ks_ref[par, :], vt_ref[:, par], jnp.where(leaf > 0, 0.0, MASKED).astype(F32))]
        s, top = soften(both(low, q_ref[here, :]), spans)
        top = jnp.maximum(top, old)
        new, total = weigh(s, top, spans)
        fade = jnp.exp(old - top)
        total = old_total * fade + total
        out = (acc_ref[:, here] * per_half(fade) + new) / per_half(total)
        o_ref[here, :] = out.T.astype(BF16)
        log = top + jnp.log(total)
        for h in range(2):
            l_ref[0, h:h + 1, here] = log[:, h * TILE:(h + 1) * TILE]


def log_spec(loc):
    return pl.BlockSpec((1, 8, loc), lambda p: (p, 0, 0))


def attend_far(meta, q, far, acc, stat):
    loc, d = q.shape
    return pl.pallas_call(
        attend_far_kernel,
        grid=(d // 128,),
        in_specs=[SMEM, pair(loc), pair(SLOTS), pair(SLOTS), pl.BlockSpec((128, loc), lambda p: (p, 0)), log_spec(loc)],
        out_specs=[pair(loc), log_spec(loc)],
        out_shape=[shape(loc, d, BF16), jax.ShapeDtypeStruct((d // 128, 8, loc), F32)],
        scratch_shapes=[pltpu.VMEM((128, SLOTS), BF16)],
        compiler_params=params(),
        cost_estimate=cost(9),
        name="attend_far",
    )(meta, q, *far, acc, stat)


def split_cores(core, got, kept_ref, away_ref, where):
    @pl.when(core == 0)
    def _():
        kept_ref[where] = got[:, 0]
        away_ref[where] = got[:, 1]

    @pl.when(core == 1)
    def _():
        kept_ref[where] = got[:, 1]
        away_ref[where] = got[:, 0]


def ffn_kernel(at_ref, x_ref, o_ref, ct_ref, gain_ref, wo_ref, w_ref,
               mixed_ref, do_ref, dhb_ref, dh_ref, sum_ref, kept_ref, away_ref, c_s, m_s, dg_s, du_s, ct_t, c_t):
    step = pl.program_id(0)
    loc, d = ct_ref.shape
    n = x_ref.shape[0]
    parts, hid = m_s.shape[0], m_s.shape[2]

    def slab(t, j):
        return w_ref[:, t, :, j * hid:(j + 1) * hid].reshape(d, hid)

    @pl.when(step < loc // n)
    def _():
        here = aligned(step * n, n, 16)
        ct = ct_ref[here, :]
        h = x_ref[...].astype(F32) + dot(o_ref[...], wo_ref[...], COLS)
        scale = inv_rms(h)
        c_hat = h * scale
        gain = gain_ref[1:2, :]
        c = (c_hat * gain).astype(BF16)
        c_s[here, :] = c
        y = h
        dc = jnp.zeros_like(h)
        for t in range(parts):
            g = dot(c, slab(t, 0))
            u = dot(c, slab(t, 1))
            dm = dot(ct, slab(t, 2))
            sig = jax.nn.sigmoid(g)
            silu = g * sig
            m = (silu * u).astype(BF16)
            dg = (dm * u * (sig * (1.0 + g * (1.0 - sig)))).astype(BF16)
            du = (dm * silu).astype(BF16)
            y = y + dot(m, slab(t, 2), COLS)
            dc = dc + dot(dg, slab(t, 0), COLS) + dot(du, slab(t, 1), COLS)
            m_s[t, here, :] = m
            dg_s[t, here, :] = dg
            du_s[t, here, :] = du
        mixed_ref[...] = y.astype(BF16)
        part = jnp.sum(dc * c_hat, axis=0, keepdims=True)

        @pl.when(step == 0)
        def _():
            sum_ref[...] = jnp.zeros_like(sum_ref)

        sum_ref[0:1, :] += part
        scaled = dc * gain
        dh = ct.astype(F32) + scale * (scaled - c_hat * jnp.mean(scaled * c_hat, axis=-1, keepdims=True))
        dh_ref[...] = dh
        dhb = dh.astype(BF16)
        dhb_ref[...] = dhb
        do_ref[...] = dot(dhb, wo_ref[...]).astype(BF16)

    @pl.when(step == loc // n)
    def _():
        ct_t[...] = ct_ref[...].T
        c_t[...] = c_s[...].T

    @pl.when(step >= loc // n)
    def _():
        t = step - loc // n
        for j, (left, right) in enumerate(((c_t, dg_s), (c_t, du_s), (ct_t, m_s))):
            got = dot(left[...], right[t]).astype(BF16)
            chips, _, rows, _ = kept_ref.shape
            split_cores(at_ref[1] % 2, got.reshape(chips, 2, rows, hid), kept_ref, away_ref,
                        (slice(None), 0, slice(None), slice(j * hid, (j + 1) * hid)))


def feed_forward(at_core, x, o, ct, gains, w, rest):
    loc, d = x.shape
    dp, parts, rows, wide = rest.shape
    hid = wide // 3
    steps = 2
    n = loc // steps
    at = lambda i: (jnp.minimum(i, steps - 1), 0)
    tile = pl.BlockSpec((n, d), at)
    grads = pl.BlockSpec((dp // 2, 1, rows, wide), lambda i: (0, jnp.maximum(i - steps, 0), 0, 0))
    return pl.pallas_call(
        ffn_kernel,
        grid=(steps + parts,),
        in_specs=[SMEM, tile, tile, fixed((loc, d)), fixed((8, d)), weight(d, 3), fixed(rest.shape)],
        out_specs=[tile, tile, tile, tile, pl.BlockSpec((8, d), lambda i: (0, 0)), grads, grads],
        out_shape=[shape(loc, d, BF16), shape(loc, d, BF16), shape(loc, d, BF16), shape(loc, d, F32), shape(8, d, F32)]
        + [jax.ShapeDtypeStruct((dp // 2, parts, rows, wide), BF16)] * 2,
        scratch_shapes=[pltpu.VMEM((loc, d), BF16)] + [pltpu.VMEM((parts, loc, hid), BF16)] * 3 + [pltpu.VMEM((d, loc), BF16)] * 2,
        compiler_params=params(),
        cost_estimate=cost(40),
        name="feed_forward",
    )(at_core, x, o, ct, gains, w, rest)


def unrotate(w, cos, sin):
    return w * cos - half_turn(w) * sin


def back_setup(low, q_ref, do_ref, o_ref, l_ref, here):
    do = do_ref[here, :]
    dots = (do.astype(F32) * o_ref[here, :].astype(F32)).T
    row_dot = [jnp.sum(dots[h * HEAD_DIM:(h + 1) * HEAD_DIM, :], axis=0, keepdims=True) for h in range(2)]
    log = [l_ref[0, h:h + 1, here] for h in range(2)]
    return both(low, q_ref[here, :]), both(low, do), jnp.concatenate(log, axis=1), jnp.concatenate(row_dot, axis=1)


def back_span(setup, kk, vv, kt, bias, acc, dk_acc, dv_acc):
    q, do, log, row_dot = setup
    s = dot(kk, q, COLS)
    if bias is not None:
        s = s + bias
    p = jnp.exp(s - log)
    ds = (p * (dot(vv, do, COLS) - row_dot)).astype(BF16)
    dv_acc[acc, :] += dot(p.astype(BF16), do)
    dk_acc[acc, :] += dot(ds, q)
    return diagonal(dot(kt, ds))


def back_far_kernel(meta_ref, slot_ref, q_ref, do_ref, o_ref, l_ref, kn_ref, vn_ref, ks_ref, vs_ref, cos_ref, sin_ref,
                    dq_ref, dk_ref, dv_ref, root_ref, krt_ref, kst_ref, dk_acc, dv_acc):
    @pl.when(pl.program_id(0) == 0)
    def _():
        fill_bias(root_ref, None, 0)

    low = low_half()
    root = pl.ds(0, ROOT)
    for ref in (dk_acc, dv_acc):
        ref[...] = jnp.zeros_like(ref)
    krt_ref[...] = kn_ref[root, :].T
    kst_ref[...] = ks_ref[...].T
    tiles = do_ref.shape[0] // TILE

    def one(i, rooted):
        sub, leaf, par, own, here = tile_of(meta_ref, i)
        setup = back_setup(low, q_ref, do_ref, o_ref, l_ref, here)
        dq = back_span(setup, kn_ref[root, :], vn_ref[root, :], krt_ref[...], root_ref[i] if rooted else None, root, dk_acc, dv_acc)
        if not rooted:
            acc = aligned(meta_ref[i, 2] + ROOT, BLOCK, BLOCK)
            hide = jnp.where(leaf > 0, 0.0, MASKED).astype(F32)
            dq = dq + back_span(setup, ks_ref[par, :], vs_ref[par, :], kst_ref[:, par], hide, acc, dk_acc, dv_acc)
        dq_ref[:, here] = dq

    @pl.when(meta_ref[0, 0] > 0)
    def _():
        for i in range(tiles):
            one(i, False)

    @pl.when(meta_ref[0, 0] == 0)
    def _():
        for i in range(tiles):
            one(i, i < ROOT // TILE)

    dk_ref[root, :] = unrotate(dk_acc[root, :], cos_ref[root, :], sin_ref[root, :]).astype(BF16)
    for h in range(2 * BRANCHES):
        at, back = pl.ds(ROOT + h * TILE, TILE), aligned(slot_ref[h, 2] * TILE, TILE)
        dk_ref[at, :] = unrotate(dk_acc[at, :], cos_ref[back, :], sin_ref[back, :]).astype(BF16)
    dv_ref[...] = dv_acc[...].astype(BF16)


def turned(loc):
    return pl.BlockSpec((128, loc), lambda p: (p, 0))


def back_far(meta, slots, q, do, o, logs, near, far, tab):
    loc, d = do.shape
    n = ROOT + TILE
    return pl.pallas_call(
        back_far_kernel,
        grid=(d // 128,),
        in_specs=[SMEM, SMEM, pair(loc), pair(loc), pair(loc), log_spec(loc), pair(n), pair(n), pair(SLOTS), pair(SLOTS)]
        + [fixed(one.shape) for one in tab],
        out_specs=[turned(loc), pair(FAR), pair(FAR)],
        out_shape=[shape(d, loc, F32), shape(FAR, d, BF16), shape(FAR, d, BF16)],
        scratch_shapes=[bias_scratch(0)[0], pltpu.VMEM((128, ROOT), BF16), pltpu.VMEM((128, SLOTS), BF16),
                        pltpu.VMEM((FAR, 128), F32), pltpu.VMEM((FAR, 128), F32)],
        compiler_params=params(),
        cost_estimate=cost(50),
        name="back_far",
    )(meta, slots, q, do, o, logs, *near, *far, *tab)


def back_near_kernel(meta_ref, q_ref, do_ref, o_ref, l_ref, kn_ref, vn_ref, k_ref, v_ref, cos_ref, sin_ref, part_ref,
                     dq_ref, dk_ref, dv_ref, dke_ref, dve_ref, own_ref, ko_ref, vo_ref, kt_ref, dk_acc, dv_acc):
    @pl.when(pl.program_id(0) == 0)
    def _():
        fill_bias(None, own_ref, 0)

    line_up(ko_ref, kn_ref, k_ref)
    line_up(vo_ref, vn_ref, v_ref)
    kt_ref[...] = ko_ref[...].T
    low = low_half()
    loc = do_ref.shape[0]
    t = meta_ref[0, 5]
    for ref in (dk_acc, dv_acc):
        ref[...] = jnp.zeros_like(ref)

    def one(i, rooted):
        sub, leaf, par, own, here = tile_of(meta_ref, i)
        dq = part_ref[:, here]
        if not rooted:
            setup = back_setup(low, q_ref, do_ref, o_ref, l_ref, here)
            dq = dq + back_span(setup, ko_ref[own, :], vo_ref[own, :], kt_ref[:, own], own_ref[sub % 2], own, dk_acc, dv_acc)
        back = aligned(sub * TILE, TILE)
        dq_ref[here, :] = unrotate(dq.T * HEAD_DIM ** -0.5, cos_ref[back, :], sin_ref[back, :]).astype(BF16)

    @pl.when(t > 0)
    def _():
        for i in range(loc // TILE):
            one(i, False)

    @pl.when(t == 0)
    def _():
        for i in range(loc // TILE):
            one(i, i < ROOT // TILE)

    edge, mine = pl.ds(0, TILE), pl.ds(TILE, loc)
    before = aligned(jnp.maximum(t * loc - TILE, 0), TILE)
    here = aligned(t * loc, loc)
    dke_ref[...] = unrotate(dk_acc[edge, :], cos_ref[before, :], sin_ref[before, :]).astype(BF16)
    dve_ref[...] = dv_acc[edge, :].astype(BF16)
    dk_ref[...] = unrotate(dk_acc[mine, :], cos_ref[here, :], sin_ref[here, :]).astype(BF16)
    dv_ref[...] = dv_acc[mine, :].astype(BF16)


def back_near(deps, meta, q, do, o, logs, near, own, tab, dq_part):
    loc, d = do.shape
    n = ROOT + TILE
    return pl.pallas_call(
        after(len(deps), back_near_kernel),
        grid=(d // 128,),
        in_specs=[ANY] * len(deps) + [SMEM, pair(loc), pair(loc), pair(loc), log_spec(loc), pair(n), pair(n), pair(loc), pair(loc)]
        + [fixed(one.shape) for one in tab] + [turned(loc)],
        out_specs=[pair(loc)] * 3 + [pair(TILE)] * 2,
        out_shape=[shape(loc, d, BF16)] * 3 + [shape(TILE, d, BF16)] * 2,
        scratch_shapes=[bias_scratch(0)[1], line_scratch(loc, BF16), line_scratch(loc, BF16),
                        pltpu.VMEM((128, loc + 2 * TILE), BF16), line_scratch(loc, F32), line_scratch(loc, F32)],
        compiler_params=params(),
        cost_estimate=cost(25),
        name="back_near",
    )(*deps, meta, q, do, o, logs, *near, *own, *tab, dq_part)


def spread_kernel(dk_ref, dv_ref, xn_ref, xs_ref, wk_ref, wv_ref, early_ref, late_ref, sum_ref):
    step = pl.program_id(0)
    da = dot(dk_ref[...], wk_ref[...], COLS) + dot(dv_ref[...], wv_ref[...], COLS)

    @pl.when(step < EARLY // BLOCK)
    def _():
        early_ref[...] = da.astype(BF16)

    @pl.when(step >= EARLY // BLOCK)
    def _():
        late_ref[...] = da.astype(BF16)

    x = jnp.where(step < ROOT // BLOCK, xn_ref[...], xs_ref[...]).astype(F32)

    @pl.when(step == 0)
    def _():
        sum_ref[...] = jnp.zeros_like(sum_ref)

    sum_ref[0:1, :] += jnp.sum(da * (x * inv_rms(x)), axis=0, keepdims=True)


def spread(deps, dk, dv, x_near, x_slot, w):
    d = w.shape[0]
    near, early = ROOT // BLOCK, EARLY // BLOCK
    at = lambda f: pl.BlockSpec((BLOCK, d), lambda i: (f(i), 0))
    return pl.pallas_call(
        after(len(deps), spread_kernel),
        grid=(FAR // BLOCK,),
        in_specs=[ANY] * len(deps) + [at(lambda i: i), at(lambda i: i), at(lambda i: jnp.minimum(i, near - 1)), at(lambda i: jnp.maximum(i - near, 0)),
                  weight(d, 1), weight(d, 2)],
        out_specs=[at(lambda i: jnp.minimum(i, early - 1)), at(lambda i: jnp.maximum(i - early, 0)),
                   pl.BlockSpec((8, d), lambda i: (0, 0))],
        out_shape=[shape(EARLY, d, BF16), shape(FAR - EARLY, d, BF16), shape(8, d, F32)],
        compiler_params=params(),
        cost_estimate=cost(6),
        name="spread",
    )(*deps, dk, dv, x_near, x_slot, w, w)


def own_back_kernel(x_ref, xe_ref, dq_ref, dk_ref, dv_ref, dke_ref, dve_ref, wq_ref, wk_ref, wv_ref, da_ref, edge_ref, sum_ref):
    step = pl.program_id(0)
    wk, wv = wk_ref[...], wv_ref[...]

    def gain_part(da, x):
        x = x.astype(F32)
        return jnp.sum(da * (x * inv_rms(x)), axis=0, keepdims=True)

    @pl.when(step == 0)
    def _():
        edge = dot(dke_ref[...], wk, COLS) + dot(dve_ref[...], wv, COLS)
        edge_ref[...] = edge.astype(BF16)
        sum_ref[...] = jnp.zeros_like(sum_ref)
        sum_ref[0:1, :] = gain_part(edge, xe_ref[pl.ds(ROOT, TILE), :])

    da = dot(dq_ref[...], wq_ref[...], COLS) + dot(dk_ref[...], wk, COLS) + dot(dv_ref[...], wv, COLS)
    da_ref[...] = da
    sum_ref[0:1, :] += gain_part(da, x_ref[...])


def own_back(deps, x, x_near, dq, dk, dv, dke, dve, w):
    loc, d = x.shape
    n = loc // 2
    return pl.pallas_call(
        after(len(deps), own_back_kernel),
        grid=(2,),
        in_specs=[ANY] * len(deps) + [tiled(n, d), fixed(x_near.shape), tiled(n, d), tiled(n, d), tiled(n, d), fixed((TILE, d)), fixed((TILE, d)),
                  weight(d, 0), weight(d, 1), weight(d, 2)],
        out_specs=[tiled(n, d), pl.BlockSpec((TILE, d), lambda i: (0, 0)), pl.BlockSpec((8, d), lambda i: (0, 0))],
        out_shape=[shape(loc, d, F32), shape(TILE, d, BF16), shape(8, d, F32)],
        compiler_params=params(),
        cost_estimate=cost(6),
        name="own_back",
    )(*deps, x, x_near, dq, dk, dv, dke, dve, w, w, w)


def spill(core, got, kept_ref, away_ref):
    chips, rows, _ = kept_ref.shape
    split_cores(core, got.astype(BF16).reshape(chips, 2, rows, got.shape[1]), kept_ref, away_ref, (slice(None),) * 3)


def keyed(a_ref, an_ref, as_ref, own, far, edge):
    root, tail = pl.ds(0, ROOT), pl.ds(ROOT, TILE)
    return (dot(a_ref[...], own[...], ROWS) + dot(an_ref[root, :], far[root, :], ROWS)
            + dot(as_ref[...], far[pl.ds(ROOT, SLOTS), :], ROWS) + dot(an_ref[tail, :], edge[...], ROWS))


def first_kernel(at_ref, s1_ref, s2_ref, s3_ref, a_ref, dq_ref, dhb_ref, o_ref, kept_ref, away_ref, kept_gain, away_gain):
    step, core = pl.program_id(0), at_ref[1] % 2

    @pl.when(step == 0)
    def _():
        line = lax.broadcasted_iota(jnp.int32, (GAIN_LANES, a_ref.shape[1]), 0)
        table = jnp.where(line == 0, s1_ref[0:1, :] + s2_ref[0:1, :], jnp.where(line == 1, s3_ref[0:1, :], 0.0))
        spill(core, table.T, kept_gain, away_gain)
        spill(core, dot(a_ref[...], dq_ref[...], ROWS), kept_ref, away_ref)

    @pl.when(step == 1)
    def _():
        spill(core, dot(dhb_ref[...], o_ref[...], ROWS), kept_ref, away_ref)


def second_kernel(at_ref, a_ref, an_ref, as_ref, dk_ref, dv_ref, dkf_ref, dvf_ref, dke_ref, dve_ref, kept_ref, away_ref):
    step, core = pl.program_id(0), at_ref[1] % 2

    @pl.when(step == 0)
    def _():
        spill(core, keyed(a_ref, an_ref, as_ref, dk_ref, dkf_ref, dke_ref), kept_ref, away_ref)

    @pl.when(step == 1)
    def _():
        spill(core, keyed(a_ref, an_ref, as_ref, dv_ref, dvf_ref, dve_ref), kept_ref, away_ref)


def weight_sums(kernel, deps, at, arrays, dp, gains):
    d = arrays[-1].shape[1]
    chips, rows = dp // 2, d // dp
    widths = [(2 * d, pl.BlockSpec((chips, rows, d), lambda i: (0, 0, i)))] * 2
    if gains:
        widths += [(GAIN_LANES, pl.BlockSpec((chips, rows, GAIN_LANES), lambda i: (0, 0, 0)))] * 2
    return pl.pallas_call(
        after(len(deps), kernel),
        grid=(2,),
        in_specs=[ANY] * len(deps) + [SMEM] + [fixed(one.shape) for one in arrays],
        out_specs=[spec for _, spec in widths],
        out_shape=[jax.ShapeDtypeStruct((chips, rows, wide), BF16) for wide, _ in widths],
        compiler_params=params(),
        cost_estimate=cost(8),
        name="weight_sums",
    )(*deps, at, *arrays)


def finish_kernel(meta_ref, da_ref, dh_ref, x_ref, gain_ref, early2_ref, late2_ref, early_ref, late_ref, edge_ref, out_ref):
    t = meta_ref[0, 5]
    tiles = x_ref.shape[0] // TILE

    def one(i, carry):
        here = aligned(i * TILE, TILE)
        given = meta_ref[i, 4]
        x = x_ref[here, :].astype(F32)
        scale = inv_rms(x)
        x_hat = x * scale
        gain = gain_ref[0:1, :]
        da = da_ref[here, :]
        none = jnp.zeros((TILE, x.shape[1]), F32)
        slot = jnp.maximum(given, 0)
        late = late_ref[aligned(slot, TILE), :].astype(F32) + late2_ref[aligned(slot, TILE), :].astype(F32)
        front = aligned(jnp.minimum(i * TILE, EARLY - TILE), TILE)
        early = early_ref[front, :].astype(F32) + early2_ref[front, :].astype(F32)
        da = da + jnp.where(given >= 0, late, none)
        da = da + jnp.where((t == 0) & (i < EARLY // TILE), early, none)
        da = da + jnp.where((i == tiles - 1) & (t % 2 == 0), edge_ref[...].astype(F32), none)
        scaled = da * gain
        out_ref[here, :] = dh_ref[here, :] + scale * (scaled - x_hat * jnp.mean(scaled * x_hat, axis=-1, keepdims=True))
        return carry

    lax.fori_loop(0, tiles, one, 0)


def finish(deps, meta, da, dh, x, gains, early2, late2, early, late, edge):
    loc, d = x.shape
    arrays = (da, dh, x, gains, early2, late2, early, late, edge)
    return pl.pallas_call(
        after(len(deps), finish_kernel),
        grid=(1,),
        in_specs=[ANY] * len(deps) + [SMEM] + [fixed(one.shape) for one in arrays],
        out_specs=fixed((loc, d)),
        out_shape=shape(loc, d, F32),
        compiler_params=params(),
        cost_estimate=cost(6),
        name="finish",
    )(*deps, meta, *arrays)


def tables(pos):
    half = HEAD_DIM // 2
    freq = jnp.exp(-jnp.log(10000.0) * (2.0 * jnp.arange(half, dtype=F32) / HEAD_DIM))
    angle = pos.astype(F32)[:, None] * jnp.concatenate([freq, freq, freq, freq])[None, :]
    sign = jnp.where(jnp.arange(2 * HEAD_DIM) % HEAD_DIM < half, -1.0, 1.0).astype(F32)
    return jnp.cos(angle), jnp.sin(angle) * sign[None, :]


def swap(x, axis, mask):
    return lax.ppermute(x, axis, [(i, i ^ mask) for i in range(lax.axis_size(axis))])


def send(x, *pairs):
    return lax.ppermute(x, "tensor", list(pairs))


def three(g):
    high = lax.reduce_precision(g, 8, 7)
    mid = lax.reduce_precision(g - high, 8, 7)
    return [high.astype(BF16), mid.astype(BF16), (g - high - mid).astype(BF16)]


def total_kernel(own_ref, *refs):
    ins, out_ref = refs[:-1], refs[-1]
    out_ref[...] = sum((one[...].astype(F32) for one in ins), own_ref[...].astype(F32)).astype(BF16)


def total(deps, *parts):
    one = fixed(parts[0].shape)
    return pl.pallas_call(
        after(len(deps), total_kernel),
        grid=(1,),
        in_specs=[ANY] * len(deps) + [one] * len(parts),
        out_specs=one,
        out_shape=jax.ShapeDtypeStruct(parts[0].shape, BF16),
        compiler_params=params(),
        cost_estimate=cost(3),
        name="total",
    )(*deps, *parts)


def meet_chips(deps, blocks):
    return total(deps, blocks[0], *(swap(block, "dp", 2 * m) for m, block in enumerate(blocks) if m))


def per_device(tokens, gain_attn, w_query, w_key, w_value, w_out, gain_ffn, w_gate, w_up, w_down,
               segment_ids, parent_ids, positions, cotangent):
    loc, d = tokens.shape
    t_size, t_at = lax.axis_size("tensor"), lax.axis_index("tensor")
    d_size, d_at = lax.axis_size("dp"), lax.axis_index("dp")
    tiles = loc // TILE
    own_gain = gain_attn.shape[0]
    rows, hid = w_gate.shape
    n = w_query.shape[1]
    at = jnp.stack([t_at, d_at]).astype(jnp.int32)

    up = [(i, i + 1) for i in range(t_size - 1)]
    a1 = send(tokens[:ROOT], *up)
    gain_cols = jnp.stack(three(gain_attn) + three(gain_ffn), axis=1)
    gain_cols = lax.dynamic_update_slice(jnp.zeros((rows, GAIN_LANES), BF16), gain_cols, (t_at * own_gain, 0))
    pack = jnp.concatenate([w_query, w_key, w_value, w_out.T, gain_cols], axis=1)
    others = [pack] + [swap(pack, "tensor", m) for m in range(1, t_size)]
    meta, slots = plan(at[:1], segment_ids, parent_ids, tiles)
    tab = tables(positions)
    lined = line((a1, *tab), others)
    a2 = send(a1, *up[1:])
    pieces = [None] * d_size
    for m in range(0, d_size, 2):
        pieces[m] = swap(lined, "dp", m) if m else lined
    ready = (a2, *(pieces[m] for m in range(2, d_size, 2)))
    rest, front = begin(ready, tokens, w_gate, w_up, w_down.T)
    b1 = send(front, *up)
    a3 = send(a2, *up[2:])
    for m in range(0, d_size, 2):
        pieces[m + 1] = swap(pieces[m], "dp", 1)
    if rows % 16:
        whole = jnp.zeros((d_size * rows, lined.shape[1]), BF16)
        for m in range(d_size):
            whole = lax.dynamic_update_slice_in_dim(whole, pieces[m], (d_at ^ m) * rows, 0)
        pieces = [whole]
    rest = lax.all_gather(rest, ("dp", "tensor"), axis=0, tiled=False).reshape(d_size, t_size, rows, 3 * hid)
    w, gains, a_own, q, k_own, v_own = project_own((), at, tokens, tab, pieces)
    front = join((a3, k_own), tokens[ROOT:])
    b2 = send(front, (0, 2), (1, 3))
    b3 = send(front, (0, 3))
    x_near, a_near, k_near, v_near = project_near(at, tokens, a1, a2, a3, b1, gains, w, tab)
    near, own = (k_near, v_near), (k_own, v_own)
    acc, stat = attend_near(meta, q, near, own)
    x_slot, a_slot, k_slot, v_slot = project_far(meta, slots, tokens, (a1, a2, a3, b1, b2, b3), gains, w, tab)
    far = (k_slot, v_slot)
    o, logs = attend_far(meta, q, far, acc, stat)

    mixed, do, dhb, dh, ffn_sum, kept, away = feed_forward(at, tokens, o, cotangent, gains, w, rest)
    away = swap(away, "dp", 1)
    dq_part, dk_far, dv_far = back_far(meta, slots, q, do, o, logs, near, far, tab)
    rest_blocks = meet_rest(at, kept, away)
    early, late, far_sum = spread((rest_blocks[0],), dk_far, dv_far, x_near, x_slot, w)
    keep, away = fold(at, rest_blocks[0], *(swap(block, "dp", 2 * m) for m, block in enumerate(rest_blocks) if m))
    early_in = send(early, (3, 2), (1, 0))
    dq, dk, dv, dke, dve = back_near((early,), meta, q, do, o, logs, near, own, tab, dq_part)
    late_in = send(join((dq,), late), (3, 2))
    early = total((dq,), early, early_in)
    early_in = send(early, (2, 0))
    da, edge, own_sum = own_back((early,), tokens, x_near, dq, dk, dv, dke, dve, w)
    kept_a, away_a, kept_gain, away_gain = weight_sums(
        first_kernel, (keep,), at, (far_sum, own_sum, ffn_sum, a_own, dq, dhb, o), d_size, True)
    away_a = swap(jnp.concatenate([away_a, away_gain], axis=2), "dp", 1)
    late = total((dq,), late, late_in)
    late_in = send(late, (2, 1))
    kept_b, away_b = weight_sums(
        second_kernel, (keep, late, early_in), at, (a_own, a_near, a_slot, dk, dv, dk_far, dv_far, dke, dve), d_size, False)
    away = swap(away, "tensor", 2)
    away_b = swap(away_b, "dp", 1)
    kept_a = jnp.concatenate([kept_a, kept_gain], axis=2)
    blocks = meet((), at, (kept_a, kept_b), (away_a, away_b))
    summed = meet_chips((late_in,), blocks)
    mine, away = middle((summed,), keep, away)
    rest_owned = mine.astype(F32) + swap(away, "tensor", 1).astype(F32)
    crossing = (slots[2, 0] == 0) & (t_at == 1)
    edge = send(edge + jnp.where(crossing, late[:TILE] + late_in[:TILE], jnp.zeros_like(edge)), (1, 0), (3, 2))
    grad_tokens = finish((summed,), meta, da, dh, tokens, gains, early, late, early_in, late_in, edge)
    starts = (0, d, 2 * d + GAIN_LANES, 3 * d + GAIN_LANES)

    def share(m):
        return jnp.concatenate([summed[:, at + m * n:at + (m + 1) * n] for at in starts] + [summed[:, 2 * d:2 * d + GAIN_LANES]], axis=1)

    owned = share(0).astype(F32)
    for m in range(1, t_size):
        owned = owned + swap(share(m), "tensor", m).astype(F32)
    gain_sums = lax.dynamic_slice(owned, (t_at * own_gain, 4 * n), (own_gain, GAIN_LANES))
    return (mixed, grad_tokens, gain_sums[:, 0], owned[:, :n], owned[:, 2 * n:3 * n], owned[:, 3 * n:4 * n], owned[:, n:2 * n].T,
            gain_sums[:, 1], rest_owned[:, :hid], rest_owned[:, hid:2 * hid], rest_owned[:, 2 * hid:].T)


def solution(mesh):
    rows = P(("dp", "tensor"), None)
    gain = P(("dp", "tensor"))
    wide = P("dp", "tensor")
    tall = P("tensor", "dp")
    return jax.shard_map(
        per_device,
        mesh=mesh,
        in_specs=(rows, gain, wide, wide, wide, tall, gain, wide, wide, tall, P("dp"), P("dp"), P("dp"), rows),
        out_specs=(rows, rows, gain, wide, wide, wide, tall, gain, wide, wide, tall),
        check_vma=False,
    )
```

```python
import functools

import jax
import jax.numpy as jnp
from jax import lax
from jax.experimental import pallas as pl
from jax.experimental.pallas import tpu as pltpu
from jax.sharding import PartitionSpec as P

HEAD_DIM = 64
BLOCK = 256
TILE = 128
ROOT = 512
BRANCHES = 4
SLOTS = BRANCHES * BLOCK
FAR = ROOT + SLOTS
EARLY = ROOT + BLOCK
GAIN_LANES = 128
EPSILON = 1e-05
MASKED = -1e30
VMEM = 60 * 1024 * 1024
F32 = jnp.float32
BF16 = jnp.bfloat16
PLAIN = (((1,), (0,)), ((), ()))
ROWS = (((0,), (0,)), ((), ()))
COLS = (((1,), (1,)), ((), ()))


def dot(a, b, dims=PLAIN):
    return lax.dot_general(a, b, dims, preferred_element_type=F32)


def cost(us):
    return pl.CostEstimate(flops=int(us * 3e7), bytes_accessed=0, transcendentals=0)


def params():
    return pltpu.CompilerParams(vmem_limit_bytes=VMEM)


def half_turn(u):
    lane = lax.broadcasted_iota(jnp.int32, u.shape, 1)
    return jnp.where(lane % HEAD_DIM < HEAD_DIM // 2, pltpu.roll(u, 96, 1), pltpu.roll(u, 32, 1))


SMEM = pl.BlockSpec(memory_space=pltpu.SMEM)
ANY = pl.BlockSpec(memory_space=pl.ANY)


def after(count, kernel):
    return lambda *refs: kernel(*refs[count:])


def fixed(shape):
    return pl.BlockSpec(shape, lambda i: (0,) * len(shape), pipeline_mode=pl.Buffered(1))


def tiled(n, w):
    return pl.BlockSpec((n, w), lambda i: (i, 0))


def pair(n):
    return pl.BlockSpec((n, 128), lambda p: (0, p))


def aligned(row, n, unit=TILE):
    return pl.ds(pl.multiple_of(row, unit), n)


def shape(n, w, kind):
    return jax.ShapeDtypeStruct((n, w), kind)


def inv_rms(x):
    return lax.rsqrt(jnp.mean(x * x, axis=-1, keepdims=True) + EPSILON)


def plan_kernel(tiles, blocks, at_ref, seg_ref, par_ref, meta_ref, slot_ref):
    t = at_ref[0]
    first = ROOT // BLOCK
    root = seg_ref[0]
    seg = [seg_ref[b * BLOCK] for b in range(blocks)]
    par = [par_ref[b * BLOCK] for b in range(blocks)]
    rank = []
    count = jnp.int32(0)
    for b in range(blocks):
        rank.append(count)
        if b >= first:
            count = count + (par[b] == root).astype(jnp.int32)
    for beta in range(BRANCHES):
        at = jnp.int32(0)
        for b in range(first, blocks):
            at = jnp.where((par[b] == root) & (rank[b] == beta), b, at)
        for half in range(2):
            sub = 2 * at + half
            h = 2 * beta + half
            slot_ref[h, 0] = sub // tiles
            slot_ref[h, 1] = sub % tiles
            slot_ref[h, 2] = sub
            for j in range(3, 8):
                slot_ref[h, j] = 0
    for i in range(8):
        sub = t * tiles + min(i, tiles - 1)
        block = sub // 2
        mine = par_ref[block * BLOCK]
        leaf = ((mine != root) & (block >= first)).astype(jnp.int32)
        slot = jnp.int32(0)
        for b in range(first, blocks):
            slot = jnp.where((seg[b] == mine) & (par[b] == root), rank[b], slot)
        given = jnp.int32(-1)
        for h in range(2, 2 * BRANCHES):
            given = jnp.where((slot_ref[h, 2] == sub) & (t > 0), (h - 2) * TILE, given)
        meta_ref[i, 0] = sub
        meta_ref[i, 1] = leaf
        meta_ref[i, 2] = slot * leaf * BLOCK
        meta_ref[i, 3] = block * BLOCK - t * tiles * TILE + TILE
        meta_ref[i, 4] = given
        meta_ref[i, 5] = t
        meta_ref[i, 6] = jnp.where(t == 0, (slot_ref[2, 0] == 0).astype(jnp.int32), 0)
        meta_ref[i, 7] = 0


def plan(t_at, seg, par, tiles):
    out = jax.ShapeDtypeStruct((8, 8), jnp.int32)
    return pl.pallas_call(
        functools.partial(plan_kernel, tiles, seg.shape[0] // BLOCK),
        in_specs=[SMEM] * 3,
        out_specs=[SMEM] * 2,
        out_shape=[out, out],
        name="plan",
    )(t_at.reshape(1), seg, par)


def normed(x, gain):
    return (x * inv_rms(x) * gain).astype(BF16)


def rotated(u, cos, sin, out_ref, rows, factor):
    for c in range(u.shape[1] // 128):
        part = u[:, c * 128:(c + 1) * 128]
        r = (part * cos + half_turn(part) * sin).astype(BF16)
        out_ref[rows, c * 128:(c + 1) * 128] = r * factor if factor is not None else r


def line_kernel(out_ref, parts):
    n = (parts[0].shape[1] - GAIN_LANES) // 4
    for j in range(4):
        for r, part in enumerate(parts):
            out_ref[:, (j * len(parts) + r) * n:(j * len(parts) + r + 1) * n] = part[:, j * n:(j + 1) * n]
    out_ref[:, 4 * n * len(parts):] = sum(part[:, 4 * n:] for part in parts)


def line(deps, parts):
    rows, wide = parts[0].shape
    out = (rows, (wide - GAIN_LANES) * len(parts) + GAIN_LANES)
    return pl.pallas_call(
        after(len(deps), lambda *refs: line_kernel(refs[-1], refs[:-1])),
        grid=(1,),
        in_specs=[ANY] * len(deps) + [fixed(one.shape) for one in parts],
        out_specs=fixed(out),
        out_shape=shape(*out, BF16),
        compiler_params=params(),
        cost_estimate=cost(2),
        name="line",
    )(*deps, *parts)


def join_kernel(ins, out_ref):
    at = 0
    for part in ins:
        out_ref[:, at:at + part.shape[1]] = part[...]
        at += part.shape[1]


def join(deps, *parts):
    out = (parts[0].shape[0], sum(part.shape[1] for part in parts))
    return pl.pallas_call(
        after(len(deps), lambda *refs: join_kernel(refs[:-1], refs[-1])),
        grid=(1,),
        in_specs=[ANY] * len(deps) + [fixed(one.shape) for one in parts],
        out_specs=fixed(out),
        out_shape=shape(*out, BF16),
        compiler_params=params(),
        cost_estimate=cost(2),
        name="join",
    )(*deps, *parts)


def begin_kernel(x_ref, *refs):
    ins, rest_ref, front_ref = refs[:-2], refs[-2], refs[-1]
    join_kernel(ins, rest_ref)
    front_ref[...] = x_ref[ROOT:, :]


def begin(deps, x, *parts):
    outs = ((parts[0].shape[0], sum(part.shape[1] for part in parts)), (x.shape[0] - ROOT, x.shape[1]))
    return pl.pallas_call(
        after(len(deps), begin_kernel),
        grid=(1,),
        in_specs=[ANY] * len(deps) + [fixed(one.shape) for one in (x, *parts)],
        out_specs=[fixed(one) for one in outs],
        out_shape=[shape(*one, BF16) for one in outs],
        compiler_params=params(),
        cost_estimate=cost(2),
        name="begin",
    )(*deps, x, *parts)


def cores_kernel(at_ref, kept_ref, away_ref, *outs):
    chip = at_ref[1] // 2
    for m, out_ref in enumerate(outs):
        out_ref[0] = (kept_ref[chip ^ m, 0].astype(F32) + away_ref[chip ^ m, 0].astype(F32)).astype(BF16)


def meet_rest(at, kept, away):
    chips, parts, rows, wide = kept.shape
    block = pl.BlockSpec((chips, 1, rows, wide), lambda i: (0, i, 0, 0))
    out = pl.BlockSpec((1, rows, wide), lambda i: (i, 0, 0))
    return pl.pallas_call(
        cores_kernel,
        grid=(parts,),
        in_specs=[SMEM, block, block],
        out_specs=[out] * chips,
        out_shape=[jax.ShapeDtypeStruct((parts, rows, wide), BF16)] * chips,
        compiler_params=params(),
        cost_estimate=cost(5),
        name="meet_rest",
    )(at, kept, away)


def meet_kernel(count, at_ref, *refs):
    ins, outs = refs[:2 * count], refs[2 * count:]
    chip = at_ref[1] // 2
    for m, out_ref in enumerate(outs):
        at = 0
        for kept, away in zip(ins[:count], ins[count:]):
            n = kept.shape[2]
            out_ref[:, at:at + n] = (kept[chip ^ m].astype(F32) + away[chip ^ m].astype(F32)).astype(BF16)
            at += n


def meet(deps, at, kept, away):
    chips, rows, _ = kept[0].shape
    ins = (*kept, *away)
    out = (rows, sum(one.shape[2] for one in kept))
    return pl.pallas_call(
        after(len(deps), functools.partial(meet_kernel, len(kept))),
        grid=(1,),
        in_specs=[ANY] * len(deps) + [SMEM] + [fixed(one.shape) for one in ins],
        out_specs=[fixed(out)] * chips,
        out_shape=[shape(*out, BF16)] * chips,
        compiler_params=params(),
        cost_estimate=cost(4),
        name="meet",
    )(*deps, at, *ins)


def fold_kernel(at_ref, *refs):
    ins, (keep_ref, send_ref) = refs[:-2], refs[-2:]
    t = at_ref[0]
    half = keep_ref.shape[0]
    for r in range(2 * half):
        got = sum((one[t ^ r].astype(F32) for one in ins[1:]), ins[0][t ^ r].astype(F32)).astype(BF16)
        if r < half:
            keep_ref[r] = got
        else:
            send_ref[r - half] = got


def fold(deps, at, *blocks):
    parts, rows, wide = blocks[0].shape
    out = (parts // 2, rows, wide)
    return pl.pallas_call(
        after(len(deps), fold_kernel),
        grid=(1,),
        in_specs=[ANY] * len(deps) + [SMEM] + [fixed(one.shape) for one in blocks],
        out_specs=[fixed(out)] * 2,
        out_shape=[jax.ShapeDtypeStruct(out, BF16)] * 2,
        compiler_params=params(),
        cost_estimate=cost(4),
        name="fold",
    )(*deps, at, *blocks)


def middle_kernel(keep_ref, got_ref, mine_ref, send_ref):
    for r, out_ref in enumerate((mine_ref, send_ref)):
        out_ref[...] = (keep_ref[r].astype(F32) + got_ref[r].astype(F32)).astype(BF16)


def middle(deps, keep, got):
    out = keep.shape[1:]
    return pl.pallas_call(
        after(len(deps), middle_kernel),
        grid=(1,),
        in_specs=[ANY] * len(deps) + [fixed(keep.shape)] * 2,
        out_specs=[fixed(out)] * 2,
        out_shape=[shape(*out, BF16)] * 2,
        compiler_params=params(),
        cost_estimate=cost(2),
        name="middle",
    )(*deps, keep, got)


def own_kernel(count, at_ref, x_ref, cos_ref, sin_ref, *refs):
    pieces, (w_ref, gain_ref, a_ref, q_ref, k_ref, v_ref) = refs[:count], refs[count:]
    d = x_ref.shape[1]
    t, dp = at_ref[0], at_ref[1]
    step = pl.program_id(0)

    @pl.when(step == 0)
    def _():
        cols = []
        for m, piece in enumerate(pieces):
            rows = piece.shape[0]
            w_ref[aligned((dp ^ m) * rows if count > 1 else 0, rows, 8), :] = piece[:, :4 * d]
        for j in range(count):
            row = jnp.zeros((pieces[0].shape[0], GAIN_LANES), F32)
            for m, piece in enumerate(pieces):
                row = jnp.where((dp ^ m) == j if count > 1 else True, piece[:, 4 * d:].astype(F32), row)
            cols.append(row)
        table = jnp.concatenate(cols, axis=0).T
        gain_ref[...] = jnp.zeros_like(gain_ref)
        gain_ref[0:1, :] = table[0:1, :] + table[1:2, :] + table[2:3, :]
        gain_ref[1:2, :] = table[3:4, :] + table[4:5, :] + table[5:6, :]

    n = x_ref.shape[0]
    here = aligned(t * (n * pl.num_programs(0)) + step * n, n, 16)
    cos, sin = cos_ref[here, :], sin_ref[here, :]
    a = normed(x_ref[...].astype(F32), gain_ref[0:1, :])
    a_ref[...] = a
    rotated(dot(a, w_ref[:, :d]), cos, sin, q_ref, slice(None), jnp.asarray(HEAD_DIM ** -0.5, BF16))
    rotated(dot(a, w_ref[:, d:2 * d]), cos, sin, k_ref, slice(None), None)
    v_ref[...] = dot(a, w_ref[:, 2 * d:3 * d]).astype(BF16)


def project_own(deps, at, x, tab, pieces):
    loc, d = x.shape
    n = loc // 2
    return pl.pallas_call(
        after(len(deps), functools.partial(own_kernel, len(pieces))),
        grid=(2,),
        in_specs=[ANY] * len(deps) + [SMEM, tiled(n, d), fixed(tab[0].shape), fixed(tab[0].shape)] + [fixed(one.shape) for one in pieces],
        out_specs=[pl.BlockSpec((d, 4 * d), lambda i: (0, 0)), pl.BlockSpec((8, d), lambda i: (0, 0))] + [tiled(n, d)] * 4,
        out_shape=[shape(d, 4 * d, BF16), shape(8, d, F32)] + [shape(loc, d, BF16)] * 4,
        compiler_params=params(),
        cost_estimate=cost(10),
        name="project_own",
    )(*deps, at, x, *tab, *pieces)


def near_rows_kernel(at_ref, x_ref, r1_ref, r2_ref, r3_ref, f1_ref, gain_ref, wk_ref, wv_ref, cos_ref, sin_ref,
                     x_out, a_ref, k_ref, v_ref):
    t = at_ref[0]
    loc = x_ref.shape[0]
    root = pl.ds(0, ROOT)
    edge = pl.ds(ROOT, TILE)

    @pl.when(t == 0)
    def _():
        x_out[root, :] = x_ref[root, :]

    for at, ref in ((1, r1_ref), (2, r2_ref), (3, r3_ref)):
        @pl.when(t == at)
        def _():
            x_out[root, :] = ref[...]

    x_out[edge, :] = f1_ref[f1_ref.shape[0] - TILE:, :]

    a = normed(x_out[...].astype(F32), gain_ref[0:1, :])
    a_ref[...] = a
    k = dot(a, wk_ref[...])
    back = aligned(jnp.maximum(t * loc - TILE, 0), TILE)
    rotated(k[:ROOT], cos_ref[root, :], sin_ref[root, :], k_ref, root, None)
    rotated(k[ROOT:], cos_ref[back, :], sin_ref[back, :], k_ref, edge, None)
    v_ref[...] = dot(a, wv_ref[...]).astype(BF16)


def weight(d, j):
    return pl.BlockSpec((d, d), lambda i: (0, j), pipeline_mode=pl.Buffered(1))


def project_near(at, x, r1, r2, r3, f1, gains, w, tab):
    d = x.shape[1]
    n = ROOT + TILE
    return pl.pallas_call(
        near_rows_kernel,
        grid=(1,),
        in_specs=[SMEM] + [fixed(one.shape) for one in (x, r1, r2, r3, f1, gains)] + [weight(d, 1), weight(d, 2)]
        + [fixed(one.shape) for one in tab],
        out_specs=[fixed((n, d))] * 4,
        out_shape=[shape(n, d, BF16)] * 4,
        compiler_params=params(),
        cost_estimate=cost(5),
        name="project_near",
    )(at, x, r1, r2, r3, f1, gains, w, w, *tab)


def far_rows_kernel(meta_ref, slot_ref, x_ref, a1_ref, a2_ref, a3_ref, b1_ref, b2_ref, b3_ref, gain_ref, wk_ref, wv_ref, cos_ref, sin_ref,
                    x_out, a_ref, k_ref, v_ref):
    t = meta_ref[0, 5]
    for h in range(2 * BRANCHES):
        owner, at = slot_ref[h, 0], slot_ref[h, 1]
        rows = aligned(at * TILE, TILE)
        head = aligned(jnp.minimum(at * TILE, ROOT - TILE), TILE)
        back = aligned(jnp.maximum(at * TILE - ROOT, 0), TILE)
        to = pl.ds(h * TILE, TILE)

        @pl.when(owner > t)
        def _():
            x_out[to, :] = jnp.zeros((TILE, x_out.shape[1]), BF16)

        @pl.when(owner == t)
        def _():
            x_out[to, :] = x_ref[rows, :]

        for hop, a_from, b_from in ((1, a1_ref, b1_ref), (2, a2_ref, b2_ref), (3, a3_ref, b3_ref)):
            @pl.when((owner + hop == t) & (at < ROOT // TILE))
            def _():
                x_out[to, :] = a_from[head, :]

            @pl.when((owner + hop == t) & (at >= ROOT // TILE))
            def _():
                x_out[to, :] = b_from[back, :]

    a = normed(x_out[...].astype(F32), gain_ref[0:1, :])
    a_ref[...] = a
    k = dot(a, wk_ref[...])
    for h in range(2 * BRANCHES):
        back = aligned(slot_ref[h, 2] * TILE, TILE)
        rotated(k[h * TILE:(h + 1) * TILE], cos_ref[back, :], sin_ref[back, :], k_ref, pl.ds(h * TILE, TILE), None)
    v_ref[...] = dot(a, wv_ref[...]).astype(BF16)


def project_far(meta, slots, x, ups, gains, w, tab):
    d = x.shape[1]
    return pl.pallas_call(
        far_rows_kernel,
        grid=(1,),
        in_specs=[SMEM, SMEM] + [fixed(one.shape) for one in (x, *ups, gains)] + [weight(d, 1), weight(d, 2)]
        + [fixed(one.shape) for one in tab],
        out_specs=[fixed((SLOTS, d))] * 4,
        out_shape=[shape(SLOTS, d, BF16)] * 4,
        compiler_params=params(),
        cost_estimate=cost(7),
        name="project_far",
    )(meta, slots, x, *ups, gains, w, w, *tab)


def fill_bias(root_ref, own_ref, keys_axis):
    for ref in (root_ref, own_ref):
        if ref is None:
            continue
        key = lax.broadcasted_iota(jnp.int32, ref.shape[1:], keys_axis)
        row = lax.broadcasted_iota(jnp.int32, ref.shape[1:], 1 - keys_axis) % TILE
        for s in range(ref.shape[0]):
            ref[s] = jnp.where(key <= row + s * TILE, 0.0, MASKED).astype(F32)


def low_half():
    return lax.broadcasted_iota(jnp.int32, (TILE, 128), 1) < HEAD_DIM


def both(low, x):
    none = jnp.zeros_like(x)
    return jnp.concatenate([jnp.where(low, x, none), jnp.where(low, none, x)], axis=0)


def diagonal(x):
    return jnp.concatenate([x[:HEAD_DIM, :TILE], x[HEAD_DIM:, TILE:]], axis=0)


def per_half(row):
    upper = lax.broadcasted_iota(jnp.int32, (128, TILE), 0) < HEAD_DIM
    return jnp.where(upper, row[:, :TILE], row[:, TILE:])


def tile_of(meta_ref, i):
    return (meta_ref[i, 0], meta_ref[i, 1], aligned(meta_ref[i, 2], BLOCK), aligned(meta_ref[i, 3], BLOCK),
            aligned(i * TILE, TILE))


def line_up(to_ref, near_ref, own_ref):
    loc = own_ref.shape[0]
    to_ref[pl.ds(0, TILE), :] = near_ref[pl.ds(ROOT, TILE), :]
    to_ref[pl.ds(TILE, loc), :] = own_ref[...]
    to_ref[pl.ds(TILE + loc, TILE), :] = jnp.zeros((TILE, 128), to_ref.dtype)


def soften(q, spans):
    s = [dot(kk, q, COLS) if b is None else dot(kk, q, COLS) + b for kk, _, b in spans]
    top = functools.reduce(jnp.maximum, [jnp.max(part, axis=0, keepdims=True) for part in s])
    return s, top


def weigh(s, top, spans):
    e = [jnp.exp(part - top) for part in s]
    total = sum(jnp.sum(part, axis=0, keepdims=True) for part in e)
    return diagonal(sum(dot(vt, part.astype(BF16)) for part, (_, vt, _) in zip(e, spans))), total


def attend_near_kernel(meta_ref, q_ref, kn_ref, vn_ref, k_ref, v_ref, acc_ref, stat_ref, root_ref, own_ref, ko_ref, vo_ref, vr_ref):
    @pl.when(pl.program_id(0) == 0)
    def _():
        fill_bias(root_ref, own_ref, 0)

    loc = q_ref.shape[0]
    line_up(ko_ref, kn_ref, k_ref)
    root = pl.ds(0, ROOT)
    vr_ref[...] = vn_ref[root, :].T
    vo_ref[:, :TILE] = vn_ref[pl.ds(ROOT, TILE), :].T
    vo_ref[:, TILE:TILE + loc] = v_ref[...].T
    vo_ref[:, TILE + loc:] = jnp.zeros((128, TILE), BF16)
    low = low_half()
    stat_ref[...] = jnp.zeros_like(stat_ref)

    def one(i, rooted):
        sub, leaf, par, own, here = tile_of(meta_ref, i)
        q = both(low, q_ref[here, :])
        spans = [(kn_ref[root, :], vr_ref[...], root_ref[i] if rooted else None)]
        if not rooted:
            spans.append((ko_ref[own, :], vo_ref[:, own], own_ref[sub % 2]))
        s, top = soften(q, spans)
        acc, total = weigh(s, top, spans)
        acc_ref[:, here] = acc
        for h in range(2):
            stat_ref[0, h:h + 1, here] = top[:, h * TILE:(h + 1) * TILE]
            stat_ref[0, 2 + h:3 + h, here] = total[:, h * TILE:(h + 1) * TILE]

    tiles = loc // TILE

    @pl.when(meta_ref[0, 0] > 0)
    def _():
        for i in range(tiles):
            one(i, False)

    @pl.when(meta_ref[0, 0] == 0)
    def _():
        for i in range(tiles):
            one(i, i < ROOT // TILE)


def bias_scratch(keys_axis):
    def one(n):
        return pltpu.VMEM((n // TILE,) + ((n, 2 * TILE) if keys_axis == 0 else (2 * TILE, n)), F32)
    return one(ROOT), one(BLOCK)


def line_scratch(loc, kind):
    return pltpu.VMEM((loc + 2 * TILE, 128), kind)


def attend_near(meta, q, near, own):
    loc, d = q.shape
    n = ROOT + TILE
    return pl.pallas_call(
        attend_near_kernel,
        grid=(d // 128,),
        in_specs=[SMEM, pair(loc), pair(n), pair(n), pair(loc), pair(loc)],
        out_specs=[pl.BlockSpec((128, loc), lambda p: (p, 0)), log_spec(loc)],
        out_shape=[shape(d, loc, F32), jax.ShapeDtypeStruct((d // 128, 8, loc), F32)],
        scratch_shapes=[*bias_scratch(0), line_scratch(loc, BF16), pltpu.VMEM((128, loc + 2 * TILE), BF16), pltpu.VMEM((128, ROOT), BF16)],
        compiler_params=params(),
        cost_estimate=cost(20),
        name="attend_near",
    )(meta, q, *near, *own)


def attend_far_kernel(meta_ref, q_ref, ks_ref, vs_ref, acc_ref, stat_ref, o_ref, l_ref, vt_ref):
    low = low_half()
    vt_ref[...] = vs_ref[...].T
    l_ref[...] = jnp.zeros_like(l_ref)
    for i in range(o_ref.shape[0] // TILE):
        sub, leaf, par, own, here = tile_of(meta_ref, i)
        stat = stat_ref[0, :, here]
        old = jnp.concatenate([stat[0:1], stat[1:2]], axis=1)
        old_total = jnp.concatenate([stat[2:3], stat[3:4]], axis=1)
        spans = [(ks_ref[par, :], vt_ref[:, par], jnp.where(leaf > 0, 0.0, MASKED).astype(F32))]
        s, top = soften(both(low, q_ref[here, :]), spans)
        top = jnp.maximum(top, old)
        new, total = weigh(s, top, spans)
        fade = jnp.exp(old - top)
        total = old_total * fade + total
        out = (acc_ref[:, here] * per_half(fade) + new) / per_half(total)
        o_ref[here, :] = out.T.astype(BF16)
        log = top + jnp.log(total)
        for h in range(2):
            l_ref[0, h:h + 1, here] = log[:, h * TILE:(h + 1) * TILE]


def log_spec(loc):
    return pl.BlockSpec((1, 8, loc), lambda p: (p, 0, 0))


def attend_far(meta, q, far, acc, stat):
    loc, d = q.shape
    return pl.pallas_call(
        attend_far_kernel,
        grid=(d // 128,),
        in_specs=[SMEM, pair(loc), pair(SLOTS), pair(SLOTS), pl.BlockSpec((128, loc), lambda p: (p, 0)), log_spec(loc)],
        out_specs=[pair(loc), log_spec(loc)],
        out_shape=[shape(loc, d, BF16), jax.ShapeDtypeStruct((d // 128, 8, loc), F32)],
        scratch_shapes=[pltpu.VMEM((128, SLOTS), BF16)],
        compiler_params=params(),
        cost_estimate=cost(9),
        name="attend_far",
    )(meta, q, *far, acc, stat)


def split_cores(core, got, kept_ref, away_ref, where):
    @pl.when(core == 0)
    def _():
        kept_ref[where] = got[:, 0]
        away_ref[where] = got[:, 1]

    @pl.when(core == 1)
    def _():
        kept_ref[where] = got[:, 1]
        away_ref[where] = got[:, 0]


def ffn_kernel(at_ref, x_ref, o_ref, ct_ref, gain_ref, wo_ref, w_ref,
               mixed_ref, do_ref, dhb_ref, dh_ref, sum_ref, kept_ref, away_ref, c_s, m_s, dg_s, du_s, ct_t, c_t):
    step = pl.program_id(0)
    loc, d = ct_ref.shape
    n = x_ref.shape[0]
    parts, hid = m_s.shape[0], m_s.shape[2]

    def slab(t, j):
        return w_ref[:, t, :, j * hid:(j + 1) * hid].reshape(d, hid)

    @pl.when(step < loc // n)
    def _():
        here = aligned(step * n, n, 16)
        ct = ct_ref[here, :]
        h = x_ref[...].astype(F32) + dot(o_ref[...], wo_ref[...], COLS)
        scale = inv_rms(h)
        c_hat = h * scale
        gain = gain_ref[1:2, :]
        c = (c_hat * gain).astype(BF16)
        c_s[here, :] = c
        y = h
        dc = jnp.zeros_like(h)
        for t in range(parts):
            g = dot(c, slab(t, 0))
            u = dot(c, slab(t, 1))
            dm = dot(ct, slab(t, 2))
            sig = jax.nn.sigmoid(g)
            silu = g * sig
            m = (silu * u).astype(BF16)
            dg = (dm * u * (sig * (1.0 + g * (1.0 - sig)))).astype(BF16)
            du = (dm * silu).astype(BF16)
            y = y + dot(m, slab(t, 2), COLS)
            dc = dc + dot(dg, slab(t, 0), COLS) + dot(du, slab(t, 1), COLS)
            m_s[t, here, :] = m
            dg_s[t, here, :] = dg
            du_s[t, here, :] = du
        mixed_ref[...] = y.astype(BF16)
        part = jnp.sum(dc * c_hat, axis=0, keepdims=True)

        @pl.when(step == 0)
        def _():
            sum_ref[...] = jnp.zeros_like(sum_ref)

        sum_ref[0:1, :] += part
        scaled = dc * gain
        dh = ct.astype(F32) + scale * (scaled - c_hat * jnp.mean(scaled * c_hat, axis=-1, keepdims=True))
        dh_ref[...] = dh
        dhb = dh.astype(BF16)
        dhb_ref[...] = dhb
        do_ref[...] = dot(dhb, wo_ref[...]).astype(BF16)

    @pl.when(step == loc // n)
    def _():
        ct_t[...] = ct_ref[...].T
        c_t[...] = c_s[...].T

    @pl.when(step >= loc // n)
    def _():
        t = step - loc // n
        for j, (left, right) in enumerate(((c_t, dg_s), (c_t, du_s), (ct_t, m_s))):
            got = dot(left[...], right[t]).astype(BF16)
            chips, _, rows, _ = kept_ref.shape
            split_cores(at_ref[1] % 2, got.reshape(chips, 2, rows, hid), kept_ref, away_ref,
                        (slice(None), 0, slice(None), slice(j * hid, (j + 1) * hid)))


def feed_forward(at_core, x, o, ct, gains, w, rest):
    loc, d = x.shape
    dp, parts, rows, wide = rest.shape
    hid = wide // 3
    steps = 2
    n = loc // steps
    at = lambda i: (jnp.minimum(i, steps - 1), 0)
    tile = pl.BlockSpec((n, d), at)
    grads = pl.BlockSpec((dp // 2, 1, rows, wide), lambda i: (0, jnp.maximum(i - steps, 0), 0, 0))
    return pl.pallas_call(
        ffn_kernel,
        grid=(steps + parts,),
        in_specs=[SMEM, tile, tile, fixed((loc, d)), fixed((8, d)), weight(d, 3), fixed(rest.shape)],
        out_specs=[tile, tile, tile, tile, pl.BlockSpec((8, d), lambda i: (0, 0)), grads, grads],
        out_shape=[shape(loc, d, BF16), shape(loc, d, BF16), shape(loc, d, BF16), shape(loc, d, F32), shape(8, d, F32)]
        + [jax.ShapeDtypeStruct((dp // 2, parts, rows, wide), BF16)] * 2,
        scratch_shapes=[pltpu.VMEM((loc, d), BF16)] + [pltpu.VMEM((parts, loc, hid), BF16)] * 3 + [pltpu.VMEM((d, loc), BF16)] * 2,
        compiler_params=params(),
        cost_estimate=cost(40),
        name="feed_forward",
    )(at_core, x, o, ct, gains, w, rest)


def unrotate(w, cos, sin):
    return w * cos - half_turn(w) * sin


def back_setup(low, q_ref, do_ref, o_ref, l_ref, here):
    do = do_ref[here, :]
    dots = (do.astype(F32) * o_ref[here, :].astype(F32)).T
    row_dot = [jnp.sum(dots[h * HEAD_DIM:(h + 1) * HEAD_DIM, :], axis=0, keepdims=True) for h in range(2)]
    log = [l_ref[0, h:h + 1, here] for h in range(2)]
    return both(low, q_ref[here, :]), both(low, do), jnp.concatenate(log, axis=1), jnp.concatenate(row_dot, axis=1)


def back_span(setup, kk, vv, kt, bias, acc, dk_acc, dv_acc):
    q, do, log, row_dot = setup
    s = dot(kk, q, COLS)
    if bias is not None:
        s = s + bias
    p = jnp.exp(s - log)
    ds = (p * (dot(vv, do, COLS) - row_dot)).astype(BF16)
    dv_acc[acc, :] += dot(p.astype(BF16), do)
    dk_acc[acc, :] += dot(ds, q)
    return diagonal(dot(kt, ds))


def back_far_kernel(meta_ref, slot_ref, q_ref, do_ref, o_ref, l_ref, kn_ref, vn_ref, ks_ref, vs_ref, cos_ref, sin_ref,
                    dq_ref, dk_ref, dv_ref, root_ref, krt_ref, kst_ref, dk_acc, dv_acc):
    @pl.when(pl.program_id(0) == 0)
    def _():
        fill_bias(root_ref, None, 0)

    low = low_half()
    root = pl.ds(0, ROOT)
    for ref in (dk_acc, dv_acc):
        ref[...] = jnp.zeros_like(ref)
    krt_ref[...] = kn_ref[root, :].T
    kst_ref[...] = ks_ref[...].T
    tiles = do_ref.shape[0] // TILE

    def one(i, rooted):
        sub, leaf, par, own, here = tile_of(meta_ref, i)
        setup = back_setup(low, q_ref, do_ref, o_ref, l_ref, here)
        dq = back_span(setup, kn_ref[root, :], vn_ref[root, :], krt_ref[...], root_ref[i] if rooted else None, root, dk_acc, dv_acc)
        if not rooted:
            acc = aligned(meta_ref[i, 2] + ROOT, BLOCK, BLOCK)
            hide = jnp.where(leaf > 0, 0.0, MASKED).astype(F32)
            dq = dq + back_span(setup, ks_ref[par, :], vs_ref[par, :], kst_ref[:, par], hide, acc, dk_acc, dv_acc)
        dq_ref[:, here] = dq

    @pl.when(meta_ref[0, 0] > 0)
    def _():
        for i in range(tiles):
            one(i, False)

    @pl.when(meta_ref[0, 0] == 0)
    def _():
        for i in range(tiles):
            one(i, i < ROOT // TILE)

    dk_ref[root, :] = unrotate(dk_acc[root, :], cos_ref[root, :], sin_ref[root, :]).astype(BF16)
    for h in range(2 * BRANCHES):
        at, back = pl.ds(ROOT + h * TILE, TILE), aligned(slot_ref[h, 2] * TILE, TILE)
        dk_ref[at, :] = unrotate(dk_acc[at, :], cos_ref[back, :], sin_ref[back, :]).astype(BF16)
    dv_ref[...] = dv_acc[...].astype(BF16)


def turned(loc):
    return pl.BlockSpec((128, loc), lambda p: (p, 0))


def back_far(meta, slots, q, do, o, logs, near, far, tab):
    loc, d = do.shape
    n = ROOT + TILE
    return pl.pallas_call(
        back_far_kernel,
        grid=(d // 128,),
        in_specs=[SMEM, SMEM, pair(loc), pair(loc), pair(loc), log_spec(loc), pair(n), pair(n), pair(SLOTS), pair(SLOTS)]
        + [fixed(one.shape) for one in tab],
        out_specs=[turned(loc), pair(FAR), pair(FAR)],
        out_shape=[shape(d, loc, F32), shape(FAR, d, BF16), shape(FAR, d, BF16)],
        scratch_shapes=[bias_scratch(0)[0], pltpu.VMEM((128, ROOT), BF16), pltpu.VMEM((128, SLOTS), BF16),
                        pltpu.VMEM((FAR, 128), F32), pltpu.VMEM((FAR, 128), F32)],
        compiler_params=params(),
        cost_estimate=cost(50),
        name="back_far",
    )(meta, slots, q, do, o, logs, *near, *far, *tab)


def back_near_kernel(meta_ref, q_ref, do_ref, o_ref, l_ref, kn_ref, vn_ref, k_ref, v_ref, cos_ref, sin_ref, part_ref,
                     dq_ref, dk_ref, dv_ref, dke_ref, dve_ref, own_ref, ko_ref, vo_ref, kt_ref, dk_acc, dv_acc):
    @pl.when(pl.program_id(0) == 0)
    def _():
        fill_bias(None, own_ref, 0)

    line_up(ko_ref, kn_ref, k_ref)
    line_up(vo_ref, vn_ref, v_ref)
    kt_ref[...] = ko_ref[...].T
    low = low_half()
    loc = do_ref.shape[0]
    t = meta_ref[0, 5]
    for ref in (dk_acc, dv_acc):
        ref[...] = jnp.zeros_like(ref)

    def one(i, rooted):
        sub, leaf, par, own, here = tile_of(meta_ref, i)
        dq = part_ref[:, here]
        if not rooted:
            setup = back_setup(low, q_ref, do_ref, o_ref, l_ref, here)
            dq = dq + back_span(setup, ko_ref[own, :], vo_ref[own, :], kt_ref[:, own], own_ref[sub % 2], own, dk_acc, dv_acc)
        back = aligned(sub * TILE, TILE)
        dq_ref[here, :] = unrotate(dq.T * HEAD_DIM ** -0.5, cos_ref[back, :], sin_ref[back, :]).astype(BF16)

    @pl.when(t > 0)
    def _():
        for i in range(loc // TILE):
            one(i, False)

    @pl.when(t == 0)
    def _():
        for i in range(loc // TILE):
            one(i, i < ROOT // TILE)

    edge, mine = pl.ds(0, TILE), pl.ds(TILE, loc)
    before = aligned(jnp.maximum(t * loc - TILE, 0), TILE)
    here = aligned(t * loc, loc)
    dke_ref[...] = unrotate(dk_acc[edge, :], cos_ref[before, :], sin_ref[before, :]).astype(BF16)
    dve_ref[...] = dv_acc[edge, :].astype(BF16)
    dk_ref[...] = unrotate(dk_acc[mine, :], cos_ref[here, :], sin_ref[here, :]).astype(BF16)
    dv_ref[...] = dv_acc[mine, :].astype(BF16)


def back_near(deps, meta, q, do, o, logs, near, own, tab, dq_part):
    loc, d = do.shape
    n = ROOT + TILE
    return pl.pallas_call(
        after(len(deps), back_near_kernel),
        grid=(d // 128,),
        in_specs=[ANY] * len(deps) + [SMEM, pair(loc), pair(loc), pair(loc), log_spec(loc), pair(n), pair(n), pair(loc), pair(loc)]
        + [fixed(one.shape) for one in tab] + [turned(loc)],
        out_specs=[pair(loc)] * 3 + [pair(TILE)] * 2,
        out_shape=[shape(loc, d, BF16)] * 3 + [shape(TILE, d, BF16)] * 2,
        scratch_shapes=[bias_scratch(0)[1], line_scratch(loc, BF16), line_scratch(loc, BF16),
                        pltpu.VMEM((128, loc + 2 * TILE), BF16), line_scratch(loc, F32), line_scratch(loc, F32)],
        compiler_params=params(),
        cost_estimate=cost(25),
        name="back_near",
    )(*deps, meta, q, do, o, logs, *near, *own, *tab, dq_part)


def spread_kernel(dk_ref, dv_ref, xn_ref, xs_ref, wk_ref, wv_ref, early_ref, late_ref, sum_ref):
    step = pl.program_id(0)
    da = dot(dk_ref[...], wk_ref[...], COLS) + dot(dv_ref[...], wv_ref[...], COLS)

    def gain_part(part, x):
        x = x.astype(F32)
        return jnp.sum(part * (x * inv_rms(x)), axis=0, keepdims=True)

    @pl.when(step == 0)
    def _():
        early_ref[...] = da.astype(BF16)
        sum_ref[...] = jnp.zeros_like(sum_ref)
        sum_ref[0:1, :] = gain_part(da[:ROOT], xn_ref[pl.ds(0, ROOT), :]) + gain_part(da[ROOT:], xs_ref[pl.ds(0, BLOCK), :])

    @pl.when(step == 1)
    def _():
        late_ref[...] = da.astype(BF16)
        sum_ref[0:1, :] += gain_part(da, xs_ref[pl.ds(BLOCK, FAR - EARLY), :])


def spread(deps, dk, dv, x_near, x_slot, w):
    d = w.shape[0]
    once = pl.BlockSpec((EARLY, d), lambda i: (0, 0))
    return pl.pallas_call(
        after(len(deps), spread_kernel),
        grid=(2,),
        in_specs=[ANY] * len(deps) + [tiled(EARLY, d), tiled(EARLY, d), fixed(x_near.shape), fixed(x_slot.shape),
                                      weight(d, 1), weight(d, 2)],
        out_specs=[once, once, pl.BlockSpec((8, d), lambda i: (0, 0))],
        out_shape=[shape(EARLY, d, BF16), shape(FAR - EARLY, d, BF16), shape(8, d, F32)],
        compiler_params=params(),
        cost_estimate=cost(6),
        name="spread",
    )(*deps, dk, dv, x_near, x_slot, w, w)


def own_back_kernel(x_ref, xe_ref, dq_ref, dk_ref, dv_ref, dke_ref, dve_ref, wq_ref, wk_ref, wv_ref, da_ref, edge_ref, sum_ref):
    step = pl.program_id(0)
    wk, wv = wk_ref[...], wv_ref[...]

    def gain_part(da, x):
        x = x.astype(F32)
        return jnp.sum(da * (x * inv_rms(x)), axis=0, keepdims=True)

    @pl.when(step == 0)
    def _():
        edge = dot(dke_ref[...], wk, COLS) + dot(dve_ref[...], wv, COLS)
        edge_ref[...] = edge.astype(BF16)
        sum_ref[...] = jnp.zeros_like(sum_ref)
        sum_ref[0:1, :] = gain_part(edge, xe_ref[pl.ds(ROOT, TILE), :])

    da = dot(dq_ref[...], wq_ref[...], COLS) + dot(dk_ref[...], wk, COLS) + dot(dv_ref[...], wv, COLS)
    da_ref[...] = da
    sum_ref[0:1, :] += gain_part(da, x_ref[...])


def own_back(deps, x, x_near, dq, dk, dv, dke, dve, w):
    loc, d = x.shape
    n = loc // 2
    return pl.pallas_call(
        after(len(deps), own_back_kernel),
        grid=(2,),
        in_specs=[ANY] * len(deps) + [tiled(n, d), fixed(x_near.shape), tiled(n, d), tiled(n, d), tiled(n, d), fixed((TILE, d)), fixed((TILE, d)),
                  weight(d, 0), weight(d, 1), weight(d, 2)],
        out_specs=[tiled(n, d), pl.BlockSpec((TILE, d), lambda i: (0, 0)), pl.BlockSpec((8, d), lambda i: (0, 0))],
        out_shape=[shape(loc, d, F32), shape(TILE, d, BF16), shape(8, d, F32)],
        compiler_params=params(),
        cost_estimate=cost(6),
        name="own_back",
    )(*deps, x, x_near, dq, dk, dv, dke, dve, w, w, w)


def spill(core, got, kept_ref, away_ref, at=0):
    chips, rows, _ = kept_ref.shape
    split_cores(core, got.astype(BF16).reshape(chips, 2, rows, got.shape[1]), kept_ref, away_ref,
                (slice(None), slice(None), slice(at, at + got.shape[1])))


def keyed(a_ref, an_ref, as_ref, own, far, edge):
    root, tail = pl.ds(0, ROOT), pl.ds(ROOT, TILE)
    return (dot(a_ref[...], own[...], ROWS) + dot(an_ref[root, :], far[root, :], ROWS)
            + dot(as_ref[...], far[pl.ds(ROOT, SLOTS), :], ROWS) + dot(an_ref[tail, :], edge[...], ROWS))


def first_kernel(at_ref, s1_ref, s2_ref, s3_ref, a_ref, dq_ref, dhb_ref, o_ref, kept_ref, away_ref):
    core, d = at_ref[1] % 2, a_ref.shape[1]
    line = lax.broadcasted_iota(jnp.int32, (GAIN_LANES, d), 0)
    table = jnp.where(line == 0, s1_ref[0:1, :] + s2_ref[0:1, :], jnp.where(line == 1, s3_ref[0:1, :], 0.0))
    spill(core, dot(a_ref[...], dq_ref[...], ROWS), kept_ref, away_ref)
    spill(core, dot(dhb_ref[...], o_ref[...], ROWS), kept_ref, away_ref, d)
    spill(core, table.T, kept_ref, away_ref, 2 * d)


def second_kernel(at_ref, a_ref, an_ref, as_ref, dk_ref, dv_ref, dkf_ref, dvf_ref, dke_ref, dve_ref, kept_ref, away_ref):
    step, core = pl.program_id(0), at_ref[1] % 2

    @pl.when(step == 0)
    def _():
        spill(core, keyed(a_ref, an_ref, as_ref, dk_ref, dkf_ref, dke_ref), kept_ref, away_ref)

    @pl.when(step == 1)
    def _():
        spill(core, keyed(a_ref, an_ref, as_ref, dv_ref, dvf_ref, dve_ref), kept_ref, away_ref)


def weight_sums(kernel, deps, at, arrays, dp, extra):
    d = arrays[-1].shape[1]
    chips, rows, wide = dp // 2, d // dp, 2 * d + extra
    steps = 1 if extra else 2
    spec = pl.BlockSpec((chips, rows, wide // steps), lambda i: (0, 0, i))
    return pl.pallas_call(
        after(len(deps), kernel),
        grid=(steps,),
        in_specs=[ANY] * len(deps) + [SMEM] + [fixed(one.shape) for one in arrays],
        out_specs=[spec, spec],
        out_shape=[jax.ShapeDtypeStruct((chips, rows, wide), BF16)] * 2,
        compiler_params=params(),
        cost_estimate=cost(8),
        name="weight_sums",
    )(*deps, at, *arrays)


def finish_kernel(meta_ref, da_ref, dh_ref, x_ref, gain_ref, early2_ref, late2_ref, early_ref, late_ref, edge_ref, out_ref):
    t = meta_ref[0, 5]
    tiles = x_ref.shape[0] // TILE

    def one(i, carry):
        here = aligned(i * TILE, TILE)
        given = meta_ref[i, 4]
        x = x_ref[here, :].astype(F32)
        scale = inv_rms(x)
        x_hat = x * scale
        gain = gain_ref[0:1, :]
        da = da_ref[here, :]
        none = jnp.zeros((TILE, x.shape[1]), F32)
        slot = jnp.maximum(given, 0)
        late = late_ref[aligned(slot, TILE), :].astype(F32) + late2_ref[aligned(slot, TILE), :].astype(F32)
        front = aligned(jnp.minimum(i * TILE, EARLY - TILE), TILE)
        early = early_ref[front, :].astype(F32) + early2_ref[front, :].astype(F32)
        da = da + jnp.where(given >= 0, late, none)
        da = da + jnp.where((t == 0) & (i < EARLY // TILE), early, none)
        da = da + jnp.where((i == tiles - 1) & (t % 2 == 0), edge_ref[...].astype(F32), none)
        scaled = da * gain
        out_ref[here, :] = dh_ref[here, :] + scale * (scaled - x_hat * jnp.mean(scaled * x_hat, axis=-1, keepdims=True))
        return carry

    lax.fori_loop(0, tiles, one, 0)


def finish(deps, meta, da, dh, x, gains, early2, late2, early, late, edge):
    loc, d = x.shape
    arrays = (da, dh, x, gains, early2, late2, early, late, edge)
    return pl.pallas_call(
        after(len(deps), finish_kernel),
        grid=(1,),
        in_specs=[ANY] * len(deps) + [SMEM] + [fixed(one.shape) for one in arrays],
        out_specs=fixed((loc, d)),
        out_shape=shape(loc, d, F32),
        compiler_params=params(),
        cost_estimate=cost(6),
        name="finish",
    )(*deps, meta, *arrays)


def tables(pos):
    half = HEAD_DIM // 2
    freq = jnp.exp(-jnp.log(10000.0) * (2.0 * jnp.arange(half, dtype=F32) / HEAD_DIM))
    angle = pos.astype(F32)[:, None] * jnp.concatenate([freq, freq, freq, freq])[None, :]
    sign = jnp.where(jnp.arange(2 * HEAD_DIM) % HEAD_DIM < half, -1.0, 1.0).astype(F32)
    return jnp.cos(angle), jnp.sin(angle) * sign[None, :]


def swap(x, axis, mask):
    return lax.ppermute(x, axis, [(i, i ^ mask) for i in range(lax.axis_size(axis))])


def send(x, *pairs):
    return lax.ppermute(x, "tensor", list(pairs))


def three(g):
    high = lax.reduce_precision(g, 8, 7)
    mid = lax.reduce_precision(g - high, 8, 7)
    return [high.astype(BF16), mid.astype(BF16), (g - high - mid).astype(BF16)]


def total_kernel(own_ref, *refs):
    ins, out_ref = refs[:-1], refs[-1]
    out_ref[...] = sum((one[...].astype(F32) for one in ins), own_ref[...].astype(F32)).astype(BF16)


def total(deps, *parts):
    one = fixed(parts[0].shape)
    return pl.pallas_call(
        after(len(deps), total_kernel),
        grid=(1,),
        in_specs=[ANY] * len(deps) + [one] * len(parts),
        out_specs=one,
        out_shape=jax.ShapeDtypeStruct(parts[0].shape, BF16),
        compiler_params=params(),
        cost_estimate=cost(3),
        name="total",
    )(*deps, *parts)


def meet_chips(deps, blocks):
    return total(deps, blocks[0], *(swap(block, "dp", 2 * m) for m, block in enumerate(blocks) if m))


def per_device(tokens, gain_attn, w_query, w_key, w_value, w_out, gain_ffn, w_gate, w_up, w_down,
               segment_ids, parent_ids, positions, cotangent):
    loc, d = tokens.shape
    t_size, t_at = lax.axis_size("tensor"), lax.axis_index("tensor")
    d_size, d_at = lax.axis_size("dp"), lax.axis_index("dp")
    tiles = loc // TILE
    own_gain = gain_attn.shape[0]
    rows, hid = w_gate.shape
    n = w_query.shape[1]
    at = jnp.stack([t_at, d_at]).astype(jnp.int32)

    up = [(i, i + 1) for i in range(t_size - 1)]
    a1 = send(tokens[:ROOT], *up)
    gain_cols = jnp.stack(three(gain_attn) + three(gain_ffn), axis=1)
    gain_cols = lax.dynamic_update_slice(jnp.zeros((rows, GAIN_LANES), BF16), gain_cols, (t_at * own_gain, 0))
    pack = jnp.concatenate([w_query, w_key, w_value, w_out.T, gain_cols], axis=1)
    others = [pack] + [swap(pack, "tensor", m) for m in range(1, t_size)]
    meta, slots = plan(at[:1], segment_ids, parent_ids, tiles)
    tab = tables(positions)
    lined = line((a1, *tab), others)
    a2 = send(a1, *up[1:])
    pieces = [None] * d_size
    for m in range(0, d_size, 2):
        pieces[m] = swap(lined, "dp", m) if m else lined
    ready = (a2, *(pieces[m] for m in range(2, d_size, 2)))
    rest, front = begin(ready, tokens, w_gate, w_up, w_down.T)
    b1 = send(front, *up)
    a3 = send(a2, *up[2:])
    for m in range(0, d_size, 2):
        pieces[m + 1] = swap(pieces[m], "dp", 1)
    if rows % 16:
        whole = jnp.zeros((d_size * rows, lined.shape[1]), BF16)
        for m in range(d_size):
            whole = lax.dynamic_update_slice_in_dim(whole, pieces[m], (d_at ^ m) * rows, 0)
        pieces = [whole]
    rest = lax.all_gather(rest, ("dp", "tensor"), axis=0, tiled=False).reshape(d_size, t_size, rows, 3 * hid)
    w, gains, a_own, q, k_own, v_own = project_own((), at, tokens, tab, pieces)
    front = join((a3, k_own), tokens[ROOT:])
    b2 = send(front, (0, 2), (1, 3))
    b3 = send(front, (0, 3))
    x_near, a_near, k_near, v_near = project_near(at, tokens, a1, a2, a3, b1, gains, w, tab)
    near, own = (k_near, v_near), (k_own, v_own)
    acc, stat = attend_near(meta, q, near, own)
    x_slot, a_slot, k_slot, v_slot = project_far(meta, slots, tokens, (a1, a2, a3, b1, b2, b3), gains, w, tab)
    far = (k_slot, v_slot)
    o, logs = attend_far(meta, q, far, acc, stat)

    mixed, do, dhb, dh, ffn_sum, kept, away = feed_forward(at, tokens, o, cotangent, gains, w, rest)
    away = swap(away, "dp", 1)
    dq_part, dk_far, dv_far = back_far(meta, slots, q, do, o, logs, near, far, tab)
    rest_blocks = meet_rest(at, kept, away)
    early, late, far_sum = spread((rest_blocks[0],), dk_far, dv_far, x_near, x_slot, w)
    moved = [swap(block, "dp", 2 * m) for m, block in enumerate(rest_blocks) if m]
    early_in = send(early, (3, 2), (1, 0))
    dq, dk, dv, dke, dve = back_near((early,), meta, q, do, o, logs, near, own, tab, dq_part)
    late_in = send(join((dq,), late), (3, 2))
    early = total((dq,), early, early_in)
    early_in = send(early, (2, 0))
    da, edge, own_sum = own_back((early, moved[-1]), tokens, x_near, dq, dk, dv, dke, dve, w)
    kept_b, away_b = weight_sums(
        second_kernel, (da,), at, (a_own, a_near, a_slot, dk, dv, dk_far, dv_far, dke, dve), d_size, 0)
    away_b = swap(away_b, "dp", 1)
    keep, away = fold((kept_b,), at, rest_blocks[0], *moved)
    away = swap(away, "tensor", 2)
    late = total((kept_b,), late, late_in)
    late_in = send(late, (2, 1))
    kept_a, away_a = weight_sums(
        first_kernel, (keep, late, early_in), at, (far_sum, own_sum, ffn_sum, a_own, dq, dhb, o), d_size, GAIN_LANES)
    away_a = swap(away_a, "dp", 1)
    blocks = meet((), at, (kept_a, kept_b), (away_a, away_b))
    summed = meet_chips((late_in,), blocks)
    mine, away = middle((summed,), keep, away)
    rest_owned = mine.astype(F32) + swap(away, "tensor", 1).astype(F32)
    crossing = (slots[2, 0] == 0) & (t_at == 1)
    edge = send(edge + jnp.where(crossing, late[:TILE] + late_in[:TILE], jnp.zeros_like(edge)), (1, 0), (3, 2))
    grad_tokens = finish((summed,), meta, da, dh, tokens, gains, early, late, early_in, late_in, edge)
    starts = (0, d, 2 * d + GAIN_LANES, 3 * d + GAIN_LANES)

    def share(m):
        return jnp.concatenate([summed[:, at + m * n:at + (m + 1) * n] for at in starts] + [summed[:, 2 * d:2 * d + GAIN_LANES]], axis=1)

    owned = share(0).astype(F32)
    for m in range(1, t_size):
        owned = owned + swap(share(m), "tensor", m).astype(F32)
    gain_sums = lax.dynamic_slice(owned, (t_at * own_gain, 4 * n), (own_gain, GAIN_LANES))
    return (mixed, grad_tokens, gain_sums[:, 0], owned[:, :n], owned[:, 2 * n:3 * n], owned[:, 3 * n:4 * n], owned[:, n:2 * n].T,
            gain_sums[:, 1], rest_owned[:, :hid], rest_owned[:, hid:2 * hid], rest_owned[:, 2 * hid:].T)


def solution(mesh):
    rows = P(("dp", "tensor"), None)
    gain = P(("dp", "tensor"))
    wide = P("dp", "tensor")
    tall = P("tensor", "dp")
    return jax.shard_map(
        per_device,
        mesh=mesh,
        in_specs=(rows, gain, wide, wide, wide, tall, gain, wide, wide, tall, P("dp"), P("dp"), P("dp"), rows),
        out_specs=(rows, rows, gain, wide, wide, wide, tall, gain, wide, wide, tall),
        check_vma=False,
    )
```

```python
import functools

import jax
import jax.numpy as jnp
from jax import lax
from jax.experimental import pallas as pl
from jax.experimental.pallas import tpu as pltpu
from jax.sharding import PartitionSpec as P

HEAD_DIM = 64
BLOCK = 256
TILE = 128
ROOT = 512
BRANCHES = 4
SLOTS = BRANCHES * BLOCK
FAR = ROOT + SLOTS
EARLY = ROOT + BLOCK
GAIN_LANES = 128
EPSILON = 1e-05
MASKED = -1e30
VMEM = 60 * 1024 * 1024
F32 = jnp.float32
BF16 = jnp.bfloat16
PLAIN = (((1,), (0,)), ((), ()))
ROWS = (((0,), (0,)), ((), ()))
COLS = (((1,), (1,)), ((), ()))


def dot(a, b, dims=PLAIN):
    return lax.dot_general(a, b, dims, preferred_element_type=F32)


def cost(us):
    return pl.CostEstimate(flops=int(us * 3e7), bytes_accessed=0, transcendentals=0)


def params():
    return pltpu.CompilerParams(vmem_limit_bytes=VMEM)


def half_turn(u):
    lane = lax.broadcasted_iota(jnp.int32, u.shape, 1)
    return jnp.where(lane % HEAD_DIM < HEAD_DIM // 2, pltpu.roll(u, 96, 1), pltpu.roll(u, 32, 1))


SMEM = pl.BlockSpec(memory_space=pltpu.SMEM)
ANY = pl.BlockSpec(memory_space=pl.ANY)


def after(count, kernel):
    return lambda *refs: kernel(*refs[count:])


def fixed(shape):
    return pl.BlockSpec(shape, lambda i: (0,) * len(shape), pipeline_mode=pl.Buffered(1))


def tiled(n, w):
    return pl.BlockSpec((n, w), lambda i: (i, 0))


def pair(n):
    return pl.BlockSpec((n, 128), lambda p: (0, p))


def aligned(row, n, unit=TILE):
    return pl.ds(pl.multiple_of(row, unit), n)


def shape(n, w, kind):
    return jax.ShapeDtypeStruct((n, w), kind)


def inv_rms(x):
    return lax.rsqrt(jnp.mean(x * x, axis=-1, keepdims=True) + EPSILON)


def plan_kernel(tiles, blocks, at_ref, seg_ref, par_ref, meta_ref, slot_ref):
    t = at_ref[0]
    first = ROOT // BLOCK
    root = seg_ref[0]
    seg = [seg_ref[b * BLOCK] for b in range(blocks)]
    par = [par_ref[b * BLOCK] for b in range(blocks)]
    rank = []
    count = jnp.int32(0)
    for b in range(blocks):
        rank.append(count)
        if b >= first:
            count = count + (par[b] == root).astype(jnp.int32)
    for beta in range(BRANCHES):
        at = jnp.int32(0)
        for b in range(first, blocks):
            at = jnp.where((par[b] == root) & (rank[b] == beta), b, at)
        for half in range(2):
            sub = 2 * at + half
            h = 2 * beta + half
            slot_ref[h, 0] = sub // tiles
            slot_ref[h, 1] = sub % tiles
            slot_ref[h, 2] = sub
            for j in range(3, 8):
                slot_ref[h, j] = 0
    for i in range(8):
        sub = t * tiles + min(i, tiles - 1)
        block = sub // 2
        mine = par_ref[block * BLOCK]
        leaf = ((mine != root) & (block >= first)).astype(jnp.int32)
        slot = jnp.int32(0)
        for b in range(first, blocks):
            slot = jnp.where((seg[b] == mine) & (par[b] == root), rank[b], slot)
        given = jnp.int32(-1)
        for h in range(2, 2 * BRANCHES):
            given = jnp.where((slot_ref[h, 2] == sub) & (t > 0), (h - 2) * TILE, given)
        meta_ref[i, 0] = sub
        meta_ref[i, 1] = leaf
        meta_ref[i, 2] = slot * leaf * BLOCK
        meta_ref[i, 3] = block * BLOCK - t * tiles * TILE + TILE
        meta_ref[i, 4] = given
        meta_ref[i, 5] = t
        meta_ref[i, 6] = jnp.where(t == 0, (slot_ref[2, 0] == 0).astype(jnp.int32), 0)
        meta_ref[i, 7] = 0


def plan(t_at, seg, par, tiles):
    out = jax.ShapeDtypeStruct((8, 8), jnp.int32)
    return pl.pallas_call(
        functools.partial(plan_kernel, tiles, seg.shape[0] // BLOCK),
        in_specs=[SMEM] * 3,
        out_specs=[SMEM] * 2,
        out_shape=[out, out],
        name="plan",
    )(t_at.reshape(1), seg, par)


def normed(x, gain):
    return (x * inv_rms(x) * gain).astype(BF16)


def rotated(u, cos, sin, out_ref, rows, factor):
    for c in range(u.shape[1] // 128):
        part = u[:, c * 128:(c + 1) * 128]
        r = (part * cos + half_turn(part) * sin).astype(BF16)
        out_ref[rows, c * 128:(c + 1) * 128] = r * factor if factor is not None else r


def line_kernel(out_ref, parts):
    n = (parts[0].shape[1] - GAIN_LANES) // 4
    for j in range(4):
        for r, part in enumerate(parts):
            out_ref[:, (j * len(parts) + r) * n:(j * len(parts) + r + 1) * n] = part[:, j * n:(j + 1) * n]
    out_ref[:, 4 * n * len(parts):] = sum(part[:, 4 * n:] for part in parts)


def line(deps, parts):
    rows, wide = parts[0].shape
    out = (rows, (wide - GAIN_LANES) * len(parts) + GAIN_LANES)
    return pl.pallas_call(
        after(len(deps), lambda *refs: line_kernel(refs[-1], refs[:-1])),
        grid=(1,),
        in_specs=[ANY] * len(deps) + [fixed(one.shape) for one in parts],
        out_specs=fixed(out),
        out_shape=shape(*out, BF16),
        compiler_params=params(),
        cost_estimate=cost(2),
        name="line",
    )(*deps, *parts)


def join_kernel(ins, out_ref):
    at = 0
    for part in ins:
        out_ref[:, at:at + part.shape[1]] = part[...]
        at += part.shape[1]


def join(deps, *parts):
    out = (parts[0].shape[0], sum(part.shape[1] for part in parts))
    return pl.pallas_call(
        after(len(deps), lambda *refs: join_kernel(refs[:-1], refs[-1])),
        grid=(1,),
        in_specs=[ANY] * len(deps) + [fixed(one.shape) for one in parts],
        out_specs=fixed(out),
        out_shape=shape(*out, BF16),
        compiler_params=params(),
        cost_estimate=cost(2),
        name="join",
    )(*deps, *parts)


def begin_kernel(x_ref, *refs):
    ins, rest_ref, front_ref = refs[:-2], refs[-2], refs[-1]
    join_kernel(ins, rest_ref)
    front_ref[...] = x_ref[ROOT:, :]


def begin(deps, x, *parts):
    outs = ((parts[0].shape[0], sum(part.shape[1] for part in parts)), (x.shape[0] - ROOT, x.shape[1]))
    return pl.pallas_call(
        after(len(deps), begin_kernel),
        grid=(1,),
        in_specs=[ANY] * len(deps) + [fixed(one.shape) for one in (x, *parts)],
        out_specs=[fixed(one) for one in outs],
        out_shape=[shape(*one, BF16) for one in outs],
        compiler_params=params(),
        cost_estimate=cost(2),
        name="begin",
    )(*deps, x, *parts)


def meet_kernel(count, at_ref, *refs):
    ins, outs = refs[:2 * count], refs[2 * count:]
    chip = at_ref[1] // 2
    for m, out_ref in enumerate(outs):
        at = 0
        for kept, away in zip(ins[:count], ins[count:]):
            n = kept.shape[2]
            out_ref[:, at:at + n] = (kept[chip ^ m].astype(F32) + away[chip ^ m].astype(F32)).astype(BF16)
            at += n


def meet(deps, at, kept, away):
    chips, rows, _ = kept[0].shape
    ins = (*kept, *away)
    out = (rows, sum(one.shape[2] for one in kept))
    return pl.pallas_call(
        after(len(deps), functools.partial(meet_kernel, len(kept))),
        grid=(1,),
        in_specs=[ANY] * len(deps) + [SMEM] + [fixed(one.shape) for one in ins],
        out_specs=[fixed(out)] * chips,
        out_shape=[shape(*out, BF16)] * chips,
        compiler_params=params(),
        cost_estimate=cost(4),
        name="meet",
    )(*deps, at, *ins)


def fold_kernel(at_ref, late_ref, in_ref, *refs):
    ins, (keep_ref, send_ref, late_out) = refs[:-3], refs[-3:]
    t = at_ref[0]
    half = keep_ref.shape[0]
    late_out[...] = (late_ref[...].astype(F32) + in_ref[...].astype(F32)).astype(BF16)
    for r in range(2 * half):
        got = sum((one[t ^ r].astype(F32) for one in ins[1:]), ins[0][t ^ r].astype(F32)).astype(BF16)
        if r < half:
            keep_ref[r] = got
        else:
            send_ref[r - half] = got


def fold(deps, at, late, late_in, *blocks):
    parts, rows, wide = blocks[0].shape
    out = (parts // 2, rows, wide)
    return pl.pallas_call(
        after(len(deps), fold_kernel),
        grid=(1,),
        in_specs=[ANY] * len(deps) + [SMEM] + [fixed(one.shape) for one in (late, late_in, *blocks)],
        out_specs=[fixed(out), fixed(out), fixed(late.shape)],
        out_shape=[jax.ShapeDtypeStruct(out, BF16)] * 2 + [jax.ShapeDtypeStruct(late.shape, BF16)],
        compiler_params=params(),
        cost_estimate=cost(4),
        name="fold",
    )(*deps, at, late, late_in, *blocks)


def middle_kernel(keep_ref, got_ref, mine_ref, send_ref):
    for r, out_ref in enumerate((mine_ref, send_ref)):
        out_ref[...] = (keep_ref[r].astype(F32) + got_ref[r].astype(F32)).astype(BF16)


def middle(deps, keep, got):
    out = keep.shape[1:]
    return pl.pallas_call(
        after(len(deps), middle_kernel),
        grid=(1,),
        in_specs=[ANY] * len(deps) + [fixed(keep.shape)] * 2,
        out_specs=[fixed(out)] * 2,
        out_shape=[shape(*out, BF16)] * 2,
        compiler_params=params(),
        cost_estimate=cost(2),
        name="middle",
    )(*deps, keep, got)


def own_kernel(count, at_ref, x_ref, cos_ref, sin_ref, *refs):
    pieces, (w_ref, gain_ref, a_ref, q_ref, k_ref, v_ref) = refs[:count], refs[count:]
    d = x_ref.shape[1]
    t, dp = at_ref[0], at_ref[1]
    step = pl.program_id(0)

    @pl.when(step == 0)
    def _():
        cols = []
        for m, piece in enumerate(pieces):
            rows = piece.shape[0]
            w_ref[aligned((dp ^ m) * rows if count > 1 else 0, rows, 8), :] = piece[:, :4 * d]
        for j in range(count):
            row = jnp.zeros((pieces[0].shape[0], GAIN_LANES), F32)
            for m, piece in enumerate(pieces):
                row = jnp.where((dp ^ m) == j if count > 1 else True, piece[:, 4 * d:].astype(F32), row)
            cols.append(row)
        table = jnp.concatenate(cols, axis=0).T
        gain_ref[...] = jnp.zeros_like(gain_ref)
        gain_ref[0:1, :] = table[0:1, :] + table[1:2, :] + table[2:3, :]
        gain_ref[1:2, :] = table[3:4, :] + table[4:5, :] + table[5:6, :]

    n = x_ref.shape[0]
    here = aligned(t * (n * pl.num_programs(0)) + step * n, n, 16)
    cos, sin = cos_ref[here, :], sin_ref[here, :]
    a = normed(x_ref[...].astype(F32), gain_ref[0:1, :])
    a_ref[...] = a
    rotated(dot(a, w_ref[:, :d]), cos, sin, q_ref, slice(None), jnp.asarray(HEAD_DIM ** -0.5, BF16))
    rotated(dot(a, w_ref[:, d:2 * d]), cos, sin, k_ref, slice(None), None)
    v_ref[...] = dot(a, w_ref[:, 2 * d:3 * d]).astype(BF16)


def project_own(deps, at, x, tab, pieces):
    loc, d = x.shape
    n = loc // 2
    return pl.pallas_call(
        after(len(deps), functools.partial(own_kernel, len(pieces))),
        grid=(2,),
        in_specs=[ANY] * len(deps) + [SMEM, tiled(n, d), fixed(tab[0].shape), fixed(tab[0].shape)] + [fixed(one.shape) for one in pieces],
        out_specs=[pl.BlockSpec((d, 4 * d), lambda i: (0, 0)), pl.BlockSpec((8, d), lambda i: (0, 0))] + [tiled(n, d)] * 4,
        out_shape=[shape(d, 4 * d, BF16), shape(8, d, F32)] + [shape(loc, d, BF16)] * 4,
        compiler_params=params(),
        cost_estimate=cost(10),
        name="project_own",
    )(*deps, at, x, *tab, *pieces)


def near_rows_kernel(at_ref, x_ref, r1_ref, r2_ref, r3_ref, f1_ref, gain_ref, wk_ref, wv_ref, cos_ref, sin_ref,
                     x_out, a_ref, k_ref, v_ref):
    t = at_ref[0]
    loc = x_ref.shape[0]
    root = pl.ds(0, ROOT)
    edge = pl.ds(ROOT, TILE)

    @pl.when(t == 0)
    def _():
        x_out[root, :] = x_ref[root, :]

    for at, ref in ((1, r1_ref), (2, r2_ref), (3, r3_ref)):
        @pl.when(t == at)
        def _():
            x_out[root, :] = ref[...]

    x_out[edge, :] = f1_ref[f1_ref.shape[0] - TILE:, :]

    a = normed(x_out[...].astype(F32), gain_ref[0:1, :])
    a_ref[...] = a
    k = dot(a, wk_ref[...])
    back = aligned(jnp.maximum(t * loc - TILE, 0), TILE)
    rotated(k[:ROOT], cos_ref[root, :], sin_ref[root, :], k_ref, root, None)
    rotated(k[ROOT:], cos_ref[back, :], sin_ref[back, :], k_ref, edge, None)
    v_ref[...] = dot(a, wv_ref[...]).astype(BF16)


def weight(d, j):
    return pl.BlockSpec((d, d), lambda i: (0, j), pipeline_mode=pl.Buffered(1))


def project_near(at, x, r1, r2, r3, f1, gains, w, tab):
    d = x.shape[1]
    n = ROOT + TILE
    return pl.pallas_call(
        near_rows_kernel,
        grid=(1,),
        in_specs=[SMEM] + [fixed(one.shape) for one in (x, r1, r2, r3, f1, gains)] + [weight(d, 1), weight(d, 2)]
        + [fixed(one.shape) for one in tab],
        out_specs=[fixed((n, d))] * 4,
        out_shape=[shape(n, d, BF16)] * 4,
        compiler_params=params(),
        cost_estimate=cost(5),
        name="project_near",
    )(at, x, r1, r2, r3, f1, gains, w, w, *tab)


def far_rows_kernel(meta_ref, slot_ref, x_ref, a1_ref, a2_ref, a3_ref, b1_ref, b2_ref, b3_ref, gain_ref, wk_ref, wv_ref, cos_ref, sin_ref,
                    x_out, a_ref, k_ref, v_ref):
    t = meta_ref[0, 5]
    for h in range(2 * BRANCHES):
        owner, at = slot_ref[h, 0], slot_ref[h, 1]
        rows = aligned(at * TILE, TILE)
        head = aligned(jnp.minimum(at * TILE, ROOT - TILE), TILE)
        back = aligned(jnp.maximum(at * TILE - ROOT, 0), TILE)
        to = pl.ds(h * TILE, TILE)

        @pl.when(owner > t)
        def _():
            x_out[to, :] = jnp.zeros((TILE, x_out.shape[1]), BF16)

        @pl.when(owner == t)
        def _():
            x_out[to, :] = x_ref[rows, :]

        for hop, a_from, b_from in ((1, a1_ref, b1_ref), (2, a2_ref, b2_ref), (3, a3_ref, b3_ref)):
            @pl.when((owner + hop == t) & (at < ROOT // TILE))
            def _():
                x_out[to, :] = a_from[head, :]

            @pl.when((owner + hop == t) & (at >= ROOT // TILE))
            def _():
                x_out[to, :] = b_from[back, :]

    a = normed(x_out[...].astype(F32), gain_ref[0:1, :])
    a_ref[...] = a
    k = dot(a, wk_ref[...])
    for h in range(2 * BRANCHES):
        back = aligned(slot_ref[h, 2] * TILE, TILE)
        rotated(k[h * TILE:(h + 1) * TILE], cos_ref[back, :], sin_ref[back, :], k_ref, pl.ds(h * TILE, TILE), None)
    v_ref[...] = dot(a, wv_ref[...]).astype(BF16)


def project_far(meta, slots, x, ups, gains, w, tab):
    d = x.shape[1]
    return pl.pallas_call(
        far_rows_kernel,
        grid=(1,),
        in_specs=[SMEM, SMEM] + [fixed(one.shape) for one in (x, *ups, gains)] + [weight(d, 1), weight(d, 2)]
        + [fixed(one.shape) for one in tab],
        out_specs=[fixed((SLOTS, d))] * 4,
        out_shape=[shape(SLOTS, d, BF16)] * 4,
        compiler_params=params(),
        cost_estimate=cost(7),
        name="project_far",
    )(meta, slots, x, *ups, gains, w, w, *tab)


def fill_bias(root_ref, own_ref, keys_axis):
    for ref in (root_ref, own_ref):
        if ref is None:
            continue
        key = lax.broadcasted_iota(jnp.int32, ref.shape[1:], keys_axis)
        row = lax.broadcasted_iota(jnp.int32, ref.shape[1:], 1 - keys_axis) % TILE
        for s in range(ref.shape[0]):
            ref[s] = jnp.where(key <= row + s * TILE, 0.0, MASKED).astype(F32)


def low_half():
    return lax.broadcasted_iota(jnp.int32, (TILE, 128), 1) < HEAD_DIM


def both(low, x):
    none = jnp.zeros_like(x)
    return jnp.concatenate([jnp.where(low, x, none), jnp.where(low, none, x)], axis=0)


def diagonal(x):
    return jnp.concatenate([x[:HEAD_DIM, :TILE], x[HEAD_DIM:, TILE:]], axis=0)


def per_half(row):
    upper = lax.broadcasted_iota(jnp.int32, (128, TILE), 0) < HEAD_DIM
    return jnp.where(upper, row[:, :TILE], row[:, TILE:])


def tile_of(meta_ref, i):
    return (meta_ref[i, 0], meta_ref[i, 1], aligned(meta_ref[i, 2], BLOCK), aligned(meta_ref[i, 3], BLOCK),
            aligned(i * TILE, TILE))


def line_up(to_ref, near_ref, own_ref):
    loc = own_ref.shape[0]
    to_ref[pl.ds(0, TILE), :] = near_ref[pl.ds(ROOT, TILE), :]
    to_ref[pl.ds(TILE, loc), :] = own_ref[...]
    to_ref[pl.ds(TILE + loc, TILE), :] = jnp.zeros((TILE, 128), to_ref.dtype)


def soften(q, spans):
    s = [dot(kk, q, COLS) if b is None else dot(kk, q, COLS) + b for kk, _, b in spans]
    top = functools.reduce(jnp.maximum, [jnp.max(part, axis=0, keepdims=True) for part in s])
    return s, top


def weigh(s, top, spans):
    e = [jnp.exp(part - top) for part in s]
    total = sum(jnp.sum(part, axis=0, keepdims=True) for part in e)
    return diagonal(sum(dot(vt, part.astype(BF16)) for part, (_, vt, _) in zip(e, spans))), total


def attend_near_kernel(meta_ref, q_ref, kn_ref, vn_ref, k_ref, v_ref, acc_ref, stat_ref, root_ref, own_ref, ko_ref, vo_ref, vr_ref):
    @pl.when(pl.program_id(0) == 0)
    def _():
        fill_bias(root_ref, own_ref, 0)

    loc = q_ref.shape[0]
    line_up(ko_ref, kn_ref, k_ref)
    root = pl.ds(0, ROOT)
    vr_ref[...] = vn_ref[root, :].T
    vo_ref[:, :TILE] = vn_ref[pl.ds(ROOT, TILE), :].T
    vo_ref[:, TILE:TILE + loc] = v_ref[...].T
    vo_ref[:, TILE + loc:] = jnp.zeros((128, TILE), BF16)
    low = low_half()
    stat_ref[...] = jnp.zeros_like(stat_ref)

    def one(i, rooted):
        sub, leaf, par, own, here = tile_of(meta_ref, i)
        q = both(low, q_ref[here, :])
        spans = [(kn_ref[root, :], vr_ref[...], root_ref[i] if rooted else None)]
        if not rooted:
            spans.append((ko_ref[own, :], vo_ref[:, own], own_ref[sub % 2]))
        s, top = soften(q, spans)
        acc, total = weigh(s, top, spans)
        acc_ref[:, here] = acc
        for h in range(2):
            stat_ref[0, h:h + 1, here] = top[:, h * TILE:(h + 1) * TILE]
            stat_ref[0, 2 + h:3 + h, here] = total[:, h * TILE:(h + 1) * TILE]

    tiles = loc // TILE

    @pl.when(meta_ref[0, 0] > 0)
    def _():
        for i in range(tiles):
            one(i, False)

    @pl.when(meta_ref[0, 0] == 0)
    def _():
        for i in range(tiles):
            one(i, i < ROOT // TILE)


def bias_scratch(keys_axis):
    def one(n):
        return pltpu.VMEM((n // TILE,) + ((n, 2 * TILE) if keys_axis == 0 else (2 * TILE, n)), F32)
    return one(ROOT), one(BLOCK)


def line_scratch(loc, kind):
    return pltpu.VMEM((loc + 2 * TILE, 128), kind)


def attend_near(meta, q, near, own):
    loc, d = q.shape
    n = ROOT + TILE
    return pl.pallas_call(
        attend_near_kernel,
        grid=(d // 128,),
        in_specs=[SMEM, pair(loc), pair(n), pair(n), pair(loc), pair(loc)],
        out_specs=[pl.BlockSpec((128, loc), lambda p: (p, 0)), log_spec(loc)],
        out_shape=[shape(d, loc, F32), jax.ShapeDtypeStruct((d // 128, 8, loc), F32)],
        scratch_shapes=[*bias_scratch(0), line_scratch(loc, BF16), pltpu.VMEM((128, loc + 2 * TILE), BF16), pltpu.VMEM((128, ROOT), BF16)],
        compiler_params=params(),
        cost_estimate=cost(20),
        name="attend_near",
    )(meta, q, *near, *own)


def attend_far_kernel(meta_ref, q_ref, ks_ref, vs_ref, acc_ref, stat_ref, o_ref, l_ref, vt_ref):
    low = low_half()
    vt_ref[...] = vs_ref[...].T
    l_ref[...] = jnp.zeros_like(l_ref)
    for i in range(o_ref.shape[0] // TILE):
        sub, leaf, par, own, here = tile_of(meta_ref, i)
        stat = stat_ref[0, :, here]
        old = jnp.concatenate([stat[0:1], stat[1:2]], axis=1)
        old_total = jnp.concatenate([stat[2:3], stat[3:4]], axis=1)
        spans = [(ks_ref[par, :], vt_ref[:, par], jnp.where(leaf > 0, 0.0, MASKED).astype(F32))]
        s, top = soften(both(low, q_ref[here, :]), spans)
        top = jnp.maximum(top, old)
        new, total = weigh(s, top, spans)
        fade = jnp.exp(old - top)
        total = old_total * fade + total
        out = (acc_ref[:, here] * per_half(fade) + new) / per_half(total)
        o_ref[here, :] = out.T.astype(BF16)
        log = top + jnp.log(total)
        for h in range(2):
            l_ref[0, h:h + 1, here] = log[:, h * TILE:(h + 1) * TILE]


def log_spec(loc):
    return pl.BlockSpec((1, 8, loc), lambda p: (p, 0, 0))


def attend_far(meta, q, far, acc, stat):
    loc, d = q.shape
    return pl.pallas_call(
        attend_far_kernel,
        grid=(d // 128,),
        in_specs=[SMEM, pair(loc), pair(SLOTS), pair(SLOTS), pl.BlockSpec((128, loc), lambda p: (p, 0)), log_spec(loc)],
        out_specs=[pair(loc), log_spec(loc)],
        out_shape=[shape(loc, d, BF16), jax.ShapeDtypeStruct((d // 128, 8, loc), F32)],
        scratch_shapes=[pltpu.VMEM((128, SLOTS), BF16)],
        compiler_params=params(),
        cost_estimate=cost(9),
        name="attend_far",
    )(meta, q, *far, acc, stat)


def split_cores(core, got, kept_ref, away_ref, where):
    @pl.when(core == 0)
    def _():
        kept_ref[where] = got[:, 0]
        away_ref[where] = got[:, 1]

    @pl.when(core == 1)
    def _():
        kept_ref[where] = got[:, 1]
        away_ref[where] = got[:, 0]


def ffn_kernel(at_ref, x_ref, o_ref, ct_ref, gain_ref, wo_ref, w_ref,
               mixed_ref, do_ref, dhb_ref, dh_ref, sum_ref, kept_ref, away_ref, c_s, m_s, dg_s, du_s, ct_t, c_t):
    step = pl.program_id(0)
    loc, d = ct_ref.shape
    n = x_ref.shape[0]
    parts, hid = m_s.shape[0], m_s.shape[2]

    def slab(t, j):
        return w_ref[:, t, :, j * hid:(j + 1) * hid].reshape(d, hid)

    @pl.when(step < loc // n)
    def _():
        here = aligned(step * n, n, 16)
        ct = ct_ref[here, :]
        h = x_ref[...].astype(F32) + dot(o_ref[...], wo_ref[...], COLS)
        scale = inv_rms(h)
        c_hat = h * scale
        gain = gain_ref[1:2, :]
        c = (c_hat * gain).astype(BF16)
        c_s[here, :] = c
        y = h
        dc = jnp.zeros_like(h)
        for t in range(parts):
            g = dot(c, slab(t, 0))
            u = dot(c, slab(t, 1))
            dm = dot(ct, slab(t, 2))
            sig = jax.nn.sigmoid(g)
            silu = g * sig
            m = (silu * u).astype(BF16)
            dg = (dm * u * (sig * (1.0 + g * (1.0 - sig)))).astype(BF16)
            du = (dm * silu).astype(BF16)
            y = y + dot(m, slab(t, 2), COLS)
            dc = dc + dot(dg, slab(t, 0), COLS) + dot(du, slab(t, 1), COLS)
            m_s[t, here, :] = m
            dg_s[t, here, :] = dg
            du_s[t, here, :] = du
        mixed_ref[...] = y.astype(BF16)
        part = jnp.sum(dc * c_hat, axis=0, keepdims=True)

        @pl.when(step == 0)
        def _():
            sum_ref[...] = jnp.zeros_like(sum_ref)

        sum_ref[0:1, :] += part
        scaled = dc * gain
        dh = ct.astype(F32) + scale * (scaled - c_hat * jnp.mean(scaled * c_hat, axis=-1, keepdims=True))
        dh_ref[...] = dh
        dhb = dh.astype(BF16)
        dhb_ref[...] = dhb
        do_ref[...] = dot(dhb, wo_ref[...]).astype(BF16)

    @pl.when(step == loc // n)
    def _():
        ct_t[...] = ct_ref[...].T
        c_t[...] = c_s[...].T

    @pl.when(step >= loc // n)
    def _():
        t = step - loc // n
        for j, (left, right) in enumerate(((c_t, dg_s), (c_t, du_s), (ct_t, m_s))):
            got = dot(left[...], right[t]).astype(BF16)
            chips, _, rows, _ = kept_ref.shape
            split_cores(at_ref[1] % 2, got.reshape(chips, 2, rows, hid), kept_ref, away_ref,
                        (slice(None), 0, slice(None), slice(j * hid, (j + 1) * hid)))


def feed_forward(at_core, x, o, ct, gains, w, rest):
    loc, d = x.shape
    dp, parts, rows, wide = rest.shape
    hid = wide // 3
    steps = 2
    n = loc // steps
    at = lambda i: (jnp.minimum(i, steps - 1), 0)
    tile = pl.BlockSpec((n, d), at)
    grads = pl.BlockSpec((dp // 2, 1, rows, wide), lambda i: (0, jnp.maximum(i - steps, 0), 0, 0))
    return pl.pallas_call(
        ffn_kernel,
        grid=(steps + parts,),
        in_specs=[SMEM, tile, tile, fixed((loc, d)), fixed((8, d)), weight(d, 3), fixed(rest.shape)],
        out_specs=[tile, tile, tile, tile, pl.BlockSpec((8, d), lambda i: (0, 0)), grads, grads],
        out_shape=[shape(loc, d, BF16), shape(loc, d, BF16), shape(loc, d, BF16), shape(loc, d, F32), shape(8, d, F32)]
        + [jax.ShapeDtypeStruct((dp // 2, parts, rows, wide), BF16)] * 2,
        scratch_shapes=[pltpu.VMEM((loc, d), BF16)] + [pltpu.VMEM((parts, loc, hid), BF16)] * 3 + [pltpu.VMEM((d, loc), BF16)] * 2,
        compiler_params=params(),
        cost_estimate=cost(40),
        name="feed_forward",
    )(at_core, x, o, ct, gains, w, rest)


def unrotate(w, cos, sin):
    return w * cos - half_turn(w) * sin


def back_setup(low, q_ref, do_ref, o_ref, l_ref, here):
    do = do_ref[here, :]
    dots = (do.astype(F32) * o_ref[here, :].astype(F32)).T
    row_dot = [jnp.sum(dots[h * HEAD_DIM:(h + 1) * HEAD_DIM, :], axis=0, keepdims=True) for h in range(2)]
    log = [l_ref[0, h:h + 1, here] for h in range(2)]
    return both(low, q_ref[here, :]), both(low, do), jnp.concatenate(log, axis=1), jnp.concatenate(row_dot, axis=1)


def back_span(setup, kk, vv, kt, bias, acc, dk_acc, dv_acc):
    q, do, log, row_dot = setup
    s = dot(kk, q, COLS)
    if bias is not None:
        s = s + bias
    p = jnp.exp(s - log)
    ds = (p * (dot(vv, do, COLS) - row_dot)).astype(BF16)
    dv_acc[acc, :] += dot(p.astype(BF16), do)
    dk_acc[acc, :] += dot(ds, q)
    return diagonal(dot(kt, ds))


def back_far_kernel(meta_ref, slot_ref, q_ref, do_ref, o_ref, l_ref, kn_ref, vn_ref, ks_ref, vs_ref, cos_ref, sin_ref,
                    dq_ref, dk_ref, dv_ref, root_ref, krt_ref, kst_ref, dk_acc, dv_acc):
    @pl.when(pl.program_id(0) == 0)
    def _():
        fill_bias(root_ref, None, 0)

    low = low_half()
    root = pl.ds(0, ROOT)
    for ref in (dk_acc, dv_acc):
        ref[...] = jnp.zeros_like(ref)
    krt_ref[...] = kn_ref[root, :].T
    kst_ref[...] = ks_ref[...].T
    tiles = do_ref.shape[0] // TILE

    def one(i, rooted):
        sub, leaf, par, own, here = tile_of(meta_ref, i)
        setup = back_setup(low, q_ref, do_ref, o_ref, l_ref, here)
        dq = back_span(setup, kn_ref[root, :], vn_ref[root, :], krt_ref[...], root_ref[i] if rooted else None, root, dk_acc, dv_acc)
        if not rooted:
            acc = aligned(meta_ref[i, 2] + ROOT, BLOCK, BLOCK)
            hide = jnp.where(leaf > 0, 0.0, MASKED).astype(F32)
            dq = dq + back_span(setup, ks_ref[par, :], vs_ref[par, :], kst_ref[:, par], hide, acc, dk_acc, dv_acc)
        dq_ref[:, here] = dq

    @pl.when(meta_ref[0, 0] > 0)
    def _():
        for i in range(tiles):
            one(i, False)

    @pl.when(meta_ref[0, 0] == 0)
    def _():
        for i in range(tiles):
            one(i, i < ROOT // TILE)

    dk_ref[root, :] = unrotate(dk_acc[root, :], cos_ref[root, :], sin_ref[root, :]).astype(BF16)
    for h in range(2 * BRANCHES):
        at, back = pl.ds(ROOT + h * TILE, TILE), aligned(slot_ref[h, 2] * TILE, TILE)
        dk_ref[at, :] = unrotate(dk_acc[at, :], cos_ref[back, :], sin_ref[back, :]).astype(BF16)
    dv_ref[...] = dv_acc[...].astype(BF16)


def turned(loc):
    return pl.BlockSpec((128, loc), lambda p: (p, 0))


def back_far(meta, slots, q, do, o, logs, near, far, tab):
    loc, d = do.shape
    n = ROOT + TILE
    return pl.pallas_call(
        back_far_kernel,
        grid=(d // 128,),
        in_specs=[SMEM, SMEM, pair(loc), pair(loc), pair(loc), log_spec(loc), pair(n), pair(n), pair(SLOTS), pair(SLOTS)]
        + [fixed(one.shape) for one in tab],
        out_specs=[turned(loc), pair(FAR), pair(FAR)],
        out_shape=[shape(d, loc, F32), shape(FAR, d, BF16), shape(FAR, d, BF16)],
        scratch_shapes=[bias_scratch(0)[0], pltpu.VMEM((128, ROOT), BF16), pltpu.VMEM((128, SLOTS), BF16),
                        pltpu.VMEM((FAR, 128), F32), pltpu.VMEM((FAR, 128), F32)],
        compiler_params=params(),
        cost_estimate=cost(50),
        name="back_far",
    )(meta, slots, q, do, o, logs, *near, *far, *tab)


def back_near_kernel(meta_ref, q_ref, do_ref, o_ref, l_ref, kn_ref, vn_ref, k_ref, v_ref, cos_ref, sin_ref, part_ref, late_ref,
                     dq_ref, dk_ref, dv_ref, dke_ref, dve_ref, copy_ref, own_ref, ko_ref, vo_ref, kt_ref, dk_acc, dv_acc):
    @pl.when(pl.program_id(0) == 0)
    def _():
        fill_bias(None, own_ref, 0)

    copy_ref[...] = late_ref[...]
    line_up(ko_ref, kn_ref, k_ref)
    line_up(vo_ref, vn_ref, v_ref)
    kt_ref[...] = ko_ref[...].T
    low = low_half()
    loc = do_ref.shape[0]
    t = meta_ref[0, 5]
    for ref in (dk_acc, dv_acc):
        ref[...] = jnp.zeros_like(ref)

    def one(i, rooted):
        sub, leaf, par, own, here = tile_of(meta_ref, i)
        dq = part_ref[:, here]
        if not rooted:
            setup = back_setup(low, q_ref, do_ref, o_ref, l_ref, here)
            dq = dq + back_span(setup, ko_ref[own, :], vo_ref[own, :], kt_ref[:, own], own_ref[sub % 2], own, dk_acc, dv_acc)
        back = aligned(sub * TILE, TILE)
        dq_ref[here, :] = unrotate(dq.T * HEAD_DIM ** -0.5, cos_ref[back, :], sin_ref[back, :]).astype(BF16)

    @pl.when(t > 0)
    def _():
        for i in range(loc // TILE):
            one(i, False)

    @pl.when(t == 0)
    def _():
        for i in range(loc // TILE):
            one(i, i < ROOT // TILE)

    edge, mine = pl.ds(0, TILE), pl.ds(TILE, loc)
    before = aligned(jnp.maximum(t * loc - TILE, 0), TILE)
    here = aligned(t * loc, loc)
    dke_ref[...] = unrotate(dk_acc[edge, :], cos_ref[before, :], sin_ref[before, :]).astype(BF16)
    dve_ref[...] = dv_acc[edge, :].astype(BF16)
    dk_ref[...] = unrotate(dk_acc[mine, :], cos_ref[here, :], sin_ref[here, :]).astype(BF16)
    dv_ref[...] = dv_acc[mine, :].astype(BF16)


def back_near(deps, meta, q, do, o, logs, near, own, tab, dq_part, late):
    loc, d = do.shape
    n = ROOT + TILE
    return pl.pallas_call(
        after(len(deps), back_near_kernel),
        grid=(d // 128,),
        in_specs=[ANY] * len(deps) + [SMEM, pair(loc), pair(loc), pair(loc), log_spec(loc), pair(n), pair(n), pair(loc), pair(loc)]
        + [fixed(one.shape) for one in tab] + [turned(loc), pair(late.shape[0])],
        out_specs=[pair(loc)] * 3 + [pair(TILE)] * 2 + [pair(late.shape[0])],
        out_shape=[shape(loc, d, BF16)] * 3 + [shape(TILE, d, BF16)] * 2 + [shape(late.shape[0], d, BF16)],
        scratch_shapes=[bias_scratch(0)[1], line_scratch(loc, BF16), line_scratch(loc, BF16),
                        pltpu.VMEM((128, loc + 2 * TILE), BF16), line_scratch(loc, F32), line_scratch(loc, F32)],
        compiler_params=params(),
        cost_estimate=cost(25),
        name="back_near",
    )(*deps, meta, q, do, o, logs, *near, *own, *tab, dq_part, late)


def spread_kernel(at_ref, kept_ref, away_ref, dk_ref, dv_ref, xn_ref, xs_ref, wk_ref, wv_ref, early_ref, late_ref, sum_ref, *outs):
    step = pl.program_id(0)
    chip = at_ref[1] // 2
    for m, out_ref in enumerate(outs):
        out_ref[0] = (kept_ref[chip ^ m, 0].astype(F32) + away_ref[chip ^ m, 0].astype(F32)).astype(BF16)
    da = dot(dk_ref[...], wk_ref[...], COLS) + dot(dv_ref[...], wv_ref[...], COLS)
    n = da.shape[0]

    def gain_part(part, x):
        x = x.astype(F32)
        return jnp.sum(part * (x * inv_rms(x)), axis=0, keepdims=True)

    @pl.when(step == 0)
    def _():
        sum_ref[...] = jnp.zeros_like(sum_ref)

    for i in range(FAR // n):
        @pl.when(step == i)
        def _():
            near = max(min(ROOT - i * n, n), 0)
            got = jnp.zeros((1, da.shape[1]), F32)
            if near:
                got = got + gain_part(da[:near], xn_ref[pl.ds(i * n, near), :])
            if near < n:
                got = got + gain_part(da[near:], xs_ref[pl.ds(i * n + near - ROOT, n - near), :])
            sum_ref[0:1, :] += got
            if i * n < EARLY:
                early_ref[...] = da.astype(BF16)
            else:
                late_ref[...] = da.astype(BF16)


def spread(at, kept, away, dk, dv, x_near, x_slot, w):
    d = w.shape[0]
    chips, parts, rows, wide = kept.shape
    n = FAR // parts
    half = EARLY // n
    block = pl.BlockSpec((chips, 1, rows, wide), lambda i: (0, i, 0, 0))
    out = pl.BlockSpec((1, rows, wide), lambda i: (i, 0, 0))
    got = pl.pallas_call(
        spread_kernel,
        grid=(parts,),
        in_specs=[SMEM, block, block, tiled(n, d), tiled(n, d), fixed(x_near.shape), fixed(x_slot.shape), weight(d, 1), weight(d, 2)],
        out_specs=[pl.BlockSpec((n, d), lambda i: (jnp.minimum(i, half - 1), 0)), pl.BlockSpec((n, d), lambda i: (jnp.maximum(i - half, 0), 0)),
                   pl.BlockSpec((8, d), lambda i: (0, 0))] + [out] * chips,
        out_shape=[shape(EARLY, d, BF16), shape(FAR - EARLY, d, BF16), shape(8, d, F32)]
        + [jax.ShapeDtypeStruct((parts, rows, wide), BF16)] * chips,
        compiler_params=params(),
        cost_estimate=cost(9),
        name="spread",
    )(at, kept, away, dk, dv, x_near, x_slot, w, w)
    return got[0], got[1], got[2], got[3:]


def own_back_kernel(x_ref, xe_ref, dq_ref, dk_ref, dv_ref, dke_ref, dve_ref, wq_ref, wk_ref, wv_ref, da_ref, edge_ref, sum_ref):
    step = pl.program_id(0)
    wk, wv = wk_ref[...], wv_ref[...]

    def gain_part(da, x):
        x = x.astype(F32)
        return jnp.sum(da * (x * inv_rms(x)), axis=0, keepdims=True)

    @pl.when(step == 0)
    def _():
        edge = dot(dke_ref[...], wk, COLS) + dot(dve_ref[...], wv, COLS)
        edge_ref[...] = edge.astype(BF16)
        sum_ref[...] = jnp.zeros_like(sum_ref)
        sum_ref[0:1, :] = gain_part(edge, xe_ref[pl.ds(ROOT, TILE), :])

    da = dot(dq_ref[...], wq_ref[...], COLS) + dot(dk_ref[...], wk, COLS) + dot(dv_ref[...], wv, COLS)
    da_ref[...] = da
    sum_ref[0:1, :] += gain_part(da, x_ref[...])


def own_back(deps, x, x_near, dq, dk, dv, dke, dve, w):
    loc, d = x.shape
    n = loc // 2
    return pl.pallas_call(
        after(len(deps), own_back_kernel),
        grid=(2,),
        in_specs=[ANY] * len(deps) + [tiled(n, d), fixed(x_near.shape), tiled(n, d), tiled(n, d), tiled(n, d), fixed((TILE, d)), fixed((TILE, d)),
                  weight(d, 0), weight(d, 1), weight(d, 2)],
        out_specs=[tiled(n, d), pl.BlockSpec((TILE, d), lambda i: (0, 0)), pl.BlockSpec((8, d), lambda i: (0, 0))],
        out_shape=[shape(loc, d, F32), shape(TILE, d, BF16), shape(8, d, F32)],
        compiler_params=params(),
        cost_estimate=cost(6),
        name="own_back",
    )(*deps, x, x_near, dq, dk, dv, dke, dve, w, w, w)


def spill(core, got, kept_ref, away_ref, at=0):
    chips, rows, _ = kept_ref.shape
    split_cores(core, got.astype(BF16).reshape(chips, 2, rows, got.shape[1]), kept_ref, away_ref,
                (slice(None), slice(None), slice(at, at + got.shape[1])))


def keyed(a_ref, an_ref, as_ref, own, far, edge):
    root, tail = pl.ds(0, ROOT), pl.ds(ROOT, TILE)
    return (dot(a_ref[...], own[...], ROWS) + dot(an_ref[root, :], far[root, :], ROWS)
            + dot(as_ref[...], far[pl.ds(ROOT, SLOTS), :], ROWS) + dot(an_ref[tail, :], edge[...], ROWS))


def first_kernel(at_ref, s1_ref, s2_ref, s3_ref, a_ref, dq_ref, dhb_ref, o_ref, kept_ref, away_ref):
    core, d = at_ref[1] % 2, a_ref.shape[1]
    line = lax.broadcasted_iota(jnp.int32, (GAIN_LANES, d), 0)
    table = jnp.where(line == 0, s1_ref[0:1, :] + s2_ref[0:1, :], jnp.where(line == 1, s3_ref[0:1, :], 0.0))
    spill(core, dot(a_ref[...], dq_ref[...], ROWS), kept_ref, away_ref)
    spill(core, dot(dhb_ref[...], o_ref[...], ROWS), kept_ref, away_ref, d)
    spill(core, table.T, kept_ref, away_ref, 2 * d)


def second_kernel(at_ref, a_ref, an_ref, as_ref, dk_ref, dv_ref, dkf_ref, dvf_ref, dke_ref, dve_ref, kept_ref, away_ref):
    step, core = pl.program_id(0), at_ref[1] % 2

    @pl.when(step == 0)
    def _():
        spill(core, keyed(a_ref, an_ref, as_ref, dk_ref, dkf_ref, dke_ref), kept_ref, away_ref)

    @pl.when(step == 1)
    def _():
        spill(core, keyed(a_ref, an_ref, as_ref, dv_ref, dvf_ref, dve_ref), kept_ref, away_ref)


def weight_sums(kernel, deps, at, arrays, dp, extra):
    d = arrays[-1].shape[1]
    chips, rows, wide = dp // 2, d // dp, 2 * d + extra
    steps = 1 if extra else 2
    spec = pl.BlockSpec((chips, rows, wide // steps), lambda i: (0, 0, i))
    return pl.pallas_call(
        after(len(deps), kernel),
        grid=(steps,),
        in_specs=[ANY] * len(deps) + [SMEM] + [fixed(one.shape) for one in arrays],
        out_specs=[spec, spec],
        out_shape=[jax.ShapeDtypeStruct((chips, rows, wide), BF16)] * 2,
        compiler_params=params(),
        cost_estimate=cost(8),
        name="weight_sums",
    )(*deps, at, *arrays)


def finish_kernel(meta_ref, da_ref, dh_ref, x_ref, gain_ref, early2_ref, late2_ref, early_ref, late_ref, edge_ref, out_ref):
    t = meta_ref[0, 5]
    tiles = x_ref.shape[0] // TILE

    def one(i, carry):
        here = aligned(i * TILE, TILE)
        given = meta_ref[i, 4]
        x = x_ref[here, :].astype(F32)
        scale = inv_rms(x)
        x_hat = x * scale
        gain = gain_ref[0:1, :]
        da = da_ref[here, :]
        none = jnp.zeros((TILE, x.shape[1]), F32)
        slot = jnp.maximum(given, 0)
        late = late_ref[aligned(slot, TILE), :].astype(F32) + late2_ref[aligned(slot, TILE), :].astype(F32)
        front = aligned(jnp.minimum(i * TILE, EARLY - TILE), TILE)
        early = early_ref[front, :].astype(F32) + early2_ref[front, :].astype(F32)
        da = da + jnp.where(given >= 0, late, none)
        da = da + jnp.where((t == 0) & (i < EARLY // TILE), early, none)
        da = da + jnp.where((i == tiles - 1) & (t % 2 == 0), edge_ref[...].astype(F32), none)
        scaled = da * gain
        out_ref[here, :] = dh_ref[here, :] + scale * (scaled - x_hat * jnp.mean(scaled * x_hat, axis=-1, keepdims=True))
        return carry

    lax.fori_loop(0, tiles, one, 0)


def finish(deps, meta, da, dh, x, gains, early2, late2, early, late, edge):
    loc, d = x.shape
    arrays = (da, dh, x, gains, early2, late2, early, late, edge)
    return pl.pallas_call(
        after(len(deps), finish_kernel),
        grid=(1,),
        in_specs=[ANY] * len(deps) + [SMEM] + [fixed(one.shape) for one in arrays],
        out_specs=fixed((loc, d)),
        out_shape=shape(loc, d, F32),
        compiler_params=params(),
        cost_estimate=cost(6),
        name="finish",
    )(*deps, meta, *arrays)


def tables(pos):
    half = HEAD_DIM // 2
    freq = jnp.exp(-jnp.log(10000.0) * (2.0 * jnp.arange(half, dtype=F32) / HEAD_DIM))
    angle = pos.astype(F32)[:, None] * jnp.concatenate([freq, freq, freq, freq])[None, :]
    sign = jnp.where(jnp.arange(2 * HEAD_DIM) % HEAD_DIM < half, -1.0, 1.0).astype(F32)
    return jnp.cos(angle), jnp.sin(angle) * sign[None, :]


def swap(x, axis, mask):
    return lax.ppermute(x, axis, [(i, i ^ mask) for i in range(lax.axis_size(axis))])


def send(x, *pairs):
    return lax.ppermute(x, "tensor", list(pairs))


def three(g):
    high = lax.reduce_precision(g, 8, 7)
    mid = lax.reduce_precision(g - high, 8, 7)
    return [high.astype(BF16), mid.astype(BF16), (g - high - mid).astype(BF16)]


def total_kernel(own_ref, *refs):
    ins, out_ref = refs[:-1], refs[-1]
    out_ref[...] = sum((one[...].astype(F32) for one in ins), own_ref[...].astype(F32)).astype(BF16)


def total(deps, *parts):
    one = fixed(parts[0].shape)
    return pl.pallas_call(
        after(len(deps), total_kernel),
        grid=(1,),
        in_specs=[ANY] * len(deps) + [one] * len(parts),
        out_specs=one,
        out_shape=jax.ShapeDtypeStruct(parts[0].shape, BF16),
        compiler_params=params(),
        cost_estimate=cost(3),
        name="total",
    )(*deps, *parts)


def meet_chips(deps, blocks):
    return total(deps, blocks[0], *(swap(block, "dp", 2 * m) for m, block in enumerate(blocks) if m))


def per_device(tokens, gain_attn, w_query, w_key, w_value, w_out, gain_ffn, w_gate, w_up, w_down,
               segment_ids, parent_ids, positions, cotangent):
    loc, d = tokens.shape
    t_size, t_at = lax.axis_size("tensor"), lax.axis_index("tensor")
    d_size, d_at = lax.axis_size("dp"), lax.axis_index("dp")
    tiles = loc // TILE
    own_gain = gain_attn.shape[0]
    rows, hid = w_gate.shape
    n = w_query.shape[1]
    at = jnp.stack([t_at, d_at]).astype(jnp.int32)

    up = [(i, i + 1) for i in range(t_size - 1)]
    a1 = send(tokens[:ROOT], *up)
    gain_cols = jnp.stack(three(gain_attn) + three(gain_ffn), axis=1)
    gain_cols = lax.dynamic_update_slice(jnp.zeros((rows, GAIN_LANES), BF16), gain_cols, (t_at * own_gain, 0))
    pack = jnp.concatenate([w_query, w_key, w_value, w_out.T, gain_cols], axis=1)
    others = [pack] + [swap(pack, "tensor", m) for m in range(1, t_size)]
    meta, slots = plan(at[:1], segment_ids, parent_ids, tiles)
    tab = tables(positions)
    lined = line((a1, *tab), others)
    a2 = send(a1, *up[1:])
    pieces = [None] * d_size
    for m in range(0, d_size, 2):
        pieces[m] = swap(lined, "dp", m) if m else lined
    b1 = send(join((lined,), tokens[ROOT:]), *up)
    rest = join((a2, b1, *(pieces[m] for m in range(2, d_size, 2))), w_gate, w_up, w_down.T)
    a3 = send(a2, *up[2:])
    for m in range(0, d_size, 2):
        pieces[m + 1] = swap(pieces[m], "dp", 1)
    if rows % 16:
        whole = jnp.zeros((d_size * rows, lined.shape[1]), BF16)
        for m in range(d_size):
            whole = lax.dynamic_update_slice_in_dim(whole, pieces[m], (d_at ^ m) * rows, 0)
        pieces = [whole]
    rest = lax.all_gather(rest, ("dp", "tensor"), axis=0, tiled=False).reshape(d_size, t_size, rows, 3 * hid)
    w, gains, a_own, q, k_own, v_own = project_own((), at, tokens, tab, pieces)
    again, front = begin((a3, k_own), tokens, b1)
    b2 = send(again, *up[1:])
    b3 = send(front, (0, 3))
    x_near, a_near, k_near, v_near = project_near(at, tokens, a1, a2, a3, b1, gains, w, tab)
    near, own = (k_near, v_near), (k_own, v_own)
    acc, stat = attend_near(meta, q, near, own)
    x_slot, a_slot, k_slot, v_slot = project_far(meta, slots, tokens, (a1, a2, a3, b1, b2, b3), gains, w, tab)
    far = (k_slot, v_slot)
    o, logs = attend_far(meta, q, far, acc, stat)

    mixed, do, dhb, dh, ffn_sum, kept, away = feed_forward(at, tokens, o, cotangent, gains, w, rest)
    away = swap(away, "dp", 1)
    dq_part, dk_far, dv_far = back_far(meta, slots, q, do, o, logs, near, far, tab)
    early, late, far_sum, rest_blocks = spread(at, kept, away, dk_far, dv_far, x_near, x_slot, w)
    moved = [swap(block, "dp", 2 * m) for m, block in enumerate(rest_blocks) if m]
    early_in = send(early, (3, 2), (1, 0))
    dq, dk, dv, dke, dve, late = back_near((early,), meta, q, do, o, logs, near, own, tab, dq_part, late)
    late_in = send(late, (3, 2))
    early = total((dq,), early, early_in)
    early_in = send(early, (2, 0))
    da, edge, own_sum = own_back((early, moved[-1]), tokens, x_near, dq, dk, dv, dke, dve, w)
    kept_b, away_b = weight_sums(
        second_kernel, (da,), at, (a_own, a_near, a_slot, dk, dv, dk_far, dv_far, dke, dve), d_size, 0)
    away_b = swap(away_b, "dp", 1)
    keep, away, late = fold((kept_b,), at, late, late_in, rest_blocks[0], *moved)
    away = swap(away, "tensor", 2)
    late_in = send(late, (2, 1))
    kept_a, away_a = weight_sums(
        first_kernel, (keep, late, early_in), at, (far_sum, own_sum, ffn_sum, a_own, dq, dhb, o), d_size, GAIN_LANES)
    away_a = swap(away_a, "dp", 1)
    blocks = meet((), at, (kept_a, kept_b), (away_a, away_b))
    summed = meet_chips((late_in,), blocks)
    mine, away = middle((summed,), keep, away)
    rest_owned = mine.astype(F32) + swap(away, "tensor", 1).astype(F32)
    crossing = (slots[2, 0] == 0) & (t_at == 1)
    edge = send(edge + jnp.where(crossing, late[:TILE] + late_in[:TILE], jnp.zeros_like(edge)), (1, 0), (3, 2))
    grad_tokens = finish((summed,), meta, da, dh, tokens, gains, early, late, early_in, late_in, edge)
    starts = (0, d, 2 * d + GAIN_LANES, 3 * d + GAIN_LANES)

    def share(m):
        return jnp.concatenate([summed[:, at + m * n:at + (m + 1) * n] for at in starts] + [summed[:, 2 * d:2 * d + GAIN_LANES]], axis=1)

    owned = share(0).astype(F32)
    for m in range(1, t_size):
        owned = owned + swap(share(m), "tensor", m).astype(F32)
    gain_sums = lax.dynamic_slice(owned, (t_at * own_gain, 4 * n), (own_gain, GAIN_LANES))
    return (mixed, grad_tokens, gain_sums[:, 0], owned[:, :n], owned[:, 2 * n:3 * n], owned[:, 3 * n:4 * n], owned[:, n:2 * n].T,
            gain_sums[:, 1], rest_owned[:, :hid], rest_owned[:, hid:2 * hid], rest_owned[:, 2 * hid:].T)


def solution(mesh):
    rows = P(("dp", "tensor"), None)
    gain = P(("dp", "tensor"))
    wide = P("dp", "tensor")
    tall = P("tensor", "dp")
    return jax.shard_map(
        per_device,
        mesh=mesh,
        in_specs=(rows, gain, wide, wide, wide, tall, gain, wide, wide, tall, P("dp"), P("dp"), P("dp"), rows),
        out_specs=(rows, rows, gain, wide, wide, wide, tall, gain, wide, wide, tall),
        check_vma=False,
    )
```

```python
import functools

import jax
import jax.numpy as jnp
from jax import lax
from jax.experimental import pallas as pl
from jax.experimental.pallas import tpu as pltpu
from jax.sharding import PartitionSpec as P

HEAD_DIM = 64
BLOCK = 256
TILE = 128
ROOT = 512
BRANCHES = 4
SLOTS = BRANCHES * BLOCK
FAR = ROOT + SLOTS
EARLY = ROOT + BLOCK
GAIN_LANES = 128
EPSILON = 1e-05
MASKED = -1e30
VMEM = 60 * 1024 * 1024
F32 = jnp.float32
BF16 = jnp.bfloat16
PLAIN = (((1,), (0,)), ((), ()))
ROWS = (((0,), (0,)), ((), ()))
COLS = (((1,), (1,)), ((), ()))


def dot(a, b, dims=PLAIN):
    return lax.dot_general(a, b, dims, preferred_element_type=F32)


def cost(us):
    return pl.CostEstimate(flops=int(us * 3e7), bytes_accessed=0, transcendentals=0)


def params():
    return pltpu.CompilerParams(vmem_limit_bytes=VMEM)


def half_turn(u):
    lane = lax.broadcasted_iota(jnp.int32, u.shape, 1)
    return jnp.where(lane % HEAD_DIM < HEAD_DIM // 2, pltpu.roll(u, 96, 1), pltpu.roll(u, 32, 1))


SMEM = pl.BlockSpec(memory_space=pltpu.SMEM)
ANY = pl.BlockSpec(memory_space=pl.ANY)


def after(count, kernel):
    return lambda *refs: kernel(*refs[count:])


def fixed(shape):
    return pl.BlockSpec(shape, lambda i: (0,) * len(shape), pipeline_mode=pl.Buffered(1))


def tiled(n, w):
    return pl.BlockSpec((n, w), lambda i: (i, 0))


def pair(n):
    return pl.BlockSpec((n, 128), lambda p: (0, p))


def aligned(row, n, unit=TILE):
    return pl.ds(pl.multiple_of(row, unit), n)


def shape(n, w, kind):
    return jax.ShapeDtypeStruct((n, w), kind)


def inv_rms(x):
    return lax.rsqrt(jnp.mean(x * x, axis=-1, keepdims=True) + EPSILON)


def plan_kernel(tiles, blocks, at_ref, seg_ref, par_ref, meta_ref, slot_ref):
    t = at_ref[0]
    first = ROOT // BLOCK
    root = seg_ref[0]
    seg = [seg_ref[b * BLOCK] for b in range(blocks)]
    par = [par_ref[b * BLOCK] for b in range(blocks)]
    rank = []
    count = jnp.int32(0)
    for b in range(blocks):
        rank.append(count)
        if b >= first:
            count = count + (par[b] == root).astype(jnp.int32)
    for beta in range(BRANCHES):
        at = jnp.int32(0)
        for b in range(first, blocks):
            at = jnp.where((par[b] == root) & (rank[b] == beta), b, at)
        for half in range(2):
            sub = 2 * at + half
            h = 2 * beta + half
            slot_ref[h, 0] = sub // tiles
            slot_ref[h, 1] = sub % tiles
            slot_ref[h, 2] = sub
            for j in range(3, 8):
                slot_ref[h, j] = 0
    for i in range(8):
        sub = t * tiles + min(i, tiles - 1)
        block = sub // 2
        mine = par_ref[block * BLOCK]
        leaf = ((mine != root) & (block >= first)).astype(jnp.int32)
        slot = jnp.int32(0)
        for b in range(first, blocks):
            slot = jnp.where((seg[b] == mine) & (par[b] == root), rank[b], slot)
        given = jnp.int32(-1)
        for h in range(2, 2 * BRANCHES):
            given = jnp.where((slot_ref[h, 2] == sub) & (t > 0), (h - 2) * TILE, given)
        meta_ref[i, 0] = sub
        meta_ref[i, 1] = leaf
        meta_ref[i, 2] = slot * leaf * BLOCK
        meta_ref[i, 3] = block * BLOCK - t * tiles * TILE + TILE
        meta_ref[i, 4] = given
        meta_ref[i, 5] = t
        meta_ref[i, 6] = jnp.where(t == 0, (slot_ref[2, 0] == 0).astype(jnp.int32), 0)
        meta_ref[i, 7] = 0


def plan(t_at, seg, par, tiles):
    out = jax.ShapeDtypeStruct((8, 8), jnp.int32)
    return pl.pallas_call(
        functools.partial(plan_kernel, tiles, seg.shape[0] // BLOCK),
        in_specs=[SMEM] * 3,
        out_specs=[SMEM] * 2,
        out_shape=[out, out],
        name="plan",
    )(t_at.reshape(1), seg, par)


def normed(x, gain):
    return (x * inv_rms(x) * gain).astype(BF16)


def rotated(u, cos, sin, out_ref, rows, factor):
    for c in range(u.shape[1] // 128):
        part = u[:, c * 128:(c + 1) * 128]
        r = (part * cos + half_turn(part) * sin).astype(BF16)
        out_ref[rows, c * 128:(c + 1) * 128] = r * factor if factor is not None else r


def line_kernel(out_ref, parts):
    n = (parts[0].shape[1] - GAIN_LANES) // 4
    for j in range(4):
        for r, part in enumerate(parts):
            out_ref[:, (j * len(parts) + r) * n:(j * len(parts) + r + 1) * n] = part[:, j * n:(j + 1) * n]
    out_ref[:, 4 * n * len(parts):] = sum(part[:, 4 * n:] for part in parts)


def line(deps, parts):
    rows, wide = parts[0].shape
    out = (rows, (wide - GAIN_LANES) * len(parts) + GAIN_LANES)
    return pl.pallas_call(
        after(len(deps), lambda *refs: line_kernel(refs[-1], refs[:-1])),
        grid=(1,),
        in_specs=[ANY] * len(deps) + [fixed(one.shape) for one in parts],
        out_specs=fixed(out),
        out_shape=shape(*out, BF16),
        compiler_params=params(),
        cost_estimate=cost(2),
        name="line",
    )(*deps, *parts)


def join_kernel(ins, out_ref):
    at = 0
    for part in ins:
        out_ref[:, at:at + part.shape[1]] = part[...]
        at += part.shape[1]


def join(deps, *parts):
    out = (parts[0].shape[0], sum(part.shape[1] for part in parts))
    return pl.pallas_call(
        after(len(deps), lambda *refs: join_kernel(refs[:-1], refs[-1])),
        grid=(1,),
        in_specs=[ANY] * len(deps) + [fixed(one.shape) for one in parts],
        out_specs=fixed(out),
        out_shape=shape(*out, BF16),
        compiler_params=params(),
        cost_estimate=cost(2),
        name="join",
    )(*deps, *parts)


def begin_kernel(x_ref, *refs):
    ins, rest_ref, front_ref = refs[:-2], refs[-2], refs[-1]
    join_kernel(ins, rest_ref)
    front_ref[...] = x_ref[ROOT:, :]


def begin(deps, x, *parts):
    outs = ((parts[0].shape[0], sum(part.shape[1] for part in parts)), (x.shape[0] - ROOT, x.shape[1]))
    return pl.pallas_call(
        after(len(deps), begin_kernel),
        grid=(1,),
        in_specs=[ANY] * len(deps) + [fixed(one.shape) for one in (x, *parts)],
        out_specs=[fixed(one) for one in outs],
        out_shape=[shape(*one, BF16) for one in outs],
        compiler_params=params(),
        cost_estimate=cost(2),
        name="begin",
    )(*deps, x, *parts)


def meet_kernel(count, at_ref, *refs):
    ins, outs = refs[:2 * count], refs[2 * count:]
    chip = at_ref[1] // 2
    for m, out_ref in enumerate(outs):
        at = 0
        for kept, away in zip(ins[:count], ins[count:]):
            n = kept.shape[2]
            out_ref[:, at:at + n] = (kept[chip ^ m].astype(F32) + away[chip ^ m].astype(F32)).astype(BF16)
            at += n


def meet(deps, at, kept, away):
    chips, rows, _ = kept[0].shape
    ins = (*kept, *away)
    out = (rows, sum(one.shape[2] for one in kept))
    return pl.pallas_call(
        after(len(deps), functools.partial(meet_kernel, len(kept))),
        grid=(1,),
        in_specs=[ANY] * len(deps) + [SMEM] + [fixed(one.shape) for one in ins],
        out_specs=[fixed(out)] * chips,
        out_shape=[shape(*out, BF16)] * chips,
        compiler_params=params(),
        cost_estimate=cost(4),
        name="meet",
    )(*deps, at, *ins)


def fold_kernel(at_ref, late_ref, in_ref, *refs):
    ins, (keep_ref, send_ref, late_out) = refs[:-3], refs[-3:]
    t = at_ref[0]
    half = keep_ref.shape[0]
    late_out[...] = (late_ref[...].astype(F32) + in_ref[...].astype(F32)).astype(BF16)
    for r in range(2 * half):
        got = sum((one[t ^ r].astype(F32) for one in ins[1:]), ins[0][t ^ r].astype(F32)).astype(BF16)
        if r < half:
            keep_ref[r] = got
        else:
            send_ref[r - half] = got


def fold(deps, at, late, late_in, *blocks):
    parts, rows, wide = blocks[0].shape
    out = (parts // 2, rows, wide)
    return pl.pallas_call(
        after(len(deps), fold_kernel),
        grid=(1,),
        in_specs=[ANY] * len(deps) + [SMEM] + [fixed(one.shape) for one in (late, late_in, *blocks)],
        out_specs=[fixed(out), fixed(out), fixed(late.shape)],
        out_shape=[jax.ShapeDtypeStruct(out, BF16)] * 2 + [jax.ShapeDtypeStruct(late.shape, BF16)],
        compiler_params=params(),
        cost_estimate=cost(4),
        name="fold",
    )(*deps, at, late, late_in, *blocks)


def middle_kernel(keep_ref, got_ref, mine_ref, send_ref):
    for r, out_ref in enumerate((mine_ref, send_ref)):
        out_ref[...] = (keep_ref[r].astype(F32) + got_ref[r].astype(F32)).astype(BF16)


def middle(deps, keep, got):
    out = keep.shape[1:]
    return pl.pallas_call(
        after(len(deps), middle_kernel),
        grid=(1,),
        in_specs=[ANY] * len(deps) + [fixed(keep.shape)] * 2,
        out_specs=[fixed(out)] * 2,
        out_shape=[shape(*out, BF16)] * 2,
        compiler_params=params(),
        cost_estimate=cost(2),
        name="middle",
    )(*deps, keep, got)


def own_kernel(count, at_ref, x_ref, cos_ref, sin_ref, *refs):
    pieces, (w_ref, gain_ref, a_ref, q_ref, k_ref, v_ref) = refs[:count], refs[count:]
    d = x_ref.shape[1]
    t, dp = at_ref[0], at_ref[1]
    step = pl.program_id(0)

    @pl.when(step == 0)
    def _():
        cols = []
        for m, piece in enumerate(pieces):
            rows = piece.shape[0]
            w_ref[aligned((dp ^ m) * rows if count > 1 else 0, rows, 8), :] = piece[:, :4 * d]
        for j in range(count):
            row = jnp.zeros((pieces[0].shape[0], GAIN_LANES), F32)
            for m, piece in enumerate(pieces):
                row = jnp.where((dp ^ m) == j if count > 1 else True, piece[:, 4 * d:].astype(F32), row)
            cols.append(row)
        table = jnp.concatenate(cols, axis=0).T
        gain_ref[...] = jnp.zeros_like(gain_ref)
        gain_ref[0:1, :] = table[0:1, :] + table[1:2, :] + table[2:3, :]
        gain_ref[1:2, :] = table[3:4, :] + table[4:5, :] + table[5:6, :]

    n = x_ref.shape[0]
    here = aligned(t * (n * pl.num_programs(0)) + step * n, n, 16)
    cos, sin = cos_ref[here, :], sin_ref[here, :]
    a = normed(x_ref[...].astype(F32), gain_ref[0:1, :])
    a_ref[...] = a
    rotated(dot(a, w_ref[:, :d]), cos, sin, q_ref, slice(None), jnp.asarray(HEAD_DIM ** -0.5, BF16))
    rotated(dot(a, w_ref[:, d:2 * d]), cos, sin, k_ref, slice(None), None)
    v_ref[...] = dot(a, w_ref[:, 2 * d:3 * d]).astype(BF16)


def project_own(deps, at, x, tab, pieces):
    loc, d = x.shape
    n = loc // 2
    return pl.pallas_call(
        after(len(deps), functools.partial(own_kernel, len(pieces))),
        grid=(2,),
        in_specs=[ANY] * len(deps) + [SMEM, tiled(n, d), fixed(tab[0].shape), fixed(tab[0].shape)] + [fixed(one.shape) for one in pieces],
        out_specs=[pl.BlockSpec((d, 4 * d), lambda i: (0, 0)), pl.BlockSpec((8, d), lambda i: (0, 0))] + [tiled(n, d)] * 4,
        out_shape=[shape(d, 4 * d, BF16), shape(8, d, F32)] + [shape(loc, d, BF16)] * 4,
        compiler_params=params(),
        cost_estimate=cost(10),
        name="project_own",
    )(*deps, at, x, *tab, *pieces)


def near_rows_kernel(at_ref, x_ref, r1_ref, r2_ref, r3_ref, f1_ref, gain_ref, wk_ref, wv_ref, cos_ref, sin_ref,
                     x_out, a_ref, k_ref, v_ref):
    t = at_ref[0]
    loc = x_ref.shape[0]
    root = pl.ds(0, ROOT)
    edge = pl.ds(ROOT, TILE)

    @pl.when(t == 0)
    def _():
        x_out[root, :] = x_ref[root, :]

    for at, ref in ((1, r1_ref), (2, r2_ref), (3, r3_ref)):
        @pl.when(t == at)
        def _():
            x_out[root, :] = ref[...]

    x_out[edge, :] = f1_ref[f1_ref.shape[0] - TILE:, :]

    a = normed(x_out[...].astype(F32), gain_ref[0:1, :])
    a_ref[...] = a
    k = dot(a, wk_ref[...])
    back = aligned(jnp.maximum(t * loc - TILE, 0), TILE)
    rotated(k[:ROOT], cos_ref[root, :], sin_ref[root, :], k_ref, root, None)
    rotated(k[ROOT:], cos_ref[back, :], sin_ref[back, :], k_ref, edge, None)
    v_ref[...] = dot(a, wv_ref[...]).astype(BF16)


def weight(d, j):
    return pl.BlockSpec((d, d), lambda i: (0, j), pipeline_mode=pl.Buffered(1))


def project_near(at, x, r1, r2, r3, f1, gains, w, tab):
    d = x.shape[1]
    n = ROOT + TILE
    return pl.pallas_call(
        near_rows_kernel,
        grid=(1,),
        in_specs=[SMEM] + [fixed(one.shape) for one in (x, r1, r2, r3, f1, gains)] + [weight(d, 1), weight(d, 2)]
        + [fixed(one.shape) for one in tab],
        out_specs=[fixed((n, d))] * 4,
        out_shape=[shape(n, d, BF16)] * 4,
        compiler_params=params(),
        cost_estimate=cost(5),
        name="project_near",
    )(at, x, r1, r2, r3, f1, gains, w, w, *tab)


def far_rows_kernel(meta_ref, slot_ref, x_ref, a1_ref, a2_ref, a3_ref, b1_ref, b2_ref, b3_ref, gain_ref, wk_ref, wv_ref, cos_ref, sin_ref,
                    x_out, a_ref, k_ref, v_ref):
    t = meta_ref[0, 5]
    for h in range(2 * BRANCHES):
        owner, at = slot_ref[h, 0], slot_ref[h, 1]
        rows = aligned(at * TILE, TILE)
        head = aligned(jnp.minimum(at * TILE, ROOT - TILE), TILE)
        back = aligned(jnp.maximum(at * TILE - ROOT, 0), TILE)
        to = pl.ds(h * TILE, TILE)

        @pl.when(owner > t)
        def _():
            x_out[to, :] = jnp.zeros((TILE, x_out.shape[1]), BF16)

        @pl.when(owner == t)
        def _():
            x_out[to, :] = x_ref[rows, :]

        for hop, a_from, b_from in ((1, a1_ref, b1_ref), (2, a2_ref, b2_ref), (3, a3_ref, b3_ref)):
            @pl.when((owner + hop == t) & (at < ROOT // TILE))
            def _():
                x_out[to, :] = a_from[head, :]

            @pl.when((owner + hop == t) & (at >= ROOT // TILE))
            def _():
                x_out[to, :] = b_from[back, :]

    a = normed(x_out[...].astype(F32), gain_ref[0:1, :])
    a_ref[...] = a
    k = dot(a, wk_ref[...])
    for h in range(2 * BRANCHES):
        back = aligned(slot_ref[h, 2] * TILE, TILE)
        rotated(k[h * TILE:(h + 1) * TILE], cos_ref[back, :], sin_ref[back, :], k_ref, pl.ds(h * TILE, TILE), None)
    v_ref[...] = dot(a, wv_ref[...]).astype(BF16)


def project_far(meta, slots, x, ups, gains, w, tab):
    d = x.shape[1]
    return pl.pallas_call(
        far_rows_kernel,
        grid=(1,),
        in_specs=[SMEM, SMEM] + [fixed(one.shape) for one in (x, *ups, gains)] + [weight(d, 1), weight(d, 2)]
        + [fixed(one.shape) for one in tab],
        out_specs=[fixed((SLOTS, d))] * 4,
        out_shape=[shape(SLOTS, d, BF16)] * 4,
        compiler_params=params(),
        cost_estimate=cost(7),
        name="project_far",
    )(meta, slots, x, *ups, gains, w, w, *tab)


def fill_bias(root_ref, own_ref, keys_axis):
    for ref in (root_ref, own_ref):
        if ref is None:
            continue
        key = lax.broadcasted_iota(jnp.int32, ref.shape[1:], keys_axis)
        row = lax.broadcasted_iota(jnp.int32, ref.shape[1:], 1 - keys_axis) % TILE
        for s in range(ref.shape[0]):
            ref[s] = jnp.where(key <= row + s * TILE, 0.0, MASKED).astype(F32)


def low_half():
    return lax.broadcasted_iota(jnp.int32, (TILE, 128), 1) < HEAD_DIM


def both(low, x):
    none = jnp.zeros_like(x)
    return jnp.concatenate([jnp.where(low, x, none), jnp.where(low, none, x)], axis=0)


def diagonal(x):
    return jnp.concatenate([x[:HEAD_DIM, :TILE], x[HEAD_DIM:, TILE:]], axis=0)


def per_half(row):
    upper = lax.broadcasted_iota(jnp.int32, (128, TILE), 0) < HEAD_DIM
    return jnp.where(upper, row[:, :TILE], row[:, TILE:])


def tile_of(meta_ref, i):
    return (meta_ref[i, 0], meta_ref[i, 1], aligned(meta_ref[i, 2], BLOCK), aligned(meta_ref[i, 3], BLOCK),
            aligned(i * TILE, TILE))


def line_up(to_ref, near_ref, own_ref):
    loc = own_ref.shape[0]
    to_ref[pl.ds(0, TILE), :] = near_ref[pl.ds(ROOT, TILE), :]
    to_ref[pl.ds(TILE, loc), :] = own_ref[...]
    to_ref[pl.ds(TILE + loc, TILE), :] = jnp.zeros((TILE, 128), to_ref.dtype)


def soften(q, spans):
    s = [dot(kk, q, COLS) if b is None else dot(kk, q, COLS) + b for kk, _, b in spans]
    top = functools.reduce(jnp.maximum, [jnp.max(part, axis=0, keepdims=True) for part in s])
    return s, top


def weigh(s, top, spans):
    e = [jnp.exp(part - top) for part in s]
    total = sum(jnp.sum(part, axis=0, keepdims=True) for part in e)
    return diagonal(sum(dot(vt, part.astype(BF16)) for part, (_, vt, _) in zip(e, spans))), total


def attend_near_kernel(meta_ref, q_ref, kn_ref, vn_ref, k_ref, v_ref, acc_ref, stat_ref, root_ref, own_ref, ko_ref, vo_ref, vr_ref):
    @pl.when(pl.program_id(0) == 0)
    def _():
        fill_bias(root_ref, own_ref, 0)

    loc = q_ref.shape[0]
    line_up(ko_ref, kn_ref, k_ref)
    root = pl.ds(0, ROOT)
    vr_ref[...] = vn_ref[root, :].T
    vo_ref[:, :TILE] = vn_ref[pl.ds(ROOT, TILE), :].T
    vo_ref[:, TILE:TILE + loc] = v_ref[...].T
    vo_ref[:, TILE + loc:] = jnp.zeros((128, TILE), BF16)
    low = low_half()
    stat_ref[...] = jnp.zeros_like(stat_ref)

    def one(i, rooted):
        sub, leaf, par, own, here = tile_of(meta_ref, i)
        q = both(low, q_ref[here, :])
        spans = [(kn_ref[root, :], vr_ref[...], root_ref[i] if rooted else None)]
        if not rooted:
            spans.append((ko_ref[own, :], vo_ref[:, own], own_ref[sub % 2]))
        s, top = soften(q, spans)
        acc, total = weigh(s, top, spans)
        acc_ref[:, here] = acc
        for h in range(2):
            stat_ref[0, h:h + 1, here] = top[:, h * TILE:(h + 1) * TILE]
            stat_ref[0, 2 + h:3 + h, here] = total[:, h * TILE:(h + 1) * TILE]

    tiles = loc // TILE

    @pl.when(meta_ref[0, 0] > 0)
    def _():
        for i in range(tiles):
            one(i, False)

    @pl.when(meta_ref[0, 0] == 0)
    def _():
        for i in range(tiles):
            one(i, i < ROOT // TILE)


def bias_scratch(keys_axis):
    def one(n):
        return pltpu.VMEM((n // TILE,) + ((n, 2 * TILE) if keys_axis == 0 else (2 * TILE, n)), F32)
    return one(ROOT), one(BLOCK)


def line_scratch(loc, kind):
    return pltpu.VMEM((loc + 2 * TILE, 128), kind)


def attend_near(meta, q, near, own):
    loc, d = q.shape
    n = ROOT + TILE
    return pl.pallas_call(
        attend_near_kernel,
        grid=(d // 128,),
        in_specs=[SMEM, pair(loc), pair(n), pair(n), pair(loc), pair(loc)],
        out_specs=[pl.BlockSpec((128, loc), lambda p: (p, 0)), log_spec(loc)],
        out_shape=[shape(d, loc, F32), jax.ShapeDtypeStruct((d // 128, 8, loc), F32)],
        scratch_shapes=[*bias_scratch(0), line_scratch(loc, BF16), pltpu.VMEM((128, loc + 2 * TILE), BF16), pltpu.VMEM((128, ROOT), BF16)],
        compiler_params=params(),
        cost_estimate=cost(20),
        name="attend_near",
    )(meta, q, *near, *own)


def attend_far_kernel(meta_ref, q_ref, ks_ref, vs_ref, acc_ref, stat_ref, o_ref, l_ref, vt_ref):
    low = low_half()
    vt_ref[...] = vs_ref[...].T
    l_ref[...] = jnp.zeros_like(l_ref)
    for i in range(o_ref.shape[0] // TILE):
        sub, leaf, par, own, here = tile_of(meta_ref, i)
        stat = stat_ref[0, :, here]
        old = jnp.concatenate([stat[0:1], stat[1:2]], axis=1)
        old_total = jnp.concatenate([stat[2:3], stat[3:4]], axis=1)
        spans = [(ks_ref[par, :], vt_ref[:, par], jnp.where(leaf > 0, 0.0, MASKED).astype(F32))]
        s, top = soften(both(low, q_ref[here, :]), spans)
        top = jnp.maximum(top, old)
        new, total = weigh(s, top, spans)
        fade = jnp.exp(old - top)
        total = old_total * fade + total
        out = (acc_ref[:, here] * per_half(fade) + new) / per_half(total)
        o_ref[here, :] = out.T.astype(BF16)
        log = top + jnp.log(total)
        for h in range(2):
            l_ref[0, h:h + 1, here] = log[:, h * TILE:(h + 1) * TILE]


def log_spec(loc):
    return pl.BlockSpec((1, 8, loc), lambda p: (p, 0, 0))


def attend_far(meta, q, far, acc, stat):
    loc, d = q.shape
    return pl.pallas_call(
        attend_far_kernel,
        grid=(d // 128,),
        in_specs=[SMEM, pair(loc), pair(SLOTS), pair(SLOTS), pl.BlockSpec((128, loc), lambda p: (p, 0)), log_spec(loc)],
        out_specs=[pair(loc), log_spec(loc)],
        out_shape=[shape(loc, d, BF16), jax.ShapeDtypeStruct((d // 128, 8, loc), F32)],
        scratch_shapes=[pltpu.VMEM((128, SLOTS), BF16)],
        compiler_params=params(),
        cost_estimate=cost(9),
        name="attend_far",
    )(meta, q, *far, acc, stat)


def split_cores(core, got, kept_ref, away_ref, where):
    @pl.when(core == 0)
    def _():
        kept_ref[where] = got[:, 0]
        away_ref[where] = got[:, 1]

    @pl.when(core == 1)
    def _():
        kept_ref[where] = got[:, 1]
        away_ref[where] = got[:, 0]


def ffn_kernel(at_ref, x_ref, o_ref, ct_ref, gain_ref, wo_ref, w_ref,
               mixed_ref, do_ref, dhb_ref, dh_ref, sum_ref, kept_ref, away_ref, c_s, m_s, dg_s, du_s, ct_t, c_t):
    step = pl.program_id(0)
    loc, d = ct_ref.shape
    n = x_ref.shape[0]
    parts, hid = m_s.shape[0], m_s.shape[2]

    def slab(t, j):
        return w_ref[:, t, :, j * hid:(j + 1) * hid].reshape(d, hid)

    @pl.when(step < loc // n)
    def _():
        here = aligned(step * n, n, 16)
        ct = ct_ref[here, :]
        h = x_ref[...].astype(F32) + dot(o_ref[...], wo_ref[...], COLS)
        scale = inv_rms(h)
        c_hat = h * scale
        gain = gain_ref[1:2, :]
        c = (c_hat * gain).astype(BF16)
        c_s[here, :] = c
        y = h
        dc = jnp.zeros_like(h)
        for t in range(parts):
            g = dot(c, slab(t, 0))
            u = dot(c, slab(t, 1))
            dm = dot(ct, slab(t, 2))
            sig = jax.nn.sigmoid(g)
            silu = g * sig
            m = (silu * u).astype(BF16)
            dg = (dm * u * (sig * (1.0 + g * (1.0 - sig)))).astype(BF16)
            du = (dm * silu).astype(BF16)
            y = y + dot(m, slab(t, 2), COLS)
            dc = dc + dot(dg, slab(t, 0), COLS) + dot(du, slab(t, 1), COLS)
            m_s[t, here, :] = m
            dg_s[t, here, :] = dg
            du_s[t, here, :] = du
        mixed_ref[...] = y.astype(BF16)
        part = jnp.sum(dc * c_hat, axis=0, keepdims=True)

        @pl.when(step == 0)
        def _():
            sum_ref[...] = jnp.zeros_like(sum_ref)

        sum_ref[0:1, :] += part
        scaled = dc * gain
        dh = ct.astype(F32) + scale * (scaled - c_hat * jnp.mean(scaled * c_hat, axis=-1, keepdims=True))
        dh_ref[...] = dh
        dhb = dh.astype(BF16)
        dhb_ref[...] = dhb
        do_ref[...] = dot(dhb, wo_ref[...]).astype(BF16)

    @pl.when(step == loc // n)
    def _():
        ct_t[...] = ct_ref[...].T
        c_t[...] = c_s[...].T

    @pl.when(step >= loc // n)
    def _():
        t = step - loc // n
        for j, (left, right) in enumerate(((c_t, dg_s), (c_t, du_s), (ct_t, m_s))):
            got = dot(left[...], right[t]).astype(BF16)
            chips, _, rows, _ = kept_ref.shape
            split_cores(at_ref[1] % 2, got.reshape(chips, 2, rows, hid), kept_ref, away_ref,
                        (slice(None), 0, slice(None), slice(j * hid, (j + 1) * hid)))


def feed_forward(at_core, x, o, ct, gains, w, rest):
    loc, d = x.shape
    dp, parts, rows, wide = rest.shape
    hid = wide // 3
    steps = 2
    n = loc // steps
    at = lambda i: (jnp.minimum(i, steps - 1), 0)
    tile = pl.BlockSpec((n, d), at)
    grads = pl.BlockSpec((dp // 2, 1, rows, wide), lambda i: (0, jnp.maximum(i - steps, 0), 0, 0))
    return pl.pallas_call(
        ffn_kernel,
        grid=(steps + parts,),
        in_specs=[SMEM, tile, tile, fixed((loc, d)), fixed((8, d)), weight(d, 3), fixed(rest.shape)],
        out_specs=[tile, tile, tile, tile, pl.BlockSpec((8, d), lambda i: (0, 0)), grads, grads],
        out_shape=[shape(loc, d, BF16), shape(loc, d, BF16), shape(loc, d, BF16), shape(loc, d, F32), shape(8, d, F32)]
        + [jax.ShapeDtypeStruct((dp // 2, parts, rows, wide), BF16)] * 2,
        scratch_shapes=[pltpu.VMEM((loc, d), BF16)] + [pltpu.VMEM((parts, loc, hid), BF16)] * 3 + [pltpu.VMEM((d, loc), BF16)] * 2,
        compiler_params=params(),
        cost_estimate=cost(40),
        name="feed_forward",
    )(at_core, x, o, ct, gains, w, rest)


def unrotate(w, cos, sin):
    return w * cos - half_turn(w) * sin


def back_setup(low, q_ref, do_ref, o_ref, l_ref, here):
    do = do_ref[here, :]
    dots = (do.astype(F32) * o_ref[here, :].astype(F32)).T
    row_dot = [jnp.sum(dots[h * HEAD_DIM:(h + 1) * HEAD_DIM, :], axis=0, keepdims=True) for h in range(2)]
    log = [l_ref[0, h:h + 1, here] for h in range(2)]
    return both(low, q_ref[here, :]), both(low, do), jnp.concatenate(log, axis=1), jnp.concatenate(row_dot, axis=1)


def back_span(setup, kk, vv, kt, bias, acc, dk_acc, dv_acc):
    q, do, log, row_dot = setup
    s = dot(kk, q, COLS)
    if bias is not None:
        s = s + bias
    p = jnp.exp(s - log)
    ds = (p * (dot(vv, do, COLS) - row_dot)).astype(BF16)
    dv_acc[acc, :] += dot(p.astype(BF16), do)
    dk_acc[acc, :] += dot(ds, q)
    return diagonal(dot(kt, ds))


def back_far_kernel(meta_ref, slot_ref, q_ref, do_ref, o_ref, l_ref, kn_ref, vn_ref, ks_ref, vs_ref, cos_ref, sin_ref,
                    dq_ref, dk_ref, dv_ref, root_ref, krt_ref, kst_ref, dk_acc, dv_acc):
    @pl.when(pl.program_id(0) == 0)
    def _():
        fill_bias(root_ref, None, 0)

    low = low_half()
    root = pl.ds(0, ROOT)
    for ref in (dk_acc, dv_acc):
        ref[...] = jnp.zeros_like(ref)
    krt_ref[...] = kn_ref[root, :].T
    kst_ref[...] = ks_ref[...].T
    tiles = do_ref.shape[0] // TILE

    def one(i, rooted):
        sub, leaf, par, own, here = tile_of(meta_ref, i)
        setup = back_setup(low, q_ref, do_ref, o_ref, l_ref, here)
        dq = back_span(setup, kn_ref[root, :], vn_ref[root, :], krt_ref[...], root_ref[i] if rooted else None, root, dk_acc, dv_acc)
        if not rooted:
            acc = aligned(meta_ref[i, 2] + ROOT, BLOCK, BLOCK)
            hide = jnp.where(leaf > 0, 0.0, MASKED).astype(F32)
            dq = dq + back_span(setup, ks_ref[par, :], vs_ref[par, :], kst_ref[:, par], hide, acc, dk_acc, dv_acc)
        dq_ref[:, here] = dq

    @pl.when(meta_ref[0, 0] > 0)
    def _():
        for i in range(tiles):
            one(i, False)

    @pl.when(meta_ref[0, 0] == 0)
    def _():
        for i in range(tiles):
            one(i, i < ROOT // TILE)

    dk_ref[root, :] = unrotate(dk_acc[root, :], cos_ref[root, :], sin_ref[root, :]).astype(BF16)
    for h in range(2 * BRANCHES):
        at, back = pl.ds(ROOT + h * TILE, TILE), aligned(slot_ref[h, 2] * TILE, TILE)
        dk_ref[at, :] = unrotate(dk_acc[at, :], cos_ref[back, :], sin_ref[back, :]).astype(BF16)
    dv_ref[...] = dv_acc[...].astype(BF16)


def turned(loc):
    return pl.BlockSpec((128, loc), lambda p: (p, 0))


def back_far(meta, slots, q, do, o, logs, near, far, tab):
    loc, d = do.shape
    n = ROOT + TILE
    return pl.pallas_call(
        back_far_kernel,
        grid=(d // 128,),
        in_specs=[SMEM, SMEM, pair(loc), pair(loc), pair(loc), log_spec(loc), pair(n), pair(n), pair(SLOTS), pair(SLOTS)]
        + [fixed(one.shape) for one in tab],
        out_specs=[turned(loc), pair(FAR), pair(FAR)],
        out_shape=[shape(d, loc, F32), shape(FAR, d, BF16), shape(FAR, d, BF16)],
        scratch_shapes=[bias_scratch(0)[0], pltpu.VMEM((128, ROOT), BF16), pltpu.VMEM((128, SLOTS), BF16),
                        pltpu.VMEM((FAR, 128), F32), pltpu.VMEM((FAR, 128), F32)],
        compiler_params=params(),
        cost_estimate=cost(50),
        name="back_far",
    )(meta, slots, q, do, o, logs, *near, *far, *tab)


def back_near_kernel(meta_ref, q_ref, do_ref, o_ref, l_ref, kn_ref, vn_ref, k_ref, v_ref, cos_ref, sin_ref, part_ref, late_ref,
                     dq_ref, dk_ref, dv_ref, dke_ref, dve_ref, copy_ref, own_ref, ko_ref, vo_ref, kt_ref, dk_acc, dv_acc):
    @pl.when(pl.program_id(0) == 0)
    def _():
        fill_bias(None, own_ref, 0)

    copy_ref[...] = late_ref[...]
    line_up(ko_ref, kn_ref, k_ref)
    line_up(vo_ref, vn_ref, v_ref)
    kt_ref[...] = ko_ref[...].T
    low = low_half()
    loc = do_ref.shape[0]
    t = meta_ref[0, 5]
    for ref in (dk_acc, dv_acc):
        ref[...] = jnp.zeros_like(ref)

    def one(i, rooted):
        sub, leaf, par, own, here = tile_of(meta_ref, i)
        dq = part_ref[:, here]
        if not rooted:
            setup = back_setup(low, q_ref, do_ref, o_ref, l_ref, here)
            dq = dq + back_span(setup, ko_ref[own, :], vo_ref[own, :], kt_ref[:, own], own_ref[sub % 2], own, dk_acc, dv_acc)
        back = aligned(sub * TILE, TILE)
        dq_ref[here, :] = unrotate(dq.T * HEAD_DIM ** -0.5, cos_ref[back, :], sin_ref[back, :]).astype(BF16)

    @pl.when(t > 0)
    def _():
        for i in range(loc // TILE):
            one(i, False)

    @pl.when(t == 0)
    def _():
        for i in range(loc // TILE):
            one(i, i < ROOT // TILE)

    edge, mine = pl.ds(0, TILE), pl.ds(TILE, loc)
    before = aligned(jnp.maximum(t * loc - TILE, 0), TILE)
    here = aligned(t * loc, loc)
    dke_ref[...] = unrotate(dk_acc[edge, :], cos_ref[before, :], sin_ref[before, :]).astype(BF16)
    dve_ref[...] = dv_acc[edge, :].astype(BF16)
    dk_ref[...] = unrotate(dk_acc[mine, :], cos_ref[here, :], sin_ref[here, :]).astype(BF16)
    dv_ref[...] = dv_acc[mine, :].astype(BF16)


def back_near(deps, meta, q, do, o, logs, near, own, tab, dq_part, late):
    loc, d = do.shape
    n = ROOT + TILE
    return pl.pallas_call(
        after(len(deps), back_near_kernel),
        grid=(d // 128,),
        in_specs=[ANY] * len(deps) + [SMEM, pair(loc), pair(loc), pair(loc), log_spec(loc), pair(n), pair(n), pair(loc), pair(loc)]
        + [fixed(one.shape) for one in tab] + [turned(loc), pair(late.shape[0])],
        out_specs=[pair(loc)] * 3 + [pair(TILE)] * 2 + [pair(late.shape[0])],
        out_shape=[shape(loc, d, BF16)] * 3 + [shape(TILE, d, BF16)] * 2 + [shape(late.shape[0], d, BF16)],
        scratch_shapes=[bias_scratch(0)[1], line_scratch(loc, BF16), line_scratch(loc, BF16),
                        pltpu.VMEM((128, loc + 2 * TILE), BF16), line_scratch(loc, F32), line_scratch(loc, F32)],
        compiler_params=params(),
        cost_estimate=cost(25),
        name="back_near",
    )(*deps, meta, q, do, o, logs, *near, *own, *tab, dq_part, late)


def spread_kernel(at_ref, kept_ref, away_ref, dk_ref, dv_ref, xn_ref, xs_ref, wk_ref, wv_ref, early_ref, late_ref, sum_ref, *outs):
    step = pl.program_id(0)
    chip = at_ref[1] // 2
    for m, out_ref in enumerate(outs):
        out_ref[0] = (kept_ref[chip ^ m, 0].astype(F32) + away_ref[chip ^ m, 0].astype(F32)).astype(BF16)
    da = dot(dk_ref[...], wk_ref[...], COLS) + dot(dv_ref[...], wv_ref[...], COLS)
    n = da.shape[0]

    def gain_part(part, x):
        x = x.astype(F32)
        return jnp.sum(part * (x * inv_rms(x)), axis=0, keepdims=True)

    @pl.when(step == 0)
    def _():
        sum_ref[...] = jnp.zeros_like(sum_ref)

    for i in range(FAR // n):
        @pl.when(step == i)
        def _():
            near = max(min(ROOT - i * n, n), 0)
            got = jnp.zeros((1, da.shape[1]), F32)
            if near:
                got = got + gain_part(da[:near], xn_ref[pl.ds(i * n, near), :])
            if near < n:
                got = got + gain_part(da[near:], xs_ref[pl.ds(i * n + near - ROOT, n - near), :])
            sum_ref[0:1, :] += got
            if i * n < EARLY:
                early_ref[...] = da.astype(BF16)
            else:
                late_ref[...] = da.astype(BF16)


def spread(at, kept, away, dk, dv, x_near, x_slot, w):
    d = w.shape[0]
    chips, parts, rows, wide = kept.shape
    n = FAR // parts
    half = EARLY // n
    block = pl.BlockSpec((chips, 1, rows, wide), lambda i: (0, i, 0, 0))
    out = pl.BlockSpec((1, rows, wide), lambda i: (i, 0, 0))
    got = pl.pallas_call(
        spread_kernel,
        grid=(parts,),
        in_specs=[SMEM, block, block, tiled(n, d), tiled(n, d), fixed(x_near.shape), fixed(x_slot.shape), weight(d, 1), weight(d, 2)],
        out_specs=[pl.BlockSpec((n, d), lambda i: (jnp.minimum(i, half - 1), 0)), pl.BlockSpec((n, d), lambda i: (jnp.maximum(i - half, 0), 0)),
                   pl.BlockSpec((8, d), lambda i: (0, 0))] + [out] * chips,
        out_shape=[shape(EARLY, d, BF16), shape(FAR - EARLY, d, BF16), shape(8, d, F32)]
        + [jax.ShapeDtypeStruct((parts, rows, wide), BF16)] * chips,
        compiler_params=params(),
        cost_estimate=cost(9),
        name="spread",
    )(at, kept, away, dk, dv, x_near, x_slot, w, w)
    return got[0], got[1], got[2], got[3:]


def own_back_kernel(x_ref, xe_ref, dq_ref, dk_ref, dv_ref, dke_ref, dve_ref, wq_ref, wk_ref, wv_ref, da_ref, edge_ref, sum_ref):
    step = pl.program_id(0)
    wk, wv = wk_ref[...], wv_ref[...]

    def gain_part(da, x):
        x = x.astype(F32)
        return jnp.sum(da * (x * inv_rms(x)), axis=0, keepdims=True)

    @pl.when(step == 0)
    def _():
        edge = dot(dke_ref[...], wk, COLS) + dot(dve_ref[...], wv, COLS)
        edge_ref[...] = edge.astype(BF16)
        sum_ref[...] = jnp.zeros_like(sum_ref)
        sum_ref[0:1, :] = gain_part(edge, xe_ref[pl.ds(ROOT, TILE), :])

    da = dot(dq_ref[...], wq_ref[...], COLS) + dot(dk_ref[...], wk, COLS) + dot(dv_ref[...], wv, COLS)
    da_ref[...] = da
    sum_ref[0:1, :] += gain_part(da, x_ref[...])


def own_back(deps, x, x_near, dq, dk, dv, dke, dve, w):
    loc, d = x.shape
    n = loc // 2
    return pl.pallas_call(
        after(len(deps), own_back_kernel),
        grid=(2,),
        in_specs=[ANY] * len(deps) + [tiled(n, d), fixed(x_near.shape), tiled(n, d), tiled(n, d), tiled(n, d), fixed((TILE, d)), fixed((TILE, d)),
                  weight(d, 0), weight(d, 1), weight(d, 2)],
        out_specs=[tiled(n, d), pl.BlockSpec((TILE, d), lambda i: (0, 0)), pl.BlockSpec((8, d), lambda i: (0, 0))],
        out_shape=[shape(loc, d, F32), shape(TILE, d, BF16), shape(8, d, F32)],
        compiler_params=params(),
        cost_estimate=cost(6),
        name="own_back",
    )(*deps, x, x_near, dq, dk, dv, dke, dve, w, w, w)


def spill(core, got, kept_ref, away_ref, at=0):
    chips, rows, _ = kept_ref.shape
    split_cores(core, got.astype(BF16).reshape(chips, 2, rows, got.shape[1]), kept_ref, away_ref,
                (slice(None), slice(None), slice(at, at + got.shape[1])))


def keyed(a_ref, an_ref, as_ref, own, far, edge):
    root, tail = pl.ds(0, ROOT), pl.ds(ROOT, TILE)
    return (dot(a_ref[...], own[...], ROWS) + dot(an_ref[root, :], far[root, :], ROWS)
            + dot(as_ref[...], far[pl.ds(ROOT, SLOTS), :], ROWS) + dot(an_ref[tail, :], edge[...], ROWS))


def first_kernel(at_ref, s1_ref, s2_ref, s3_ref, a_ref, dq_ref, dhb_ref, o_ref, kept_ref, away_ref):
    core, d = at_ref[1] % 2, a_ref.shape[1]
    line = lax.broadcasted_iota(jnp.int32, (GAIN_LANES, d), 0)
    table = jnp.where(line == 0, s1_ref[0:1, :] + s2_ref[0:1, :], jnp.where(line == 1, s3_ref[0:1, :], 0.0))
    spill(core, dot(a_ref[...], dq_ref[...], ROWS), kept_ref, away_ref)
    spill(core, dot(dhb_ref[...], o_ref[...], ROWS), kept_ref, away_ref, d)
    spill(core, table.T, kept_ref, away_ref, 2 * d)


def second_kernel(at_ref, a_ref, an_ref, as_ref, dk_ref, dv_ref, dkf_ref, dvf_ref, dke_ref, dve_ref, kept_ref, away_ref):
    step, core = pl.program_id(0), at_ref[1] % 2

    @pl.when(step == 0)
    def _():
        spill(core, keyed(a_ref, an_ref, as_ref, dk_ref, dkf_ref, dke_ref), kept_ref, away_ref)

    @pl.when(step == 1)
    def _():
        spill(core, keyed(a_ref, an_ref, as_ref, dv_ref, dvf_ref, dve_ref), kept_ref, away_ref)


def weight_sums(kernel, deps, at, arrays, dp, extra):
    d = arrays[-1].shape[1]
    chips, rows, wide = dp // 2, d // dp, 2 * d + extra
    steps = 1 if extra else 2
    spec = pl.BlockSpec((chips, rows, wide // steps), lambda i: (0, 0, i))
    return pl.pallas_call(
        after(len(deps), kernel),
        grid=(steps,),
        in_specs=[ANY] * len(deps) + [SMEM] + [fixed(one.shape) for one in arrays],
        out_specs=[spec, spec],
        out_shape=[jax.ShapeDtypeStruct((chips, rows, wide), BF16)] * 2,
        compiler_params=params(),
        cost_estimate=cost(8),
        name="weight_sums",
    )(*deps, at, *arrays)


def finish_kernel(meta_ref, da_ref, dh_ref, x_ref, gain_ref, early2_ref, late2_ref, early_ref, late_ref, edge_ref, out_ref):
    t = meta_ref[0, 5]
    tiles = x_ref.shape[0] // TILE

    def one(i, carry):
        here = aligned(i * TILE, TILE)
        given = meta_ref[i, 4]
        x = x_ref[here, :].astype(F32)
        scale = inv_rms(x)
        x_hat = x * scale
        gain = gain_ref[0:1, :]
        da = da_ref[here, :]
        none = jnp.zeros((TILE, x.shape[1]), F32)
        slot = jnp.maximum(given, 0)
        late = late_ref[aligned(slot, TILE), :].astype(F32) + late2_ref[aligned(slot, TILE), :].astype(F32)
        front = aligned(jnp.minimum(i * TILE, EARLY - TILE), TILE)
        early = early_ref[front, :].astype(F32) + early2_ref[front, :].astype(F32)
        da = da + jnp.where(given >= 0, late, none)
        da = da + jnp.where((t == 0) & (i < EARLY // TILE), early, none)
        da = da + jnp.where((i == tiles - 1) & (t % 2 == 0), edge_ref[...].astype(F32), none)
        scaled = da * gain
        out_ref[here, :] = dh_ref[here, :] + scale * (scaled - x_hat * jnp.mean(scaled * x_hat, axis=-1, keepdims=True))
        return carry

    lax.fori_loop(0, tiles, one, 0)


def finish(deps, meta, da, dh, x, gains, early2, late2, early, late, edge):
    loc, d = x.shape
    arrays = (da, dh, x, gains, early2, late2, early, late, edge)
    return pl.pallas_call(
        after(len(deps), finish_kernel),
        grid=(1,),
        in_specs=[ANY] * len(deps) + [SMEM] + [fixed(one.shape) for one in arrays],
        out_specs=fixed((loc, d)),
        out_shape=shape(loc, d, F32),
        compiler_params=params(),
        cost_estimate=cost(6),
        name="finish",
    )(*deps, meta, *arrays)


def tables(pos):
    half = HEAD_DIM // 2
    freq = jnp.exp(-jnp.log(10000.0) * (2.0 * jnp.arange(half, dtype=F32) / HEAD_DIM))
    angle = pos.astype(F32)[:, None] * jnp.concatenate([freq, freq, freq, freq])[None, :]
    sign = jnp.where(jnp.arange(2 * HEAD_DIM) % HEAD_DIM < half, -1.0, 1.0).astype(F32)
    return jnp.cos(angle), jnp.sin(angle) * sign[None, :]


def swap(x, axis, mask):
    return lax.ppermute(x, axis, [(i, i ^ mask) for i in range(lax.axis_size(axis))])


def send(x, *pairs):
    return lax.ppermute(x, "tensor", list(pairs))


def three(g):
    high = lax.reduce_precision(g, 8, 7)
    mid = lax.reduce_precision(g - high, 8, 7)
    return [high.astype(BF16), mid.astype(BF16), (g - high - mid).astype(BF16)]


def total_kernel(own_ref, *refs):
    ins, out_ref = refs[:-1], refs[-1]
    out_ref[...] = sum((one[...].astype(F32) for one in ins), own_ref[...].astype(F32)).astype(BF16)


def total(deps, *parts):
    one = fixed(parts[0].shape)
    return pl.pallas_call(
        after(len(deps), total_kernel),
        grid=(1,),
        in_specs=[ANY] * len(deps) + [one] * len(parts),
        out_specs=one,
        out_shape=jax.ShapeDtypeStruct(parts[0].shape, BF16),
        compiler_params=params(),
        cost_estimate=cost(3),
        name="total",
    )(*deps, *parts)


def meet_chips(deps, blocks):
    return total(deps, blocks[0], *(swap(block, "dp", 2 * m) for m, block in enumerate(blocks) if m))


def per_device(tokens, gain_attn, w_query, w_key, w_value, w_out, gain_ffn, w_gate, w_up, w_down,
               segment_ids, parent_ids, positions, cotangent):
    loc, d = tokens.shape
    t_size, t_at = lax.axis_size("tensor"), lax.axis_index("tensor")
    d_size, d_at = lax.axis_size("dp"), lax.axis_index("dp")
    tiles = loc // TILE
    own_gain = gain_attn.shape[0]
    rows, hid = w_gate.shape
    n = w_query.shape[1]
    at = jnp.stack([t_at, d_at]).astype(jnp.int32)

    up = [(i, i + 1) for i in range(t_size - 1)]
    a1 = send(tokens[:ROOT], *up)
    gain_cols = jnp.stack(three(gain_attn) + three(gain_ffn), axis=1)
    gain_cols = lax.dynamic_update_slice(jnp.zeros((rows, GAIN_LANES), BF16), gain_cols, (t_at * own_gain, 0))
    pack = jnp.concatenate([w_query, w_key, w_value, w_out.T, gain_cols], axis=1)
    others = [pack] + [swap(pack, "tensor", m) for m in range(1, t_size)]
    meta, slots = plan(at[:1], segment_ids, parent_ids, tiles)
    tab = tables(positions)
    lined = line((a1,), others)
    a2 = send(a1, *up[1:])
    pieces = [None] * d_size
    for m in range(0, d_size, 2):
        pieces[m] = swap(lined, "dp", m) if m else lined
    b1 = send(join((lined,), tokens[ROOT:]), *up)
    rest = join((a2, b1, *tab, *(pieces[m] for m in range(2, d_size, 2))), w_gate, w_up, w_down.T)
    a3 = send(a2, *up[2:])
    for m in range(0, d_size, 2):
        pieces[m + 1] = swap(pieces[m], "dp", 1)
    if rows % 16:
        whole = jnp.zeros((d_size * rows, lined.shape[1]), BF16)
        for m in range(d_size):
            whole = lax.dynamic_update_slice_in_dim(whole, pieces[m], (d_at ^ m) * rows, 0)
        pieces = [whole]
    rest = lax.all_gather(rest, ("dp", "tensor"), axis=0, tiled=False).reshape(d_size, t_size, rows, 3 * hid)
    w, gains, a_own, q, k_own, v_own = project_own((), at, tokens, tab, pieces)
    again, front = begin((a3, k_own), tokens, b1)
    b2 = send(again, *up[1:])
    b3 = send(front, (0, 3))
    x_near, a_near, k_near, v_near = project_near(at, tokens, a1, a2, a3, b1, gains, w, tab)
    near, own = (k_near, v_near), (k_own, v_own)
    acc, stat = attend_near(meta, q, near, own)
    x_slot, a_slot, k_slot, v_slot = project_far(meta, slots, tokens, (a1, a2, a3, b1, b2, b3), gains, w, tab)
    far = (k_slot, v_slot)
    o, logs = attend_far(meta, q, far, acc, stat)

    mixed, do, dhb, dh, ffn_sum, kept, away = feed_forward(at, tokens, o, cotangent, gains, w, rest)
    away = swap(away, "dp", 1)
    dq_part, dk_far, dv_far = back_far(meta, slots, q, do, o, logs, near, far, tab)
    early, late, far_sum, rest_blocks = spread(at, kept, away, dk_far, dv_far, x_near, x_slot, w)
    moved = [swap(block, "dp", 2 * m) for m, block in enumerate(rest_blocks) if m]
    early_in = send(early, (3, 2), (1, 0))
    dq, dk, dv, dke, dve, late = back_near((early,), meta, q, do, o, logs, near, own, tab, dq_part, late)
    late_in = send(late, (3, 2))
    early = total((dq,), early, early_in)
    early_in = send(early, (2, 0))
    da, edge, own_sum = own_back((early, moved[-1]), tokens, x_near, dq, dk, dv, dke, dve, w)
    kept_b, away_b = weight_sums(
        second_kernel, (da,), at, (a_own, a_near, a_slot, dk, dv, dk_far, dv_far, dke, dve), d_size, 0)
    away_b = swap(away_b, "dp", 1)
    keep, away, late = fold((kept_b,), at, late, late_in, rest_blocks[0], *moved)
    away = swap(away, "tensor", 2)
    late_in = send(late, (2, 1))
    kept_a, away_a = weight_sums(
        first_kernel, (keep, late, early_in), at, (far_sum, own_sum, ffn_sum, a_own, dq, dhb, o), d_size, GAIN_LANES)
    away_a = swap(away_a, "dp", 1)
    blocks = meet((), at, (kept_a, kept_b), (away_a, away_b))
    summed = meet_chips((late_in,), blocks)
    mine, away = middle((summed,), keep, away)
    rest_owned = mine.astype(F32) + swap(away, "tensor", 1).astype(F32)
    crossing = (slots[2, 0] == 0) & (t_at == 1)
    edge = send(edge + jnp.where(crossing, late[:TILE] + late_in[:TILE], jnp.zeros_like(edge)), (1, 0), (3, 2))
    grad_tokens = finish((summed,), meta, da, dh, tokens, gains, early, late, early_in, late_in, edge)
    starts = (0, d, 2 * d + GAIN_LANES, 3 * d + GAIN_LANES)

    def share(m):
        return jnp.concatenate([summed[:, at + m * n:at + (m + 1) * n] for at in starts] + [summed[:, 2 * d:2 * d + GAIN_LANES]], axis=1)

    owned = share(0).astype(F32)
    for m in range(1, t_size):
        owned = owned + swap(share(m), "tensor", m).astype(F32)
    gain_sums = lax.dynamic_slice(owned, (t_at * own_gain, 4 * n), (own_gain, GAIN_LANES))
    return (mixed, grad_tokens, gain_sums[:, 0], owned[:, :n], owned[:, 2 * n:3 * n], owned[:, 3 * n:4 * n], owned[:, n:2 * n].T,
            gain_sums[:, 1], rest_owned[:, :hid], rest_owned[:, hid:2 * hid], rest_owned[:, 2 * hid:].T)


def solution(mesh):
    rows = P(("dp", "tensor"), None)
    gain = P(("dp", "tensor"))
    wide = P("dp", "tensor")
    tall = P("tensor", "dp")
    return jax.shard_map(
        per_device,
        mesh=mesh,
        in_specs=(rows, gain, wide, wide, wide, tall, gain, wide, wide, tall, P("dp"), P("dp"), P("dp"), rows),
        out_specs=(rows, rows, gain, wide, wide, wide, tall, gain, wide, wide, tall),
        check_vma=False,
    )
```
